128 devices in a mesh: gz: 8 (over y, z_hi), gy: 16 (over x, z_lo, core).
Axes of the slice: x: 4, y: 4, z: 4 (z_hi: 2, z_lo: 2; z = z_hi * 2 + z_lo), core: 2. Of those that a mesh axis runs over, the one named last changes fastest.
Arguments:
- activations: bfloat16 [16, 256, 12288], P('gz', 'gy'), may hold values from -6 to 6
- grad_out: bfloat16 [16, 256, 12288], P('gz', 'gy'), may hold values from -6 to 6
- relu_mask: int32 [16, 256, 12288], P('gz', 'gy'), may hold values 0 or 1
- kernel: bfloat16 [3, 3, 3, 32, 32], replicated, may hold values from -0.21875 to 0.21875
- bias: float32 [32], replicated, may hold values from -3 to 3
Outputs:
- output: bfloat16 [16, 256, 12288], P('gz', 'gy')
- grad_input: bfloat16 [16, 256, 12288], P('gz', 'gy')
- grad_kernel: float32 [3, 3, 3, 32, 32], replicated
- grad_bias: float32 [32], replicated
The draws below stay inside these ranges and needn't reach their ends.
All inputs are finite; a program needn't handle non-finite values. No bound on the sum of `relu_mask` on one device may be relied on, other than what follows from the above.
Results may differ from the reference program's by a relative error of at most 0.001.
Values may be sent and summed in bfloat16 or wider, within the bound.
No kernel may reach another device: no remote copies, remote signals or barrier semaphores. Data moves between devices by JAX's collectives and lax.ppermute only.
A program may use at most 192 MiB of HBM per device.

```python
import math
import jax
import jax.numpy as jnp
from jax import lax

C = 32
NX = 384
NZ = 16
NY = 256


def set_ends(result, stream_key, least, top_value):
    spot = [jax.random.randint(jax.random.fold_in(stream_key, axis), (), 0, length) for axis, length in enumerate(result.shape)]
    longest = result.shape.index(max(result.shape))
    beside = spot[:longest] + [(spot[longest] + 1) % result.shape[longest]] + spot[longest + 1:]
    return result.at[tuple(spot)].set(least).at[tuple(beside)].set(top_value)


def level_of(stream_key, shape, cuts, smallest, top_value):
    gain = 1.0
    for axis_at, parts in cuts:
        heights = jax.random.uniform(jax.random.fold_in(jax.random.fold_in(stream_key, 6), axis_at), (parts,), jnp.float32, smallest / len(cuts), top_value / len(cuts))
        gain = gain * jnp.repeat(jnp.exp(heights), shape[axis_at] // parts).reshape((-1,) + (1,) * (len(shape) - 1 - axis_at))
    return gain


def centred(stream_key, shape, spread, limit, shards=(), dtype=jnp.bfloat16):
    gain = level_of(stream_key, shape, shards, -0.22, 0.18) if shards else 1.0
    result = jax.random.normal(stream_key, shape, jnp.float32) * spread * gain
    return jnp.minimum(jnp.maximum(result, -limit), limit).astype(dtype)


def setup_inputs(seed: int = 0) -> dict:
    key_of = jax.random.split(jax.random.key(seed), 6)
    return {
        "activations": centred(key_of[0], (NZ, NY, NX * C), 1.0, 6.0, ((0, 8), (1, 16))),
        "grad_out": centred(key_of[1], (NZ, NY, NX * C), 1.0, 6.0, ((0, 8), (1, 16))),
        "relu_mask": set_ends((jax.random.randint(key_of[2], (NZ, NY, NX * C), 0, 2) < 1).astype(jnp.int32), jax.random.fold_in(key_of[2], 1), 0, 1),
        "kernel": centred(key_of[3], (3, 3, 3, C, C), (27 * C) ** -0.5, 0.21875),
        "bias": centred(key_of[4], (C,), 0.5, 3.0, (), jnp.float32),
    }


def convolve(volume, weights):
    return lax.conv_general_dilated(volume[None], weights, (1, 1, 1), [(1, 1), (1, 1), (1, 1)], dimension_numbers=('NDHWC', 'DHWIO', 'NDHWC'), precision=lax.Precision.HIGHEST)[0]

def reference(activations, grad_out, relu_mask, kernel, bias):
    inputs = activations.astype(jnp.float32).reshape(NZ, NY, NX, C)
    weights = kernel.astype(jnp.float32)
    preact, pullback = jax.vjp(convolve, inputs, weights)
    output = jnp.maximum(preact + bias, 0.0).astype(jnp.bfloat16).reshape(NZ, NY, NX * C)
    grad_pre = (grad_out * relu_mask.astype(jnp.bfloat16)).astype(jnp.float32).reshape(NZ, NY, NX, C)
    grad_input, grad_weights = pullback(grad_pre)
    scaling = 1.0 / math.sqrt(NZ * NY * NX)
    grad_kernel = grad_weights * scaling
    grad_bias = lax.optimization_barrier(jnp.sum(grad_pre, axis=(0, 1, 2))) * scaling
    return (output, grad_input.astype(jnp.bfloat16).reshape(NZ, NY, NX * C), grad_kernel, grad_bias)
```

```python
import functools
import math

import jax
import jax.numpy as jnp
from jax import lax
from jax.experimental import pallas as pl
from jax.experimental.pallas import tpu as pltpu
from jax.sharding import PartitionSpec as P

F32 = jnp.float32
BF16 = jnp.bfloat16
LANES = 128
VMEM_LIMIT = 48 * 1024 * 1024


def params():
    return pltpu.CompilerParams(vmem_limit_bytes=VMEM_LIMIT)


def call(body, outs, scratch, flops, moved):
    return pl.pallas_call(
        body,
        out_shape=outs,
        scratch_shapes=scratch,
        compiler_params=params(),
        cost_estimate=pl.CostEstimate(flops=flops, bytes_accessed=moved, transcendentals=0),
    )


def spread_rows(scratch, groups, group, block):
    pitch = groups + 1
    for half in range(2):
        scratch[pl.ds(half * 8 * pitch + group, 8, stride=pitch), :] = block[half * 8 : half * 8 + 8]


def group_act_body(act, low, high, scratch):
    rows, groups, _ = low.shape
    for plane, out in ((0, low), (1, high)):
        for group in range(groups):
            block = act[plane, :, group * LANES : (group + 1) * LANES].astype(F32)
            spread_rows(scratch, groups, group, block)
        for row in range(rows):
            out[row] = scratch[row * (groups + 1) : row * (groups + 1) + groups, :].astype(BF16)


def group_grad_body(grad, mask, act_low, act_high, low, high, firsts, lasts, scratch):
    rows, groups, _ = low.shape
    for plane, out in ((0, low), (1, high)):
        for group in range(groups):
            span = slice(group * LANES, (group + 1) * LANES)
            block = grad[plane, :, span].astype(F32) * mask[plane, :, span].astype(F32)
            spread_rows(scratch, groups, group, block)
        for row in range(rows):
            out[row] = scratch[row * (groups + 1) : row * (groups + 1) + groups, :].astype(BF16)
    for place, source in enumerate((act_low, act_high, low, high)):
        firsts[place] = source[0]
        lasts[place] = source[rows - 1]


def with_edges(cells):
    groups = cells.shape[0]
    wide = cells.astype(F32)
    lane = lax.broadcasted_iota(jnp.int32, wide.shape, 1)
    row = lax.broadcasted_iota(jnp.int32, wide.shape, 0)
    before = jnp.where(row == 0, 0.0, pltpu.roll(wide, 1, 0))
    after = jnp.where(row == groups - 1, 0.0, pltpu.roll(wide, groups - 1, 0))
    return jnp.concatenate([cells, jnp.where(lane < 64, after, before).astype(BF16)], axis=1)


def fill_plane(taps, place, source, first, last):
    rows = source.shape[0]
    taps[place, 0] = with_edges(first)
    taps[place, rows + 1] = with_edges(last)

    def step(row, carry):
        taps[place, row + 1] = with_edges(source[row])
        return carry

    lax.fori_loop(0, rows, step, 0, unroll=2)


def build_weights(tiled, out):
    lane = lax.broadcasted_iota(jnp.int32, (32, LANES), 1) // 32
    for tap_z in range(3):
        for tap_y in range(3):
            at = (tap_z * 3 + tap_y) * 3
            blocks = [tiled[(at + e) * 32 : (at + e + 1) * 32, :].astype(F32) for e in range(3)]
            for place in range(8):
                voxel = place if place < 6 else place - 8
                total = jnp.zeros((32, LANES), F32)
                for e in range(3):
                    total = jnp.where(lane == voxel - e + 1, blocks[e], total)
                out[tap_z, tap_y, place * 32 : place * 32 + 32, :] = total.astype(BF16)


CHUNK = 4


def local_body(
    a_low, a_high, g_low, g_high, from_left, from_right, tiled_f, tiled_g,
    pre, gin, turned, terms, bias_terms, w_f, w_g, taps,
):
    rows, groups, _ = a_low.shape
    build_weights(tiled_f, w_f)
    build_weights(tiled_g, w_g)
    sums = jnp.zeros((8, LANES), F32)
    for plane, source in enumerate((g_low, g_high)):
        flat = source[...].reshape(rows * groups, LANES)
        turned[plane * LANES : (plane + 1) * LANES, :] = flat.T
        sums = sums + jnp.sum(flat.astype(F32).reshape(-1, 8, LANES), axis=0)
    bias_terms[...] = sums

    def convolve(weights, out):
        def step(chunk, carry):
            total = None
            for plane in range(2):
                for tap_y in range(3):
                    lhs = taps[plane, pl.ds(chunk * CHUNK + tap_y, CHUNK)].reshape(CHUNK * groups, 256)
                    matrix = jnp.concatenate([weights[plane + 1, tap_y], weights[plane, tap_y]], axis=1)
                    term = jnp.dot(lhs, matrix, preferred_element_type=F32)
                    total = term if total is None else total + term
            for plane in range(2):
                part = total[:, plane * LANES : (plane + 1) * LANES]
                out[plane, pl.ds(chunk * CHUNK, CHUNK)] = part.reshape(CHUNK, groups, LANES)
            return carry

        lax.fori_loop(0, rows // CHUNK, step, 0)

    for plane, source in enumerate((g_low, g_high)):
        fill_plane(taps, plane, source, from_left[2 + plane], from_right[2 + plane])
    convolve(w_g, gin)
    for plane, source in enumerate((a_low, a_high)):
        fill_plane(taps, plane, source, from_left[plane], from_right[plane])
    convolve(w_f, pre)
    for tap_y in range(3):
        both = []
        for plane in range(2):
            rhs = taps[plane, tap_y : tap_y + rows].reshape(rows * groups, 256)
            both.append(jnp.dot(turned[...], rhs, preferred_element_type=F32))
        terms[1, tap_y] = both[0][:LANES] + both[1][LANES:]
        terms[0, tap_y] = both[0][LANES:]
        terms[2, tap_y] = both[1][:LANES]


def kernel_grad_body(below, above, corner_below, corner_above, turned, terms, bias_terms, taps, packed):
    rows, groups, _ = below.shape
    fill_plane(taps, 0, below, corner_below[0], corner_below[1])
    fill_plane(taps, 1, above, corner_above[0], corner_above[1])
    lane = lax.broadcasted_iota(jnp.int32, (32, LANES), 1)
    folded = []
    for tap_z in range(3):
        for tap_y in range(3):
            term = terms[tap_z, tap_y]
            if tap_z != 1:
                side = 0 if tap_z == 0 else 1
                rhs = taps[side, tap_y : tap_y + rows].reshape(rows * groups, 256)
                lhs = turned[side * LANES : (side + 1) * LANES, :]
                term = term + jnp.dot(lhs, rhs, preferred_element_type=F32)
            total = None
            for voxel in range(4):
                part = term[voxel * 32 : voxel * 32 + 32]
                shift = (-(voxel - 1) * 32) % 256
                if shift:
                    part = pltpu.roll(part, shift, 1)
                total = part if total is None else total + part
            folded.append(total[:, :LANES])
    row = jnp.sum(bias_terms[...], axis=0, keepdims=True)
    row = row + pltpu.roll(row, 64, 1)
    row = row + pltpu.roll(row, 32, 1)
    first = lax.broadcasted_iota(jnp.int32, (32, LANES), 0) == 0
    for place in range(7):
        if place < 6:
            extra = pltpu.roll(folded[7 + place // 3], 96 - 32 * (place % 3), 1)
        else:
            extra = jnp.where(first, jnp.broadcast_to(row, (32, LANES)), 0.0)
        packed[place * 32 : place * 32 + 32, :] = jnp.where(lane < 96, folded[place], extra)


def finish(taps, weights, partial, out, scratch, turn):
    rows, groups, _ = partial.shape[1:]
    pitch = groups + 1
    for plane in range(2):
        tap_z = 0 if plane == 0 else 2
        for chunk in range(rows // CHUNK):
            total = partial[plane, chunk * CHUNK : (chunk + 1) * CHUNK].reshape(CHUNK * groups, LANES)
            for tap_y in range(3):
                at = chunk * CHUNK + tap_y
                lhs = taps[plane, at : at + CHUNK].reshape(CHUNK * groups, 256)
                total = total + jnp.dot(lhs, weights[tap_z, tap_y], preferred_element_type=F32)
            total = turn(total)
            for row in range(CHUNK):
                at = (chunk * CHUNK + row) * pitch
                scratch[at : at + groups, :] = total[row * groups : (row + 1) * groups]
        for group in range(groups):
            halves = [scratch[pl.ds(half * 8 * pitch + group, 8, stride=pitch), :] for half in range(2)]
            block = jnp.concatenate(halves, axis=0).astype(BF16)
            out[plane, :, group * LANES : (group + 1) * LANES] = block


def output_body(taps, weights, partial, bias, out, scratch):
    line = bias[...]
    finish(taps, weights, partial, out, scratch, lambda total: jnp.maximum(total + line, 0.0))


def grad_input_body(below, above, corner_below, corner_above, weights, partial, out, taps, scratch):
    fill_plane(taps, 0, below, corner_below[2], corner_below[3])
    fill_plane(taps, 1, above, corner_above[2], corner_above[3])
    finish(taps, weights, partial, out, scratch, lambda total: total)


def unpack_body(scaling, packed, other, grad_kernel, grad_bias):
    for place in range(7):
        span = slice(place * 32, place * 32 + 32)
        block = (packed[span, :] + other[span, :]) * scaling
        turned = block.T
        grad_kernel[place * 96 : place * 96 + 96, :] = turned[:96]
        if place < 6:
            grad_kernel[(21 + place) * 32 : (22 + place) * 32, :] = turned[96:]
        else:
            grad_bias[...] = pltpu.roll(block, 32, 1)[:1, :32]


def shifted(value, axis, step):
    count = lax.axis_size(axis)
    pairs = [(i, i + step) for i in range(count) if 0 <= i + step < count]
    return lax.ppermute(value, axis, pairs)


def swapped(value, axis, bit):
    return lax.ppermute(value, axis, [(i, i ^ bit) for i in range(lax.axis_size(axis))])


def local(activations, grad_out, relu_mask, kernel, bias):
    planes, rows, width = activations.shape
    groups = width // LANES
    shape = jax.ShapeDtypeStruct
    plane = shape((rows, groups, LANES), BF16)
    lines = shape((4, groups, LANES), BF16)
    spread = pltpu.VMEM((rows * (groups + 1) + 8, LANES), F32)
    taps_shape = (2, rows + 2, groups, 2 * LANES)
    part = shape((2, rows, groups, LANES), F32)
    size = rows * groups * LANES * 2
    work = 2 * rows * groups * 256 * 256

    a_low, a_high = call(group_act_body, (plane, plane), [spread], 0, 4 * size)(activations)
    a_below = shifted(a_high, "gz", 1)
    a_above = shifted(a_low, "gz", -1)
    g_low, g_high, firsts, lasts = call(
        group_grad_body, (plane, plane, lines, lines), [spread], 0, 8 * size
    )(grad_out, relu_mask, a_low, a_high)
    from_left = shifted(lasts, "gy", 1)
    from_right = shifted(firsts, "gy", -1)
    corner_below = shifted(jnp.stack([from_left[1], from_right[1], from_left[3], from_right[3]]), "gz", 1)
    corner_above = shifted(jnp.stack([from_left[0], from_right[0], from_left[2], from_right[2]]), "gz", -1)

    tiled_f = jnp.tile(kernel.reshape(27 * 32, 32), (1, 4))
    flipped = jnp.swapaxes(kernel[::-1, ::-1, ::-1], 3, 4)
    tiled_g = jnp.tile(flipped.reshape(27 * 32, 32), (1, 4))
    weights = shape((3, 3, 256, LANES), BF16)
    pre, gin, turned, terms, bias_terms, w_f, w_g = call(
        local_body,
        (
            part, part, shape((2 * LANES, rows * groups), BF16),
            shape((3, 3, LANES, 256), F32), shape((8, LANES), F32), weights, weights,
        ),
        [pltpu.VMEM(taps_shape, BF16)],
        18 * work, 12 * size,
    )(a_low, a_high, g_low, g_high, from_left, from_right, tiled_f, tiled_g)

    g_low, g_high, a_below, a_above = lax.optimization_barrier((g_low, g_high, a_below, a_above))
    g_below = shifted(g_high, "gz", 1)
    g_above = shifted(g_low, "gz", -1)

    taps, packed = call(
        kernel_grad_body,
        (shape(taps_shape, BF16), shape((7 * 32, LANES), F32)),
        [],
        6 * work, 12 * size,
    )(a_below, a_above, corner_below, corner_above, turned, terms, bias_terms)

    steps = (("gy", 1), ("gy", 2), ("gy", 4), ("gy", 8), ("gz", 1), ("gz", 2), ("gz", 4))
    for axis, bit in steps[:-1]:
        packed = packed + swapped(packed, axis, bit)
    other = swapped(packed, *steps[-1])

    result = shape(activations.shape, BF16)
    line = jnp.tile(bias, 4).reshape(1, LANES)
    output = call(output_body, result, [spread], 6 * work, 12 * size)(taps, w_f, pre, line)
    grad_input = call(
        grad_input_body, result, [pltpu.VMEM(taps_shape, BF16), spread], 6 * work, 12 * size
    )(g_below, g_above, corner_below, corner_above, w_g, gin)

    voxels = planes * lax.axis_size("gz") * rows * lax.axis_size("gy") * (width // 32)
    grad_kernel, grad_bias = call(
        functools.partial(unpack_body, 1.0 / math.sqrt(voxels)),
        (shape((27 * 32, 32), F32), shape((1, 32), F32)),
        [],
        0, 4 * 7 * 32 * LANES,
    )(packed, other)
    return output, grad_input, grad_kernel.reshape(3, 3, 3, 32, 32), grad_bias.reshape(32)


def solution(mesh):
    block = P("gz", "gy", None)
    return jax.shard_map(
        local,
        mesh=mesh,
        in_specs=(block, block, block, P(), P()),
        out_specs=(block, block, P(), P()),
        check_vma=False,
    )
```

```python
import functools
import math

import jax
import jax.numpy as jnp
from jax import lax
from jax.experimental import pallas as pl
from jax.experimental.pallas import tpu as pltpu
from jax.sharding import PartitionSpec as P

F32 = jnp.float32
BF16 = jnp.bfloat16
LANES = 128
MIB = 1024 * 1024


def call(body, outs, scratch, args):
    return pl.pallas_call(
        body,
        out_shape=outs,
        scratch_shapes=scratch,
        compiler_params=pltpu.CompilerParams(vmem_limit_bytes=20 * MIB),
    )(*args)


def blocked(body, grid, outs, out_specs, scratch, args, in_specs, aliases=None):
    return pl.pallas_call(
        body,
        grid=(grid,),
        out_shape=outs,
        in_specs=in_specs,
        out_specs=out_specs,
        scratch_shapes=scratch,
        input_output_aliases=aliases or {},
        compiler_params=pltpu.CompilerParams(vmem_limit_bytes=56 * MIB),
    )(*args)


def part_of(shape, *index):
    return pl.BlockSpec(shape, lambda step: index)


def spread_rows(scratch, groups, group, block):
    pitch = groups + 1
    for half in range(2):
        scratch[pl.ds(half * 8 * pitch + group, 8, stride=pitch), :] = block[half * 8 : half * 8 + 8]


def group_body(act_in, grad_in, mask_in, low, high, firsts, lasts, scratch, act, grad, mask, arrived):
    rows, groups = act.shape[1], low.shape[1]
    copies = [
        [
            pltpu.make_async_copy(source.at[plane], target.at[plane], arrived.at[plane, place])
            for place, (source, target) in enumerate(((act_in, act), (mask_in, mask), (grad_in, grad)))
        ]
        for plane in range(2)
    ]
    for plane in (1, 0):
        for copy in copies[plane]:
            copy.start()
    for plane, out in ((1, high), (0, low)):
        for kind in range(2):
            for copy in copies[plane][:1] if kind == 0 else copies[plane][1:]:
                copy.wait()
            for group in range(groups):
                span = slice(group * LANES, (group + 1) * LANES)
                if kind == 0:
                    block = act[plane, :, span].astype(F32)
                else:
                    block = grad[plane, :, span].astype(F32) * mask[plane, :, span].astype(F32)
                spread_rows(scratch, groups, group, block)
            for row in range(rows):
                at = row * (groups + 1)
                out[kind * rows + row] = scratch[at : at + groups, :].astype(BF16)
            firsts[plane * 2 + kind] = out[kind * rows]
            lasts[plane * 2 + kind] = out[kind * rows + rows - 1]


def with_edges(cells):
    groups = cells.shape[0]
    wide = cells.astype(F32)
    lane = lax.broadcasted_iota(jnp.int32, wide.shape, 1)
    row = lax.broadcasted_iota(jnp.int32, wide.shape, 0)
    before = jnp.where(row == 0, 0.0, pltpu.roll(wide, 1, 0))
    after = jnp.where(row == groups - 1, 0.0, pltpu.roll(wide, groups - 1, 0))
    return jnp.concatenate([cells, jnp.where(lane < 64, after, before).astype(BF16)], axis=1)


def fill_plane(taps, place, source, first, last):
    rows = source.shape[0]
    taps[place, 0] = with_edges(first)
    taps[place, rows + 1] = with_edges(last)

    def step(row, carry):
        taps[place, row + 1] = with_edges(source[row])
        return carry

    lax.fori_loop(0, rows, step, 0, unroll=2)


def build_weights(kernel, flip, out):
    lane = lax.broadcasted_iota(jnp.int32, (32, LANES), 1) // 32
    for tap_z in range(3):
        for tap_y in range(3):
            blocks = []
            for tap_x in range(3):
                at = (tap_z * 3 + tap_y) * 3 + tap_x
                at = 26 - at if flip else at
                block = kernel[at * 32 : at * 32 + 32, :].astype(F32)
                block = block.T if flip else block
                blocks.append(jnp.concatenate([block] * 4, axis=1))
            for place in range(8):
                voxel = place if place < 6 else place - 8
                total = jnp.zeros((32, LANES), F32)
                for tap_x in range(3):
                    total = jnp.where(lane == voxel - tap_x + 1, blocks[tap_x], total)
                out[tap_z, tap_y, place * 32 : place * 32 + 32, :] = total.astype(BF16)


CHUNK = 4


def fold(term):
    total = None
    for voxel in range(4):
        part = term[voxel * 32 : voxel * 32 + 32]
        shift = (-(voxel - 1) * 32) % 256
        if shift:
            part = pltpu.roll(part, shift, 1)
        total = part if total is None else total + part
    return total[:, :LANES]


def local_terms_body(low, high, edges, folded, bias_terms, turned, taps):
    rows, groups = low.shape[0] // 2, low.shape[1]
    sums = jnp.zeros((8, LANES), F32)
    blank = jnp.zeros((groups, LANES), BF16)
    for plane, source in enumerate((low, high)):
        span = slice(plane * LANES, (plane + 1) * LANES)
        flat = source[rows:].reshape(rows * groups, LANES)
        turned[span, :] = flat.T
        edges[0, span, :] = source[rows].T
        edges[1, span, :] = source[2 * rows - 1].T
        sums = sums + jnp.sum(flat.astype(F32).reshape(-1, 8, LANES), axis=0)
        fill_plane(taps, plane, source.at[:rows], blank, blank)
    bias_terms[...] = sums
    for tap_y in range(3):
        both = []
        for plane in range(2):
            rhs = taps[plane, tap_y : tap_y + rows].reshape(rows * groups, 256)
            both.append(jnp.dot(turned[...], rhs, preferred_element_type=F32))
        folded[1, tap_y] = fold(both[0][:LANES] + both[1][LANES:])
        folded[0, tap_y] = fold(both[0][LANES:])
        folded[2, tap_y] = fold(both[1][:LANES])


def kernel_grad_body(
    below, low, from_left, from_right, edges, folded, bias_terms, flag, keep, send, packed, taps, sums
):
    rows, groups = below.shape[0] // 2, below.shape[1]
    blank = jnp.zeros((groups, LANES), BF16)
    fill_plane(taps, 0, below.at[:rows], blank, blank)
    fill_plane(taps, 1, low.at[:rows], blank, blank)
    below_turned = below[rows:].reshape(rows * groups, LANES).T
    low_turned = low[rows:].reshape(rows * groups, LANES).T
    sums[1] = jnp.zeros(sums.shape[1:], F32)
    for tap_y in range(3):
        rhs = taps[0, tap_y : tap_y + rows].reshape(rows * groups, 256)
        sums[0, tap_y] = jnp.dot(low_turned, rhs, preferred_element_type=F32)
        rhs = taps[1, tap_y : tap_y + rows].reshape(rows * groups, 256)
        sums[2, tap_y] = jnp.dot(below_turned, rhs, preferred_element_type=F32)
    for side, lines in enumerate((from_left, from_right)):
        tap_y, end = 2 * side, side * (rows - 1)
        lhs = jnp.concatenate([edges[side], below[rows + end].T], axis=0)
        term = jnp.dot(lhs, with_edges(lines[0]), preferred_element_type=F32)
        sums[1, tap_y] += term[:LANES]
        sums[0, tap_y] += term[LANES : 2 * LANES]
        sums[2, tap_y] += term[2 * LANES :]
        term = jnp.dot(edges[side], with_edges(lines[2]), preferred_element_type=F32)
        sums[2, tap_y] += term[:LANES]
        sums[1, tap_y] += term[LANES:]
        sums[0, 2 - tap_y] += jnp.dot(lines[1].T, taps[0, 1 + end], preferred_element_type=F32)
    lane = lax.broadcasted_iota(jnp.int32, (32, LANES), 1)
    parts = [folded[at // 3, at % 3] + fold(sums[at // 3, at % 3]) for at in range(9)]
    row = jnp.sum(bias_terms[...], axis=0, keepdims=True)
    row = row + pltpu.roll(row, 64, 1)
    row = row + pltpu.roll(row, 32, 1)
    first = lax.broadcasted_iota(jnp.int32, (32, LANES), 0) == 0
    for place in range(7):
        if place < 6:
            extra = pltpu.roll(parts[7 + place // 3], 96 - 32 * (place % 3), 1)
        else:
            extra = jnp.where(first, jnp.broadcast_to(row, (32, LANES)), 0.0)
        packed[place * 32 : place * 32 + 32, :] = jnp.where(lane < 96, parts[place], extra)
    upper = flag[...] > 0.5
    keep[...] = jnp.where(upper, packed[HALF : 2 * HALF], packed[:HALF])
    send[...] = jnp.where(upper, packed[:HALF], packed[HALF : 2 * HALF])


def inner_sum(taps, weights, chunk, groups):
    total = None
    for plane in range(2):
        for tap_y in range(3):
            lhs = taps[plane, pl.ds(chunk * CHUNK + tap_y, CHUNK)].reshape(CHUNK * groups, 256)
            matrix = jnp.concatenate([weights[plane + 1, tap_y], weights[plane, tap_y]], axis=1)
            term = jnp.dot(lhs, matrix, preferred_element_type=F32)
            total = term if total is None else total + term
    return total


def inner_body(flip, low, high, from_left, from_right, kernel, partial, weights, taps):
    groups = low.shape[1]
    kind = 1 if flip else 0
    chunk = pl.program_id(0)

    @pl.when(chunk == 0)
    def _():
        build_weights(kernel, flip, weights)
        fill_plane(taps, 0, low, from_left[kind], from_right[kind])
        fill_plane(taps, 1, high, from_left[2 + kind], from_right[2 + kind])

    total = inner_sum(taps, weights, chunk, groups)
    for plane in range(2):
        part = total[:, plane * LANES : (plane + 1) * LANES]
        partial[plane] = part.reshape(CHUNK, groups, LANES)


def outer_body(turn, plane, source, left, right, weights, partial, line, *rest):
    out, taps, scratch = rest[-3:]
    rows, groups, _ = source.shape
    fill_plane(taps, 0, source, left[0], right[0])
    for chunk in range(rows // CHUNK):
        start = chunk * CHUNK
        total = partial[0, start : start + CHUNK].reshape(CHUNK * groups, LANES)
        for tap_y in range(3):
            lhs = taps[0, start + tap_y : start + tap_y + CHUNK].reshape(CHUNK * groups, 256)
            total = total + jnp.dot(lhs, weights[0, tap_y], preferred_element_type=F32)
        put_rows(scratch, turn(total, line), chunk, groups)
    lay_out(scratch, out, 0, rows, groups)


def rectified(total, line):
    return jnp.maximum(total + line[...], 0.0)


def kept(total, line):
    return total


def lay_out(scratch, out, plane, rows, groups):
    pitch = groups + 1
    for group in range(groups):
        halves = [scratch[pl.ds(half * 8 * pitch + group, 8, stride=pitch), :] for half in range(2)]
        block = jnp.concatenate(halves, axis=0).astype(BF16)
        out[plane, :, group * LANES : (group + 1) * LANES] = block


def put_rows(scratch, total, chunk, groups):
    for row in range(CHUNK):
        at = (chunk * CHUNK + row) * (groups + 1)
        scratch[at : at + groups, :] = total[row * groups : (row + 1) * groups]


HALF = 112


def unpack_body(scaling, part, other, flag, grad_kernel, grad_bias, packed):
    upper = flag[...] > 0.5
    packed[:HALF] = jnp.where(upper, other[...], part[...])
    packed[HALF : 2 * HALF] = jnp.where(upper, part[...], other[...])
    for place in range(7):
        block = packed[place * 32 : place * 32 + 32, :] * scaling
        turned = block.T
        grad_kernel[place * 96 : place * 96 + 96, :] = turned[:96]
        if place < 6:
            grad_kernel[(21 + place) * 32 : (22 + place) * 32, :] = turned[96:]
        else:
            grad_bias[...] = pltpu.roll(block, 32, 1)[:1, :32]


def shifted(value, axis, step):
    count = lax.axis_size(axis)
    pairs = [(i, i + step) for i in range(count) if 0 <= i + step < count]
    return lax.ppermute(value, axis, pairs)


def swapped(value, bit):
    count = lax.axis_size("gz") * lax.axis_size("gy")
    return lax.ppermute(value, ("gz", "gy"), [(i, i ^ bit) for i in range(count)])


def sum_of_four(value, low, high):
    one, two, three = (swapped(value, bit) for bit in (low, high, low + high))
    return (value + one) + (two + three)


def local(activations, grad_out, relu_mask, kernel, bias):
    planes, rows, width = activations.shape
    groups = width // LANES
    block = activations.shape
    shape = jax.ShapeDtypeStruct
    pair = shape((2 * rows, groups, LANES), BF16)
    lines = shape((4, groups, LANES), BF16)
    spread = pltpu.VMEM((rows * (groups + 1) + 8, LANES), F32)
    two_taps = pltpu.VMEM((2, rows + 2, groups, 2 * LANES), BF16)
    half = shape((HALF, LANES), F32)
    packed = pltpu.VMEM((2 * HALF, LANES), F32)
    flag = jnp.full((1, LANES), lax.axis_index("gy") % 2, F32)

    low, high, firsts, lasts = pl.pallas_call(
        group_body,
        in_specs=[pl.BlockSpec(memory_space=pl.ANY)] * 3,
        out_shape=(pair, pair, lines, lines),
        scratch_shapes=[
            spread, pltpu.VMEM(block, BF16), pltpu.VMEM(block, BF16), pltpu.VMEM(block, jnp.int32),
            pltpu.SemaphoreType.DMA((2, 3)),
        ],
        compiler_params=pltpu.CompilerParams(vmem_limit_bytes=56 * MIB),
    )(activations, grad_out, relu_mask)
    below = shifted(high, "gz", 1)
    from_left = shifted(lasts, "gy", 1)
    from_right = shifted(firsts, "gy", -1)
    corner = shifted(jnp.concatenate([from_left[2:], from_right[2:]]), "gz", 1)

    edges, folded, bias_terms = blocked(
        local_terms_body,
        1,
        (shape((2, 2 * LANES, groups), BF16), shape((3, 3, 32, LANES), F32), shape((8, LANES), F32)),
        (
            part_of((2, 2 * LANES, groups), 0, 0, 0), part_of((3, 3, 32, LANES), 0, 0, 0, 0),
            part_of((8, LANES), 0, 0),
        ),
        [pltpu.VMEM((2 * LANES, rows * groups), BF16), two_taps],
        (low, high),
        [part_of(pair.shape, 0, 0, 0)] * 2,
    )

    plane = (rows, groups, LANES)
    line = jnp.tile(bias, 4).reshape(1, LANES)
    flat_kernel = kernel.reshape(27 * 32, 32)

    def inner(kind):
        return blocked(
            functools.partial(inner_body, kind == 1),
            rows // CHUNK,
            (shape((2, *plane), F32), shape((3, 3, 256, LANES), BF16)),
            (
                pl.BlockSpec((2, CHUNK, groups, LANES), lambda step: (0, step, 0, 0)),
                part_of((3, 3, 256, LANES), 0, 0, 0, 0),
            ),
            [two_taps],
            (low, high, from_left, from_right, flat_kernel),
            [part_of(plane, kind, 0, 0)] * 2
            + [part_of(lines.shape, 0, 0, 0)] * 2
            + [part_of(flat_kernel.shape, 0, 0)],
        )

    def outer(kind, side, source, edge, weights, partial, done=None):
        row = (1, groups, LANES)
        args = [source, edge, edge, weights, partial, line]
        first = 2 * rows if edge is source else 0
        specs = [
            part_of(plane, kind, 0, 0), part_of(row, first + kind, 0, 0), part_of(row, first + 2 + kind, 0, 0),
            part_of((1, 3, 256, LANES), 2 * side, 0, 0, 0), part_of((1, *plane), side, 0, 0, 0),
            part_of((1, LANES), 0, 0),
        ]
        if done is not None:
            args.append(done)
            specs.append(pl.BlockSpec(memory_space=pl.ANY))
        return blocked(
            functools.partial(outer_body, kept if kind else rectified, side),
            1,
            shape(block, BF16),
            part_of((1, *block[1:]), side, 0, 0),
            [pltpu.VMEM((1, rows + 2, groups, 2 * LANES), BF16), spread],
            args,
            specs,
            None if done is None else {6: 0},
        )

    partial_f, weights_f = inner(0)
    partial_g, weights_g = inner(1)

    ends = (from_left[:2], from_right[:2])
    ends, folded, partial_f, partial_g = lax.optimization_barrier((ends, folded, partial_f, partial_g))
    down = jnp.concatenate([low, *ends])
    down, below, corner = lax.optimization_barrier((down, below, corner))
    above = shifted(down, "gz", -1)

    part, send = call(
        kernel_grad_body,
        (half, half),
        [packed, two_taps, pltpu.VMEM((3, 3, LANES, 256), F32)],
        (below, low, from_left, from_right, edges, folded, bias_terms, flag),
    )
    output = outer(0, 0, below, corner, weights_f, partial_f)
    grad_input = outer(1, 0, below, corner, weights_g, partial_g)

    part = part + swapped(send, 1)
    part = sum_of_four(part, 4, 8)
    part = sum_of_four(part, 32, 64)
    part, above, output, grad_input = lax.optimization_barrier((part, above, output, grad_input))
    part = sum_of_four(part, 2, 16)
    output = outer(0, 1, above, above, weights_f, partial_f, output)
    grad_input = outer(1, 1, above, above, weights_g, partial_g, grad_input)
    part, output, grad_input = lax.optimization_barrier((part, output, grad_input))
    other = swapped(part, 1)

    voxels = planes * lax.axis_size("gz") * rows * lax.axis_size("gy") * (width // 32)
    grad_kernel, grad_bias = call(
        functools.partial(unpack_body, 1.0 / math.sqrt(voxels)),
        (shape((27 * 32, 32), F32), shape((1, 32), F32)),
        [packed],
        (part, other, flag),
    )
    return output, grad_input, grad_kernel.reshape(3, 3, 3, 32, 32), grad_bias.reshape(32)


def solution(mesh):
    block = P("gz", "gy", None)
    return jax.shard_map(
        local,
        mesh=mesh,
        in_specs=(block, block, block, P(), P()),
        out_specs=(block, block, P(), P()),
        check_vma=False,
    )
```

```python
import functools
import math

import jax
import jax.numpy as jnp
from jax import lax
from jax.experimental import pallas as pl
from jax.experimental.pallas import tpu as pltpu
from jax.sharding import PartitionSpec as P

F32 = jnp.float32
BF16 = jnp.bfloat16
LANES = 128
MIB = 1024 * 1024


def call(body, outs, scratch, args):
    return pl.pallas_call(
        body,
        out_shape=outs,
        scratch_shapes=scratch,
        compiler_params=pltpu.CompilerParams(vmem_limit_bytes=20 * MIB),
    )(*args)


def blocked(body, grid, outs, out_specs, scratch, args, in_specs, aliases=None):
    return pl.pallas_call(
        body,
        grid=(grid,),
        out_shape=outs,
        in_specs=in_specs,
        out_specs=out_specs,
        scratch_shapes=scratch,
        input_output_aliases=aliases or {},
        compiler_params=pltpu.CompilerParams(vmem_limit_bytes=56 * MIB),
    )(*args)


def part_of(shape, *index):
    return pl.BlockSpec(shape, lambda step: index)


def spread_rows(scratch, groups, group, block):
    pitch = groups + 1
    for half in range(2):
        scratch[pl.ds(half * 8 * pitch + group, 8, stride=pitch), :] = block[half * 8 : half * 8 + 8]


def group_body(act_in, grad_in, mask_in, low, high, firsts, lasts, scratch, act, grad, mask, arrived):
    rows, groups = act.shape[1], low.shape[1]
    copies = [
        [
            pltpu.make_async_copy(source.at[plane], target.at[plane], arrived.at[plane, place])
            for place, (source, target) in enumerate(((act_in, act), (mask_in, mask), (grad_in, grad)))
        ]
        for plane in range(2)
    ]
    for plane in (1, 0):
        for copy in copies[plane]:
            copy.start()
    for plane, out in ((1, high), (0, low)):
        for kind in range(2):
            for copy in copies[plane][:1] if kind == 0 else copies[plane][1:]:
                copy.wait()
            for group in range(groups):
                span = slice(group * LANES, (group + 1) * LANES)
                if kind == 0:
                    block = act[plane, :, span].astype(F32)
                else:
                    block = grad[plane, :, span].astype(F32) * mask[plane, :, span].astype(F32)
                spread_rows(scratch, groups, group, block)
            for row in range(rows):
                at = row * (groups + 1)
                out[kind * rows + row] = scratch[at : at + groups, :].astype(BF16)
            firsts[plane * 2 + kind] = out[kind * rows]
            lasts[plane * 2 + kind] = out[kind * rows + rows - 1]


def with_edges(cells):
    groups = cells.shape[0]
    wide = cells.astype(F32)
    lane = lax.broadcasted_iota(jnp.int32, wide.shape, 1)
    row = lax.broadcasted_iota(jnp.int32, wide.shape, 0)
    before = jnp.where(row == 0, 0.0, pltpu.roll(wide, 1, 0))
    after = jnp.where(row == groups - 1, 0.0, pltpu.roll(wide, groups - 1, 0))
    return jnp.concatenate([cells, jnp.where(lane < 64, after, before).astype(BF16)], axis=1)


def fill_plane(taps, place, source, first, last):
    rows = source.shape[0]
    taps[place, 0] = with_edges(first)
    taps[place, rows + 1] = with_edges(last)

    def step(row, carry):
        taps[place, row + 1] = with_edges(source[row])
        return carry

    lax.fori_loop(0, rows, step, 0, unroll=2)


def build_weights(kernel, flip, out):
    lane = lax.broadcasted_iota(jnp.int32, (32, LANES), 1) // 32
    for tap_z in range(3):
        for tap_y in range(3):
            blocks = []
            for tap_x in range(3):
                at = (tap_z * 3 + tap_y) * 3 + tap_x
                at = 26 - at if flip else at
                block = kernel[at * 32 : at * 32 + 32, :].astype(F32)
                block = block.T if flip else block
                blocks.append(jnp.concatenate([block] * 4, axis=1))
            for place in range(8):
                voxel = place if place < 6 else place - 8
                total = jnp.zeros((32, LANES), F32)
                for tap_x in range(3):
                    total = jnp.where(lane == voxel - tap_x + 1, blocks[tap_x], total)
                out[tap_z, tap_y, place * 32 : place * 32 + 32, :] = total.astype(BF16)


CHUNK = 4


def fold(term):
    total = None
    for voxel in range(4):
        part = term[voxel * 32 : voxel * 32 + 32]
        shift = (-(voxel - 1) * 32) % 256
        if shift:
            part = pltpu.roll(part, shift, 1)
        total = part if total is None else total + part
    return total[:, :LANES]


def local_terms_body(low, high, edges, folded, bias_terms, turned, taps):
    rows, groups = low.shape[0] // 2, low.shape[1]
    sums = jnp.zeros((8, LANES), F32)
    blank = jnp.zeros((groups, LANES), BF16)
    for plane, source in enumerate((low, high)):
        span = slice(plane * LANES, (plane + 1) * LANES)
        flat = source[rows:].reshape(rows * groups, LANES)
        turned[span, :] = flat.T
        edges[0, span, :] = source[rows].T
        edges[1, span, :] = source[2 * rows - 1].T
        sums = sums + jnp.sum(flat.astype(F32).reshape(-1, 8, LANES), axis=0)
        fill_plane(taps, plane, source.at[:rows], blank, blank)
    bias_terms[...] = sums
    for tap_y in range(3):
        both = []
        for plane in range(2):
            rhs = taps[plane, tap_y : tap_y + rows].reshape(rows * groups, 256)
            both.append(jnp.dot(turned[...], rhs, preferred_element_type=F32))
        folded[1, tap_y] = fold(both[0][:LANES] + both[1][LANES:])
        folded[0, tap_y] = fold(both[0][LANES:])
        folded[2, tap_y] = fold(both[1][:LANES])


def kernel_grad_body(
    below, low, from_left, from_right, edges, folded, bias_terms, flag, keep, send, packed, taps, sums
):
    rows, groups = low.shape[0] // 2, low.shape[1]
    blank = jnp.zeros((groups, LANES), BF16)
    fill_plane(taps, 0, below.at[:rows], blank, blank)
    fill_plane(taps, 1, low.at[:rows], blank, blank)
    below_turned = below[rows : 2 * rows].reshape(rows * groups, LANES).T
    low_turned = low[rows:].reshape(rows * groups, LANES).T
    sums[1] = jnp.zeros(sums.shape[1:], F32)
    for tap_y in range(3):
        rhs = taps[0, tap_y : tap_y + rows].reshape(rows * groups, 256)
        sums[0, tap_y] = jnp.dot(low_turned, rhs, preferred_element_type=F32)
        rhs = taps[1, tap_y : tap_y + rows].reshape(rows * groups, 256)
        sums[2, tap_y] = jnp.dot(below_turned, rhs, preferred_element_type=F32)
    for side, lines in enumerate((from_left, from_right)):
        tap_y, end = 2 * side, side * (rows - 1)
        lhs = jnp.concatenate([edges[side], below[rows + end].T], axis=0)
        term = jnp.dot(lhs, with_edges(lines[0]), preferred_element_type=F32)
        sums[1, tap_y] += term[:LANES]
        sums[0, tap_y] += term[LANES : 2 * LANES]
        sums[2, tap_y] += term[2 * LANES :]
        term = jnp.dot(edges[side], with_edges(lines[2]), preferred_element_type=F32)
        sums[2, tap_y] += term[:LANES]
        sums[1, tap_y] += term[LANES:]
        sums[0, 2 - tap_y] += jnp.dot(lines[1].T, taps[0, 1 + end], preferred_element_type=F32)
    lane = lax.broadcasted_iota(jnp.int32, (32, LANES), 1)
    parts = [folded[at // 3, at % 3] + fold(sums[at // 3, at % 3]) for at in range(9)]
    row = jnp.sum(bias_terms[...], axis=0, keepdims=True)
    row = row + pltpu.roll(row, 64, 1)
    row = row + pltpu.roll(row, 32, 1)
    first = lax.broadcasted_iota(jnp.int32, (32, LANES), 0) == 0
    for place in range(7):
        if place < 6:
            extra = pltpu.roll(parts[7 + place // 3], 96 - 32 * (place % 3), 1)
        else:
            extra = jnp.where(first, jnp.broadcast_to(row, (32, LANES)), 0.0)
        packed[place * 32 : place * 32 + 32, :] = jnp.where(lane < 96, parts[place], extra)
    upper = flag[...] > 0.5
    keep[...] = jnp.where(upper, packed[HALF : 2 * HALF], packed[:HALF])
    send[...] = jnp.where(upper, packed[:HALF], packed[HALF : 2 * HALF])


def inner_sum(taps, weights, chunk, groups):
    total = None
    for plane in range(2):
        for tap_y in range(3):
            lhs = taps[plane, pl.ds(chunk * CHUNK + tap_y, CHUNK)].reshape(CHUNK * groups, 256)
            matrix = jnp.concatenate([weights[plane + 1, tap_y], weights[plane, tap_y]], axis=1)
            term = jnp.dot(lhs, matrix, preferred_element_type=F32)
            total = term if total is None else total + term
    return total


def inner_body(flip, low, high, from_left, from_right, kernel, partial, weights, taps):
    groups = low.shape[1]
    kind = 1 if flip else 0
    chunk = pl.program_id(0)

    @pl.when(chunk == 0)
    def _():
        build_weights(kernel, flip, weights)
        fill_plane(taps, 0, low, from_left[kind], from_right[kind])
        fill_plane(taps, 1, high, from_left[2 + kind], from_right[2 + kind])

    total = inner_sum(taps, weights, chunk, groups)
    for plane in range(2):
        part = total[:, plane * LANES : (plane + 1) * LANES]
        partial[plane] = part.reshape(CHUNK, groups, LANES)


def outer_body(turn, plane, source, left, right, weights, partial, line, *rest):
    out, taps, scratch = rest[-3:]
    rows, groups, _ = source.shape
    fill_plane(taps, 0, source, left[0], right[0])
    for chunk in range(rows // CHUNK):
        start = chunk * CHUNK
        total = partial[0, start : start + CHUNK].reshape(CHUNK * groups, LANES)
        for tap_y in range(3):
            lhs = taps[0, start + tap_y : start + tap_y + CHUNK].reshape(CHUNK * groups, 256)
            total = total + jnp.dot(lhs, weights[0, tap_y], preferred_element_type=F32)
        put_rows(scratch, turn(total, line), chunk, groups)
    lay_out(scratch, out, 0, rows, groups)


def rectified(total, line):
    return jnp.maximum(total + line[...], 0.0)


def kept(total, line):
    return total


def lay_out(scratch, out, plane, rows, groups):
    pitch = groups + 1
    for group in range(groups):
        halves = [scratch[pl.ds(half * 8 * pitch + group, 8, stride=pitch), :] for half in range(2)]
        block = jnp.concatenate(halves, axis=0).astype(BF16)
        out[plane, :, group * LANES : (group + 1) * LANES] = block


def put_rows(scratch, total, chunk, groups):
    for row in range(CHUNK):
        at = (chunk * CHUNK + row) * (groups + 1)
        scratch[at : at + groups, :] = total[row * groups : (row + 1) * groups]


HALF = 112


def unpack_body(scaling, part, other, flag, grad_kernel, grad_bias, packed):
    upper = flag[...] > 0.5
    packed[:HALF] = jnp.where(upper, other[...], part[...])
    packed[HALF : 2 * HALF] = jnp.where(upper, part[...], other[...])
    for place in range(7):
        block = packed[place * 32 : place * 32 + 32, :] * scaling
        turned = block.T
        grad_kernel[place * 96 : place * 96 + 96, :] = turned[:96]
        if place < 6:
            grad_kernel[(21 + place) * 32 : (22 + place) * 32, :] = turned[96:]
        else:
            grad_bias[...] = pltpu.roll(block, 32, 1)[:1, :32]


def shifted(value, axis, step):
    count = lax.axis_size(axis)
    pairs = [(i, i + step) for i in range(count) if 0 <= i + step < count]
    return lax.ppermute(value, axis, pairs)


def swapped(value, bit):
    count = lax.axis_size("gz") * lax.axis_size("gy")
    return lax.ppermute(value, ("gz", "gy"), [(i, i ^ bit) for i in range(count)])


def sum_of_four(value, low, high):
    one, two, three = (swapped(value, bit) for bit in (low, high, low + high))
    return (value + one) + (two + three)


def local(activations, grad_out, relu_mask, kernel, bias):
    planes, rows, width = activations.shape
    groups = width // LANES
    block = activations.shape
    shape = jax.ShapeDtypeStruct
    pair = shape((2 * rows, groups, LANES), BF16)
    lines = shape((4, groups, LANES), BF16)
    spread = pltpu.VMEM((rows * (groups + 1) + 8, LANES), F32)
    two_taps = pltpu.VMEM((2, rows + 2, groups, 2 * LANES), BF16)
    half = shape((HALF, LANES), F32)
    packed = pltpu.VMEM((2 * HALF, LANES), F32)
    flag = jnp.full((1, LANES), lax.axis_index("gy") % 2, F32)

    low, high, firsts, lasts = pl.pallas_call(
        group_body,
        in_specs=[pl.BlockSpec(memory_space=pl.ANY)] * 3,
        out_shape=(pair, pair, lines, lines),
        scratch_shapes=[
            spread, pltpu.VMEM(block, BF16), pltpu.VMEM(block, BF16), pltpu.VMEM(block, jnp.int32),
            pltpu.SemaphoreType.DMA((2, 3)),
        ],
        compiler_params=pltpu.CompilerParams(vmem_limit_bytes=56 * MIB),
    )(activations, grad_out, relu_mask)
    from_left = shifted(lasts, "gy", 1)
    from_right = shifted(firsts, "gy", -1)
    below = shifted(jnp.concatenate([high, from_left[2:], from_right[2:]]), "gz", 1)

    edges, folded, bias_terms = blocked(
        local_terms_body,
        1,
        (shape((2, 2 * LANES, groups), BF16), shape((3, 3, 32, LANES), F32), shape((8, LANES), F32)),
        (
            part_of((2, 2 * LANES, groups), 0, 0, 0), part_of((3, 3, 32, LANES), 0, 0, 0, 0),
            part_of((8, LANES), 0, 0),
        ),
        [pltpu.VMEM((2 * LANES, rows * groups), BF16), two_taps],
        (low, high),
        [part_of(pair.shape, 0, 0, 0)] * 2,
    )

    plane = (rows, groups, LANES)
    line = jnp.tile(bias, 4).reshape(1, LANES)
    flat_kernel = kernel.reshape(27 * 32, 32)

    def inner(kind):
        return blocked(
            functools.partial(inner_body, kind == 1),
            rows // CHUNK,
            (shape((2, *plane), F32), shape((3, 3, 256, LANES), BF16)),
            (
                pl.BlockSpec((2, CHUNK, groups, LANES), lambda step: (0, step, 0, 0)),
                part_of((3, 3, 256, LANES), 0, 0, 0, 0),
            ),
            [two_taps],
            (low, high, from_left, from_right, flat_kernel),
            [part_of(plane, kind, 0, 0)] * 2
            + [part_of(lines.shape, 0, 0, 0)] * 2
            + [part_of(flat_kernel.shape, 0, 0)],
        )

    def outer(kind, side, source, edge, weights, partial, done=None):
        row = (1, groups, LANES)
        args = [source, edge, edge, weights, partial, line]
        first = 2 * rows if edge is source else 0
        specs = [
            part_of(plane, kind, 0, 0), part_of(row, first + kind, 0, 0), part_of(row, first + 2 + kind, 0, 0),
            part_of((1, 3, 256, LANES), 2 * side, 0, 0, 0), part_of((1, *plane), side, 0, 0, 0),
            part_of((1, LANES), 0, 0),
        ]
        if done is not None:
            args.append(done)
            specs.append(pl.BlockSpec(memory_space=pl.ANY))
        return blocked(
            functools.partial(outer_body, kept if kind else rectified, side),
            1,
            shape(block, BF16),
            part_of((1, *block[1:]), side, 0, 0),
            [pltpu.VMEM((1, rows + 2, groups, 2 * LANES), BF16), spread],
            args,
            specs,
            None if done is None else {6: 0},
        )

    partial_f, weights_f = inner(0)
    partial_g, weights_g = inner(1)

    ends = (from_left[:2], from_right[:2])
    ends, folded, partial_f, partial_g = lax.optimization_barrier((ends, folded, partial_f, partial_g))
    down = jnp.concatenate([low, *ends])
    down, below = lax.optimization_barrier((down, below))
    above = shifted(down, "gz", -1)

    part, send = call(
        kernel_grad_body,
        (half, half),
        [packed, two_taps, pltpu.VMEM((3, 3, LANES, 256), F32)],
        (below, low, from_left, from_right, edges, folded, bias_terms, flag),
    )
    part = part + swapped(send, 1)
    part = sum_of_four(part, 4, 8)
    output = outer(0, 0, below, below, weights_f, partial_f)
    part, output = lax.optimization_barrier((part, output))
    part = sum_of_four(part, 32, 64)
    grad_input = outer(1, 0, below, below, weights_g, partial_g)
    part, above, grad_input = lax.optimization_barrier((part, above, grad_input))
    part = sum_of_four(part, 2, 16)
    output = outer(0, 1, above, above, weights_f, partial_f, output)
    part, output = lax.optimization_barrier((part, output))
    other = swapped(part, 1)
    grad_input = outer(1, 1, above, above, weights_g, partial_g, grad_input)

    voxels = planes * lax.axis_size("gz") * rows * lax.axis_size("gy") * (width // 32)
    grad_kernel, grad_bias = call(
        functools.partial(unpack_body, 1.0 / math.sqrt(voxels)),
        (shape((27 * 32, 32), F32), shape((1, 32), F32)),
        [packed],
        (part, other, flag),
    )
    return output, grad_input, grad_kernel.reshape(3, 3, 3, 32, 32), grad_bias.reshape(32)


def solution(mesh):
    block = P("gz", "gy", None)
    return jax.shard_map(
        local,
        mesh=mesh,
        in_specs=(block, block, block, P(), P()),
        out_specs=(block, block, P(), P()),
        check_vma=False,
    )
```

```python
import functools
import math

import jax
import jax.numpy as jnp
from jax import lax
from jax.experimental import pallas as pl
from jax.experimental.pallas import tpu as pltpu
from jax.sharding import PartitionSpec as P

F32 = jnp.float32
BF16 = jnp.bfloat16
LANES = 128
MIB = 1024 * 1024


def call(body, outs, scratch, args):
    return pl.pallas_call(
        body,
        out_shape=outs,
        scratch_shapes=scratch,
        compiler_params=pltpu.CompilerParams(vmem_limit_bytes=20 * MIB),
    )(*args)


def blocked(body, grid, outs, out_specs, scratch, args, in_specs, aliases=None, flops=0):
    return pl.pallas_call(
        body,
        grid=(grid,),
        out_shape=outs,
        in_specs=in_specs,
        out_specs=out_specs,
        scratch_shapes=scratch,
        input_output_aliases=aliases or {},
        cost_estimate=pl.CostEstimate(flops=flops, bytes_accessed=0, transcendentals=0),
        compiler_params=pltpu.CompilerParams(vmem_limit_bytes=56 * MIB),
    )(*args)


def part_of(shape, *index):
    return pl.BlockSpec(shape, lambda step: index)


def spread_rows(scratch, groups, group, block):
    pitch = groups + 1
    for half in range(2):
        scratch[pl.ds(half * 8 * pitch + group, 8, stride=pitch), :] = block[half * 8 : half * 8 + 8]


def group_body(act_in, grad_in, mask_in, low, high, firsts, lasts, scratch, act, grad, mask, arrived):
    rows, groups = act.shape[1], low.shape[1]
    copies = [
        [
            pltpu.make_async_copy(source.at[plane], target.at[plane], arrived.at[plane, place])
            for place, (source, target) in enumerate(((act_in, act), (mask_in, mask), (grad_in, grad)))
        ]
        for plane in range(2)
    ]
    for plane in (1, 0):
        for copy in copies[plane]:
            copy.start()
    for plane, out in ((1, high), (0, low)):
        for kind in range(2):
            for copy in copies[plane][:1] if kind == 0 else copies[plane][1:]:
                copy.wait()
            for group in range(groups):
                span = slice(group * LANES, (group + 1) * LANES)
                if kind == 0:
                    block = act[plane, :, span].astype(F32)
                else:
                    block = grad[plane, :, span].astype(F32) * mask[plane, :, span].astype(F32)
                spread_rows(scratch, groups, group, block)
            for row in range(rows):
                at = row * (groups + 1)
                out[kind * rows + row] = scratch[at : at + groups, :].astype(BF16)
            firsts[plane * 2 + kind] = out[kind * rows]
            lasts[plane * 2 + kind] = out[kind * rows + rows - 1]


def with_edges(cells):
    groups = cells.shape[0]
    wide = cells.astype(F32)
    lane = lax.broadcasted_iota(jnp.int32, wide.shape, 1)
    row = lax.broadcasted_iota(jnp.int32, wide.shape, 0)
    before = jnp.where(row == 0, 0.0, pltpu.roll(wide, 1, 0))
    after = jnp.where(row == groups - 1, 0.0, pltpu.roll(wide, groups - 1, 0))
    return jnp.concatenate([cells, jnp.where(lane < 64, after, before).astype(BF16)], axis=1)


def fill_plane(taps, place, source, first, last):
    rows = source.shape[0]
    taps[place, 0] = with_edges(first)
    taps[place, rows + 1] = with_edges(last)

    def step(row, carry):
        taps[place, row + 1] = with_edges(source[row])
        return carry

    lax.fori_loop(0, rows, step, 0, unroll=2)


def build_weights(kernel, flip, out):
    lane = lax.broadcasted_iota(jnp.int32, (32, LANES), 1) // 32
    for tap_z in range(3):
        for tap_y in range(3):
            blocks = []
            for tap_x in range(3):
                at = (tap_z * 3 + tap_y) * 3 + tap_x
                at = 26 - at if flip else at
                block = kernel[at * 32 : at * 32 + 32, :].astype(F32)
                block = block.T if flip else block
                blocks.append(jnp.concatenate([block] * 4, axis=1))
            for place in range(8):
                voxel = place if place < 6 else place - 8
                total = jnp.zeros((32, LANES), F32)
                for tap_x in range(3):
                    total = jnp.where(lane == voxel - tap_x + 1, blocks[tap_x], total)
                out[tap_z, tap_y, place * 32 : place * 32 + 32, :] = total.astype(BF16)


CHUNK = 4


def fold(term):
    total = None
    for voxel in range(4):
        part = term[voxel * 32 : voxel * 32 + 32]
        shift = (-(voxel - 1) * 32) % 256
        if shift:
            part = pltpu.roll(part, shift, 1)
        total = part if total is None else total + part
    return total[:, :LANES]


def local_terms_body(low, high, edges, folded, bias_terms, turned, taps):
    rows, groups = low.shape[0] // 2, low.shape[1]
    sums = jnp.zeros((8, LANES), F32)
    blank = jnp.zeros((groups, LANES), BF16)
    for plane, source in enumerate((low, high)):
        span = slice(plane * LANES, (plane + 1) * LANES)
        flat = source[rows:].reshape(rows * groups, LANES)
        turned[span, :] = flat.T
        edges[0, span, :] = source[rows].T
        edges[1, span, :] = source[2 * rows - 1].T
        sums = sums + jnp.sum(flat.astype(F32).reshape(-1, 8, LANES), axis=0)
        fill_plane(taps, plane, source.at[:rows], blank, blank)
    bias_terms[...] = sums
    for tap_y in range(3):
        both = []
        for plane in range(2):
            rhs = taps[plane, tap_y : tap_y + rows].reshape(rows * groups, 256)
            both.append(jnp.dot(turned[...], rhs, preferred_element_type=F32))
        folded[1, tap_y] = fold(both[0][:LANES] + both[1][LANES:])
        folded[0, tap_y] = fold(both[0][LANES:])
        folded[2, tap_y] = fold(both[1][:LANES])


def kernel_grad_body(
    below, low, from_left, from_right, edges, folded, bias_terms, flag, keep, send, packed, taps, sums
):
    rows, groups = below.shape[0] // 2, below.shape[1]
    blank = jnp.zeros((groups, LANES), BF16)
    fill_plane(taps, 0, below.at[:rows], blank, blank)
    fill_plane(taps, 1, low.at[:rows], blank, blank)
    below_turned = below[rows:].reshape(rows * groups, LANES).T
    low_turned = low[rows:].reshape(rows * groups, LANES).T
    sums[1] = jnp.zeros(sums.shape[1:], F32)
    for tap_y in range(3):
        rhs = taps[0, tap_y : tap_y + rows].reshape(rows * groups, 256)
        sums[0, tap_y] = jnp.dot(low_turned, rhs, preferred_element_type=F32)
        rhs = taps[1, tap_y : tap_y + rows].reshape(rows * groups, 256)
        sums[2, tap_y] = jnp.dot(below_turned, rhs, preferred_element_type=F32)
    for side, lines in enumerate((from_left, from_right)):
        tap_y, end = 2 * side, side * (rows - 1)
        lhs = jnp.concatenate([edges[side], below[rows + end].T], axis=0)
        term = jnp.dot(lhs, with_edges(lines[0]), preferred_element_type=F32)
        sums[1, tap_y] += term[:LANES]
        sums[0, tap_y] += term[LANES : 2 * LANES]
        sums[2, tap_y] += term[2 * LANES :]
        term = jnp.dot(edges[side], with_edges(lines[2]), preferred_element_type=F32)
        sums[2, tap_y] += term[:LANES]
        sums[1, tap_y] += term[LANES:]
        sums[0, 2 - tap_y] += jnp.dot(lines[1].T, taps[0, 1 + end], preferred_element_type=F32)
    lane = lax.broadcasted_iota(jnp.int32, (32, LANES), 1)
    parts = [folded[at // 3, at % 3] + fold(sums[at // 3, at % 3]) for at in range(9)]
    row = jnp.sum(bias_terms[...], axis=0, keepdims=True)
    row = row + pltpu.roll(row, 64, 1)
    row = row + pltpu.roll(row, 32, 1)
    first = lax.broadcasted_iota(jnp.int32, (32, LANES), 0) == 0
    for place in range(7):
        if place < 6:
            extra = pltpu.roll(parts[7 + place // 3], 96 - 32 * (place % 3), 1)
        else:
            extra = jnp.where(first, jnp.broadcast_to(row, (32, LANES)), 0.0)
        packed[place * 32 : place * 32 + 32, :] = jnp.where(lane < 96, parts[place], extra)
    upper = flag[...] > 0.5
    keep[...] = jnp.where(upper, packed[HALF : 2 * HALF], packed[:HALF])
    send[...] = jnp.where(upper, packed[:HALF], packed[HALF : 2 * HALF])


def inner_sum(taps, weights, chunk, groups):
    total = None
    for plane in range(2):
        for tap_y in range(3):
            lhs = taps[plane, pl.ds(chunk * CHUNK + tap_y, CHUNK)].reshape(CHUNK * groups, 256)
            matrix = jnp.concatenate([weights[plane + 1, tap_y], weights[plane, tap_y]], axis=1)
            term = jnp.dot(lhs, matrix, preferred_element_type=F32)
            total = term if total is None else total + term
    return total


def inner_body(flip, low, high, from_left, from_right, kernel, partial, weights, taps):
    groups = low.shape[1]
    kind = 1 if flip else 0
    chunk = pl.program_id(0)

    @pl.when(chunk == 0)
    def _():
        build_weights(kernel, flip, weights)
        fill_plane(taps, 0, low, from_left[kind], from_right[kind])
        fill_plane(taps, 1, high, from_left[2 + kind], from_right[2 + kind])

    total = inner_sum(taps, weights, chunk, groups)
    for plane in range(2):
        part = total[:, plane * LANES : (plane + 1) * LANES]
        partial[plane] = part.reshape(CHUNK, groups, LANES)


def outer_body(turn, plane, source, left, right, weights, partial, line, *rest):
    out, taps, scratch = rest[-3:]
    rows, groups, _ = source.shape
    fill_plane(taps, 0, source, left[0], right[0])
    for chunk in range(rows // CHUNK):
        start = chunk * CHUNK
        total = partial[0, start : start + CHUNK].reshape(CHUNK * groups, LANES)
        for tap_y in range(3):
            lhs = taps[0, start + tap_y : start + tap_y + CHUNK].reshape(CHUNK * groups, 256)
            total = total + jnp.dot(lhs, weights[0, tap_y], preferred_element_type=F32)
        put_rows(scratch, turn(total, line), chunk, groups)
    lay_out(scratch, out, 0, rows, groups)


def rectified(total, line):
    return jnp.maximum(total + line[...], 0.0)


def kept(total, line):
    return total


def lay_out(scratch, out, plane, rows, groups):
    pitch = groups + 1
    for group in range(groups):
        halves = [scratch[pl.ds(half * 8 * pitch + group, 8, stride=pitch), :] for half in range(2)]
        block = jnp.concatenate(halves, axis=0).astype(BF16)
        out[plane, :, group * LANES : (group + 1) * LANES] = block


def put_rows(scratch, total, chunk, groups):
    for row in range(CHUNK):
        at = (chunk * CHUNK + row) * (groups + 1)
        scratch[at : at + groups, :] = total[row * groups : (row + 1) * groups]


HALF = 112


def unpack_body(scaling, part, other, flag, grad_kernel, grad_bias, packed):
    upper = flag[...] > 0.5
    packed[:HALF] = jnp.where(upper, other[...], part[...])
    packed[HALF : 2 * HALF] = jnp.where(upper, part[...], other[...])
    for place in range(7):
        block = packed[place * 32 : place * 32 + 32, :] * scaling
        turned = block.T
        grad_kernel[place * 96 : place * 96 + 96, :] = turned[:96]
        if place < 6:
            grad_kernel[(21 + place) * 32 : (22 + place) * 32, :] = turned[96:]
        else:
            grad_bias[...] = pltpu.roll(block, 32, 1)[:1, :32]


def shifted(value, axis, step):
    count = lax.axis_size(axis)
    pairs = [(i, i + step) for i in range(count) if 0 <= i + step < count]
    return lax.ppermute(value, axis, pairs)


def swapped(value, bit):
    count = lax.axis_size("gz") * lax.axis_size("gy")
    return lax.ppermute(value, ("gz", "gy"), [(i, i ^ bit) for i in range(count)])


def sum_of_four(value, low, high):
    one, two, three = (swapped(value, bit) for bit in (low, high, low + high))
    return (value + one) + (two + three)


def local(activations, grad_out, relu_mask, kernel, bias):
    planes, rows, width = activations.shape
    groups = width // LANES
    block = activations.shape
    shape = jax.ShapeDtypeStruct
    pair = shape((2 * rows, groups, LANES), BF16)
    lines = shape((4, groups, LANES), BF16)
    spread = pltpu.VMEM((rows * (groups + 1) + 8, LANES), F32)
    two_taps = pltpu.VMEM((2, rows + 2, groups, 2 * LANES), BF16)
    half = shape((HALF, LANES), F32)
    packed = pltpu.VMEM((2 * HALF, LANES), F32)
    flag = jnp.full((1, LANES), lax.axis_index("gy") % 2, F32)

    low, high, firsts, lasts = pl.pallas_call(
        group_body,
        in_specs=[pl.BlockSpec(memory_space=pl.ANY)] * 3,
        out_shape=(pair, pair, lines, lines),
        scratch_shapes=[
            spread, pltpu.VMEM(block, BF16), pltpu.VMEM(block, BF16), pltpu.VMEM(block, jnp.int32),
            pltpu.SemaphoreType.DMA((2, 3)),
        ],
        compiler_params=pltpu.CompilerParams(vmem_limit_bytes=56 * MIB),
    )(activations, grad_out, relu_mask)
    from_left = shifted(lasts, "gy", 1)
    from_right = shifted(firsts, "gy", -1)
    below = shifted(high, "gz", 1)
    corner = shifted(jnp.concatenate([from_left[2:], from_right[2:]]), "gz", 1)

    edges, folded, bias_terms = blocked(
        local_terms_body,
        1,
        (shape((2, 2 * LANES, groups), BF16), shape((3, 3, 32, LANES), F32), shape((8, LANES), F32)),
        (
            part_of((2, 2 * LANES, groups), 0, 0, 0), part_of((3, 3, 32, LANES), 0, 0, 0, 0),
            part_of((8, LANES), 0, 0),
        ),
        [pltpu.VMEM((2 * LANES, rows * groups), BF16), two_taps],
        (low, high),
        [part_of(pair.shape, 0, 0, 0)] * 2,
        flops=0,
    )

    plane = (rows, groups, LANES)
    line = jnp.tile(bias, 4).reshape(1, LANES)
    flat_kernel = kernel.reshape(27 * 32, 32)

    def inner(kind):
        return blocked(
            functools.partial(inner_body, kind == 1),
            rows // CHUNK,
            (shape((2, *plane), F32), shape((3, 3, 256, LANES), BF16)),
            (
                pl.BlockSpec((2, CHUNK, groups, LANES), lambda step: (0, step, 0, 0)),
                part_of((3, 3, 256, LANES), 0, 0, 0, 0),
            ),
            [two_taps],
            (low, high, from_left, from_right, flat_kernel),
            [part_of(plane, kind, 0, 0)] * 2
            + [part_of(lines.shape, 0, 0, 0)] * 2
            + [part_of(flat_kernel.shape, 0, 0)],
        )

    def outer(kind, side, source, edge, weights, partial, done=None):
        row = (1, groups, LANES)
        args = [source, edge, edge, weights, partial, line]
        first = 2 * rows if edge is source else 0
        specs = [
            part_of(plane, kind, 0, 0), part_of(row, first + kind, 0, 0), part_of(row, first + 2 + kind, 0, 0),
            part_of((1, 3, 256, LANES), 2 * side, 0, 0, 0), part_of((1, *plane), side, 0, 0, 0),
            part_of((1, LANES), 0, 0),
        ]
        if done is not None:
            args.append(done)
            specs.append(pl.BlockSpec(memory_space=pl.ANY))
        return blocked(
            functools.partial(outer_body, kept if kind else rectified, side),
            1,
            shape(block, BF16),
            part_of((1, *block[1:]), side, 0, 0),
            [pltpu.VMEM((1, rows + 2, groups, 2 * LANES), BF16), spread],
            args,
            specs,
            None if done is None else {6: 0},
        )

    partial_f, weights_f = inner(0)
    partial_g, weights_g = inner(1)

    ends = (from_left[:2], from_right[:2])
    ends, folded, partial_f, partial_g = lax.optimization_barrier((ends, folded, partial_f, partial_g))
    down = jnp.concatenate([low, *ends])
    down, corner = lax.optimization_barrier((down, corner))
    above = shifted(down, "gz", -1)

    part, send = call(
        kernel_grad_body,
        (half, half),
        [packed, two_taps, pltpu.VMEM((3, 3, LANES, 256), F32)],
        (below, low, from_left, from_right, edges, folded, bias_terms, flag),
    )
    part = part + swapped(send, 1)
    part = sum_of_four(part, 4, 8)
    output = outer(0, 0, below, corner, weights_f, partial_f)
    part, output = lax.optimization_barrier((part, output))
    part = sum_of_four(part, 32, 64)
    grad_input = outer(1, 0, below, corner, weights_g, partial_g)
    part, above, grad_input = lax.optimization_barrier((part, above, grad_input))
    part = sum_of_four(part, 2, 16)
    output = outer(0, 1, above, above, weights_f, partial_f, output)
    part, output = lax.optimization_barrier((part, output))
    other = swapped(part, 1)
    grad_input = outer(1, 1, above, above, weights_g, partial_g, grad_input)

    voxels = planes * lax.axis_size("gz") * rows * lax.axis_size("gy") * (width // 32)
    grad_kernel, grad_bias = call(
        functools.partial(unpack_body, 1.0 / math.sqrt(voxels)),
        (shape((27 * 32, 32), F32), shape((1, 32), F32)),
        [packed],
        (part, other, flag),
    )
    return output, grad_input, grad_kernel.reshape(3, 3, 3, 32, 32), grad_bias.reshape(32)


def solution(mesh):
    block = P("gz", "gy", None)
    return jax.shard_map(
        local,
        mesh=mesh,
        in_specs=(block, block, block, P(), P()),
        out_specs=(block, block, P(), P()),
        check_vma=False,
    )
```

```python
import functools
import math

import jax
import jax.numpy as jnp
from jax import lax
from jax.experimental import pallas as pl
from jax.experimental.pallas import tpu as pltpu
from jax.sharding import PartitionSpec as P

F32 = jnp.float32
BF16 = jnp.bfloat16
LANES = 128
MIB = 1024 * 1024


def call(body, outs, scratch, args):
    return pl.pallas_call(
        body,
        out_shape=outs,
        scratch_shapes=scratch,
        compiler_params=pltpu.CompilerParams(vmem_limit_bytes=20 * MIB),
    )(*args)


def blocked(body, grid, outs, out_specs, scratch, args, in_specs, aliases=None, flops=0):
    return pl.pallas_call(
        body,
        grid=(grid,),
        out_shape=outs,
        in_specs=in_specs,
        out_specs=out_specs,
        scratch_shapes=scratch,
        input_output_aliases=aliases or {},
        cost_estimate=pl.CostEstimate(flops=flops, bytes_accessed=0, transcendentals=0),
        compiler_params=pltpu.CompilerParams(vmem_limit_bytes=56 * MIB),
    )(*args)


def part_of(shape, *index):
    return pl.BlockSpec(shape, lambda step: index)


def spread_rows(scratch, groups, group, block):
    pitch = groups + 1
    for half in range(2):
        scratch[pl.ds(half * 8 * pitch + group, 8, stride=pitch), :] = block[half * 8 : half * 8 + 8]


def group_body(act_in, grad_in, mask_in, low, high, firsts, lasts, scratch, act, grad, mask, arrived):
    rows, groups = act.shape[1], low.shape[1]
    copies = [
        [
            pltpu.make_async_copy(source.at[plane], target.at[plane], arrived.at[plane, place])
            for place, (source, target) in enumerate(((act_in, act), (mask_in, mask), (grad_in, grad)))
        ]
        for plane in range(2)
    ]
    for plane in (1, 0):
        for copy in copies[plane]:
            copy.start()
    for plane, out in ((1, high), (0, low)):
        for kind in range(2):
            for copy in copies[plane][:1] if kind == 0 else copies[plane][1:]:
                copy.wait()
            for group in range(groups):
                span = slice(group * LANES, (group + 1) * LANES)
                if kind == 0:
                    block = act[plane, :, span].astype(F32)
                else:
                    block = grad[plane, :, span].astype(F32) * mask[plane, :, span].astype(F32)
                spread_rows(scratch, groups, group, block)
            for row in range(rows):
                at = row * (groups + 1)
                out[kind * rows + row] = scratch[at : at + groups, :].astype(BF16)
            firsts[plane * 2 + kind] = out[kind * rows]
            lasts[plane * 2 + kind] = out[kind * rows + rows - 1]


def with_edges(cells):
    groups = cells.shape[0]
    wide = cells.astype(F32)
    lane = lax.broadcasted_iota(jnp.int32, wide.shape, 1)
    row = lax.broadcasted_iota(jnp.int32, wide.shape, 0)
    before = jnp.where(row == 0, 0.0, pltpu.roll(wide, 1, 0))
    after = jnp.where(row == groups - 1, 0.0, pltpu.roll(wide, groups - 1, 0))
    return jnp.concatenate([cells, jnp.where(lane < 64, after, before).astype(BF16)], axis=1)


def fill_plane(taps, place, source, first, last):
    rows = source.shape[0]
    taps[place, 0] = with_edges(first)
    taps[place, rows + 1] = with_edges(last)

    def step(row, carry):
        taps[place, row + 1] = with_edges(source[row])
        return carry

    lax.fori_loop(0, rows, step, 0, unroll=2)


def build_weights(kernel, flip, out):
    lane = lax.broadcasted_iota(jnp.int32, (32, LANES), 1) // 32
    for tap_z in range(3):
        for tap_y in range(3):
            blocks = []
            for tap_x in range(3):
                at = (tap_z * 3 + tap_y) * 3 + tap_x
                at = 26 - at if flip else at
                block = kernel[at * 32 : at * 32 + 32, :].astype(F32)
                block = block.T if flip else block
                blocks.append(jnp.concatenate([block] * 4, axis=1))
            for place in range(8):
                voxel = place if place < 6 else place - 8
                total = jnp.zeros((32, LANES), F32)
                for tap_x in range(3):
                    total = jnp.where(lane == voxel - tap_x + 1, blocks[tap_x], total)
                out[tap_z, tap_y, place * 32 : place * 32 + 32, :] = total.astype(BF16)


CHUNK = 4


def fold(term):
    total = None
    for voxel in range(4):
        part = term[voxel * 32 : voxel * 32 + 32]
        shift = (-(voxel - 1) * 32) % 256
        if shift:
            part = pltpu.roll(part, shift, 1)
        total = part if total is None else total + part
    return total[:, :LANES]


def own_body(
    low, high, from_left, from_right, kernel,
    folded, bias_terms, partial_f, weights_f, partial_g, weights_g, turned, taps,
):
    rows, groups = low.shape[0] // 2, low.shape[1]
    chunks = rows // CHUNK
    step = pl.program_id(0)

    def fill(kind):
        for plane, source in enumerate((low, high)):
            at = 2 * plane + kind
            fill_plane(taps, plane, source.at[kind * rows : kind * rows + rows], from_left[at], from_right[at])

    @pl.when(step == 0)
    def _():
        sums = jnp.zeros((8, LANES), F32)
        for plane, source in enumerate((low, high)):
            flat = source[rows:].reshape(rows * groups, LANES)
            turned[plane * LANES : (plane + 1) * LANES, :] = flat.T
            sums = sums + jnp.sum(flat.astype(F32).reshape(-1, 8, LANES), axis=0)
        bias_terms[...] = sums
        build_weights(kernel, False, weights_f)
        build_weights(kernel, True, weights_g)
        fill(0)
        for tap_y in range(3):
            both = []
            for plane in range(2):
                rhs = taps[plane, tap_y : tap_y + rows].reshape(rows * groups, 256)
                both.append(jnp.dot(turned[...], rhs, preferred_element_type=F32))
            folded[1, tap_y] = fold(both[0][:LANES] + both[1][LANES:])
            folded[0, tap_y] = fold(both[0][LANES:])
            folded[2, tap_y] = fold(both[1][:LANES])

    @pl.when(step == chunks)
    def _():
        fill(1)

    def add(weights, partial, chunk):
        total = inner_sum(taps, weights, chunk, groups)
        for plane in range(2):
            part = total[:, plane * LANES : (plane + 1) * LANES]
            partial[plane] = part.reshape(CHUNK, groups, LANES)

    @pl.when(step < chunks)
    def _():
        add(weights_f, partial_f, step)

    @pl.when(step >= chunks)
    def _():
        add(weights_g, partial_g, step - chunks)


def kernel_grad_body(below, low, from_left, from_right, folded, bias_terms, flag, keep, send, packed, taps, sums):
    rows, groups = low.shape[0] // 2, low.shape[1]
    blank = jnp.zeros((groups, LANES), BF16)
    fill_plane(taps, 0, below.at[:rows], blank, blank)
    fill_plane(taps, 1, low.at[:rows], from_left[0], from_right[0])
    below_turned = below[rows : 2 * rows].reshape(rows * groups, LANES).T
    low_turned = low[rows:].reshape(rows * groups, LANES).T
    for tap_y in range(3):
        rhs = taps[0, tap_y : tap_y + rows].reshape(rows * groups, 256)
        sums[0, tap_y] = jnp.dot(low_turned, rhs, preferred_element_type=F32)
        rhs = taps[1, tap_y : tap_y + rows].reshape(rows * groups, 256)
        sums[1, tap_y] = jnp.dot(below_turned, rhs, preferred_element_type=F32)
    sums[0, 2] += jnp.dot(from_left[1].T, taps[0, 1], preferred_element_type=F32)
    sums[0, 0] += jnp.dot(from_right[1].T, taps[0, rows], preferred_element_type=F32)
    lane = lax.broadcasted_iota(jnp.int32, (32, LANES), 1)
    parts = [folded[at // 3, at % 3] for at in range(9)]
    for tap_y in range(3):
        parts[tap_y] += fold(sums[0, tap_y])
        parts[6 + tap_y] += fold(sums[1, tap_y])
    row = jnp.sum(bias_terms[...], axis=0, keepdims=True)
    row = row + pltpu.roll(row, 64, 1)
    row = row + pltpu.roll(row, 32, 1)
    first = lax.broadcasted_iota(jnp.int32, (32, LANES), 0) == 0
    for place in range(7):
        if place < 6:
            extra = pltpu.roll(parts[7 + place // 3], 96 - 32 * (place % 3), 1)
        else:
            extra = jnp.where(first, jnp.broadcast_to(row, (32, LANES)), 0.0)
        packed[place * 32 : place * 32 + 32, :] = jnp.where(lane < 96, parts[place], extra)
    upper = flag[...] > 0.5
    keep[...] = jnp.where(upper, packed[HALF : 2 * HALF], packed[:HALF])
    send[...] = jnp.where(upper, packed[:HALF], packed[HALF : 2 * HALF])


def inner_sum(taps, weights, chunk, groups):
    total = None
    for plane in range(2):
        for tap_y in range(3):
            lhs = taps[plane, pl.ds(chunk * CHUNK + tap_y, CHUNK)].reshape(CHUNK * groups, 256)
            matrix = jnp.concatenate([weights[plane + 1, tap_y], weights[plane, tap_y]], axis=1)
            term = jnp.dot(lhs, matrix, preferred_element_type=F32)
            total = term if total is None else total + term
    return total


def outer_body(plane, source, edge, weights_f, weights_g, partial_f, partial_g, line, *rest):
    output, grad_input, taps, scratch = rest[-4:]
    rows, groups = partial_f.shape[1:3]
    first = edge.shape[0] - 4
    for kind, (weights, partial, out, turn) in enumerate(
        ((weights_f, partial_f, output, rectified), (weights_g, partial_g, grad_input, kept))
    ):
        span = source.at[kind * rows : kind * rows + rows]
        fill_plane(taps, kind, span, edge[first + kind], edge[first + 2 + kind])
        for chunk in range(rows // CHUNK):
            start = chunk * CHUNK
            total = partial[0, start : start + CHUNK].reshape(CHUNK * groups, LANES)
            for tap_y in range(3):
                at = start + tap_y
                lhs = taps[kind, at : at + CHUNK].reshape(CHUNK * groups, 256)
                total = total + jnp.dot(lhs, weights[0, tap_y], preferred_element_type=F32)
            put_rows(scratch, turn(total, line), chunk, groups)
        lay_out(scratch, out, 0, rows, groups)


def rectified(total, line):
    return jnp.maximum(total + line[...], 0.0)


def kept(total, line):
    return total


def lay_out(scratch, out, plane, rows, groups):
    pitch = groups + 1
    for group in range(groups):
        halves = [scratch[pl.ds(half * 8 * pitch + group, 8, stride=pitch), :] for half in range(2)]
        block = jnp.concatenate(halves, axis=0).astype(BF16)
        out[plane, :, group * LANES : (group + 1) * LANES] = block


def put_rows(scratch, total, chunk, groups):
    for row in range(CHUNK):
        at = (chunk * CHUNK + row) * (groups + 1)
        scratch[at : at + groups, :] = total[row * groups : (row + 1) * groups]


HALF = 112


def join_body(part, other, flag, packed):
    upper = flag[...] > 0.5
    packed[:HALF] = jnp.where(upper, other[...], part[...])
    packed[HALF : 2 * HALF] = jnp.where(upper, part[...], other[...])


def unpack_body(scaling, part, one, two, three, grad_kernel, grad_bias):
    for place in range(7):
        span = slice(place * 32, place * 32 + 32)
        block = ((part[span, :] + one[span, :]) + (two[span, :] + three[span, :])) * scaling
        turned = block.T
        grad_kernel[place * 96 : place * 96 + 96, :] = turned[:96]
        if place < 6:
            grad_kernel[(21 + place) * 32 : (22 + place) * 32, :] = turned[96:]
        else:
            grad_bias[...] = pltpu.roll(block, 32, 1)[:1, :32]


def shifted(value, axis, step):
    count = lax.axis_size(axis)
    pairs = [(i, i + step) for i in range(count) if 0 <= i + step < count]
    return lax.ppermute(value, axis, pairs)


def swapped(value, bit):
    count = lax.axis_size("gz") * lax.axis_size("gy")
    return lax.ppermute(value, ("gz", "gy"), [(i, i ^ bit) for i in range(count)])


def sum_of_four(value, low, high):
    one, two, three = (swapped(value, bit) for bit in (low, high, low + high))
    return (value + one) + (two + three)


def local(activations, grad_out, relu_mask, kernel, bias):
    planes, rows, width = activations.shape
    groups = width // LANES
    block = activations.shape
    shape = jax.ShapeDtypeStruct
    pair = shape((2 * rows, groups, LANES), BF16)
    lines = shape((4, groups, LANES), BF16)
    spread = pltpu.VMEM((rows * (groups + 1) + 8, LANES), F32)
    two_taps = pltpu.VMEM((2, rows + 2, groups, 2 * LANES), BF16)
    half = shape((HALF, LANES), F32)
    packed = pltpu.VMEM((2 * HALF, LANES), F32)
    flag = jnp.full((1, LANES), lax.axis_index("gy") % 2, F32)

    low, high, firsts, lasts = pl.pallas_call(
        group_body,
        in_specs=[pl.BlockSpec(memory_space=pl.ANY)] * 3,
        out_shape=(pair, pair, lines, lines),
        scratch_shapes=[
            spread, pltpu.VMEM(block, BF16), pltpu.VMEM(block, BF16), pltpu.VMEM(block, jnp.int32),
            pltpu.SemaphoreType.DMA((2, 3)),
        ],
        compiler_params=pltpu.CompilerParams(vmem_limit_bytes=56 * MIB),
    )(activations, grad_out, relu_mask)
    from_left = shifted(lasts, "gy", 1)
    from_right = shifted(firsts, "gy", -1)
    below = shifted(high, "gz", 1)
    corner = shifted(jnp.concatenate([from_left[2:], from_right[2:]]), "gz", 1)

    line = jnp.tile(bias, 4).reshape(1, LANES)
    flat_kernel = kernel.reshape(27 * 32, 32)
    chunks = rows // CHUNK
    plane = (rows, groups, LANES)
    folded_shape, bias_shape, weights_shape = (3, 3, 32, LANES), (8, LANES), (3, 3, 256, LANES)
    piece = (2, CHUNK, groups, LANES)
    folded, bias_terms, partial_f, weights_f, partial_g, weights_g = blocked(
        own_body,
        2 * chunks,
        (
            shape(folded_shape, F32), shape(bias_shape, F32),
            shape((2, *plane), F32), shape(weights_shape, BF16),
            shape((2, *plane), F32), shape(weights_shape, BF16),
        ),
        (
            part_of(folded_shape, 0, 0, 0, 0), part_of(bias_shape, 0, 0),
            pl.BlockSpec(piece, lambda step: (0, jnp.minimum(step, chunks - 1), 0, 0)),
            part_of(weights_shape, 0, 0, 0, 0),
            pl.BlockSpec(piece, lambda step: (0, jnp.maximum(step - chunks, 0), 0, 0)),
            part_of(weights_shape, 0, 0, 0, 0),
        ),
        [pltpu.VMEM((2 * LANES, rows * groups), BF16), two_taps],
        (low, high, from_left, from_right, flat_kernel),
        [part_of(pair.shape, 0, 0, 0)] * 2 + [part_of(lines.shape, 0, 0, 0)] * 2 + [part_of(flat_kernel.shape, 0, 0)],
    )

    def outer(side, source, edge, done=()):
        weights, partial = part_of((1, 3, 256, LANES), 2 * side, 0, 0, 0), part_of((1, *plane), side, 0, 0, 0)
        return blocked(
            functools.partial(outer_body, side),
            1,
            (shape(block, BF16), shape(block, BF16)),
            (part_of((1, *block[1:]), side, 0, 0),) * 2,
            [two_taps, spread],
            (source, edge, weights_f, weights_g, partial_f, partial_g, line, *done),
            [
                part_of(source.shape, 0, 0, 0), part_of(edge.shape, 0, 0, 0),
                weights, weights, partial, partial, part_of((1, LANES), 0, 0),
                *[pl.BlockSpec(memory_space=pl.ANY)] * len(done),
            ],
            {7: 0, 8: 1} if done else None,
        )

    ends = (from_left[:2], from_right[:2])
    ends, folded, partial_g = lax.optimization_barrier((ends, folded, partial_g))
    down = jnp.concatenate([low, *ends])
    down, corner = lax.optimization_barrier((down, corner))
    above = shifted(down, "gz", -1)

    part, send = call(
        kernel_grad_body,
        (half, half),
        [packed, two_taps, pltpu.VMEM((2, 3, LANES, 256), F32)],
        (below, low, from_left, from_right, folded, bias_terms, flag),
    )
    part = part + swapped(send, 1)
    part = sum_of_four(part, 4, 8)
    part = sum_of_four(part, 32, 64)
    results = outer(0, below, corner)
    part, results = lax.optimization_barrier((part, results))
    part = call(join_body, shape((2 * HALF, LANES), F32), [], (part, swapped(part, 1), flag))
    part, above = lax.optimization_barrier((part, above))
    others = [swapped(part, bit) for bit in (2, 16, 18)]
    results = outer(1, above, above, results)

    voxels = planes * lax.axis_size("gz") * rows * lax.axis_size("gy") * (width // 32)
    grad_kernel, grad_bias = call(
        functools.partial(unpack_body, 1.0 / math.sqrt(voxels)),
        (shape((27 * 32, 32), F32), shape((1, 32), F32)),
        [],
        (part, *others),
    )
    return *results, grad_kernel.reshape(3, 3, 3, 32, 32), grad_bias.reshape(32)


def solution(mesh):
    block = P("gz", "gy", None)
    return jax.shard_map(
        local,
        mesh=mesh,
        in_specs=(block, block, block, P(), P()),
        out_specs=(block, block, P(), P()),
        check_vma=False,
    )
```

```python
import functools
import math

import jax
import jax.numpy as jnp
from jax import lax
from jax.experimental import pallas as pl
from jax.experimental.pallas import tpu as pltpu
from jax.sharding import PartitionSpec as P

F32 = jnp.float32
BF16 = jnp.bfloat16
LANES = 128
MIB = 1024 * 1024


def call(body, outs, scratch, args):
    return pl.pallas_call(
        body,
        out_shape=outs,
        scratch_shapes=scratch,
        compiler_params=pltpu.CompilerParams(vmem_limit_bytes=20 * MIB),
    )(*args)


def blocked(body, grid, outs, out_specs, scratch, args, in_specs, aliases=None, flops=0):
    return pl.pallas_call(
        body,
        grid=(grid,),
        out_shape=outs,
        in_specs=in_specs,
        out_specs=out_specs,
        scratch_shapes=scratch,
        input_output_aliases=aliases or {},
        cost_estimate=pl.CostEstimate(flops=flops, bytes_accessed=0, transcendentals=0),
        compiler_params=pltpu.CompilerParams(vmem_limit_bytes=56 * MIB),
    )(*args)


def part_of(shape, *index):
    return pl.BlockSpec(shape, lambda step: index)


def spread_rows(scratch, groups, group, block):
    pitch = groups + 1
    for half in range(2):
        scratch[pl.ds(half * 8 * pitch + group, 8, stride=pitch), :] = block[half * 8 : half * 8 + 8]


def group_body(act_in, grad_in, mask_in, low, high_first, high_rest, firsts, lasts, scratch, act, grad, mask, arrived):
    rows, groups = act.shape[1], low.shape[1]
    copies = [
        [
            pltpu.make_async_copy(source.at[plane], target.at[plane], arrived.at[plane, place])
            for place, (source, target) in enumerate(((act_in, act), (mask_in, mask), (grad_in, grad)))
        ]
        for plane in range(2)
    ]
    for plane in (1, 0):
        for copy in copies[plane]:
            copy.start()
    for plane in (1, 0):
        for kind in range(2):
            out = high_first if plane else low
            for copy in copies[plane][:1] if kind == 0 else copies[plane][1:]:
                copy.wait()
            for group in range(groups):
                span = slice(group * LANES, (group + 1) * LANES)
                if kind == 0:
                    block = act[plane, :, span].astype(F32)
                else:
                    block = grad[plane, :, span].astype(F32) * mask[plane, :, span].astype(F32)
                spread_rows(scratch, groups, group, block)
            for row in range(rows):
                at = row * (groups + 1)
                cells = scratch[at : at + groups, :].astype(BF16)
                if plane and kind and row >= EARLY:
                    high_rest[row - EARLY] = cells
                else:
                    out[kind * rows + row] = cells
                if row == 0:
                    firsts[plane * 2 + kind] = cells
                if row == rows - 1:
                    lasts[plane * 2 + kind] = cells


def with_edges(cells):
    groups = cells.shape[0]
    wide = cells.astype(F32)
    lane = lax.broadcasted_iota(jnp.int32, wide.shape, 1)
    row = lax.broadcasted_iota(jnp.int32, wide.shape, 0)
    before = jnp.where(row == 0, 0.0, pltpu.roll(wide, 1, 0))
    after = jnp.where(row == groups - 1, 0.0, pltpu.roll(wide, groups - 1, 0))
    return jnp.concatenate([cells, jnp.where(lane < 64, after, before).astype(BF16)], axis=1)


def fill_plane(taps, place, source, first, last):
    rows = source.shape[0]
    taps[place, 0] = with_edges(first)
    taps[place, rows + 1] = with_edges(last)

    def step(row, carry):
        taps[place, row + 1] = with_edges(source[row])
        return carry

    lax.fori_loop(0, rows, step, 0, unroll=2)


def build_weights(kernel, flip, out):
    lane = lax.broadcasted_iota(jnp.int32, (32, LANES), 1) // 32
    for tap_z in range(3):
        for tap_y in range(3):
            blocks = []
            for tap_x in range(3):
                at = (tap_z * 3 + tap_y) * 3 + tap_x
                at = 26 - at if flip else at
                block = kernel[at * 32 : at * 32 + 32, :].astype(F32)
                block = block.T if flip else block
                blocks.append(jnp.concatenate([block] * 4, axis=1))
            for place in range(8):
                voxel = place if place < 6 else place - 8
                total = jnp.zeros((32, LANES), F32)
                for tap_x in range(3):
                    total = jnp.where(lane == voxel - tap_x + 1, blocks[tap_x], total)
                out[tap_z, tap_y, place * 32 : place * 32 + 32, :] = total.astype(BF16)


CHUNK = 4
EARLY = 8


def fold(term):
    total = None
    for voxel in range(4):
        part = term[voxel * 32 : voxel * 32 + 32]
        shift = (-(voxel - 1) * 32) % 256
        if shift:
            part = pltpu.roll(part, shift, 1)
        total = part if total is None else total + part
    return total[:, :LANES]


def gather_grad(first, rest, grad):
    rows = grad.shape[0]
    if first.shape == rest.shape:
        grad[...] = first[rows : 2 * rows]
    else:
        grad[:EARLY] = first[rows:]
        grad[EARLY:] = rest[: rows - EARLY]


def own_body(
    low, high_first, high_rest, from_left, from_right, kernel,
    folded, bias_terms, partial_f, weights_f, partial_g, weights_g, turned, taps, high_grad,
):
    rows, groups = low.shape[0] // 2, low.shape[1]
    chunks = rows // CHUNK
    step = pl.program_id(0)

    def fill(kind):
        for plane, source in enumerate((low.at[kind * rows : kind * rows + rows], (high_first.at[:rows], high_grad)[kind])):
            at = 2 * plane + kind
            fill_plane(taps, plane, source, from_left[at], from_right[at])

    @pl.when(step == 0)
    def _():
        gather_grad(high_first, high_rest, high_grad)
        sums = jnp.zeros((8, LANES), F32)
        for plane, source in enumerate((low.at[rows:], high_grad)):
            flat = source[...].reshape(rows * groups, LANES)
            turned[plane * LANES : (plane + 1) * LANES, :] = flat.T
            sums = sums + jnp.sum(flat.astype(F32).reshape(-1, 8, LANES), axis=0)
        bias_terms[...] = sums
        build_weights(kernel, False, weights_f)
        build_weights(kernel, True, weights_g)
        fill(0)
        for tap_y in range(3):
            both = []
            for plane in range(2):
                rhs = taps[plane, tap_y : tap_y + rows].reshape(rows * groups, 256)
                both.append(jnp.dot(turned[...], rhs, preferred_element_type=F32))
            folded[1, tap_y] = fold(both[0][:LANES] + both[1][LANES:])
            folded[0, tap_y] = fold(both[0][LANES:])
            folded[2, tap_y] = fold(both[1][:LANES])

    @pl.when(step == chunks)
    def _():
        fill(1)

    def add(weights, partial, chunk):
        total = inner_sum(taps, weights, chunk, groups)
        for plane in range(2):
            part = total[:, plane * LANES : (plane + 1) * LANES]
            partial[plane] = part.reshape(CHUNK, groups, LANES)

    @pl.when(step < chunks)
    def _():
        add(weights_f, partial_f, step)

    @pl.when(step >= chunks)
    def _():
        add(weights_g, partial_g, step - chunks)


def kernel_grad_body(
    below_first, below_rest, low, from_left, from_right, folded, bias_terms, flag,
    keep, send, packed, taps, sums, below_grad,
):
    rows, groups = low.shape[0] // 2, low.shape[1]
    blank = jnp.zeros((groups, LANES), BF16)
    gather_grad(below_first, below_rest, below_grad)
    fill_plane(taps, 0, below_first.at[:rows], blank, blank)
    fill_plane(taps, 1, low.at[:rows], from_left[0], from_right[0])
    below_turned = below_grad[...].reshape(rows * groups, LANES).T
    low_turned = low[rows:].reshape(rows * groups, LANES).T
    for tap_y in range(3):
        rhs = taps[0, tap_y : tap_y + rows].reshape(rows * groups, 256)
        sums[0, tap_y] = jnp.dot(low_turned, rhs, preferred_element_type=F32)
        rhs = taps[1, tap_y : tap_y + rows].reshape(rows * groups, 256)
        sums[1, tap_y] = jnp.dot(below_turned, rhs, preferred_element_type=F32)
    sums[0, 2] += jnp.dot(from_left[1].T, taps[0, 1], preferred_element_type=F32)
    sums[0, 0] += jnp.dot(from_right[1].T, taps[0, rows], preferred_element_type=F32)
    lane = lax.broadcasted_iota(jnp.int32, (32, LANES), 1)
    parts = [folded[at // 3, at % 3] for at in range(9)]
    for tap_y in range(3):
        parts[tap_y] += fold(sums[0, tap_y])
        parts[6 + tap_y] += fold(sums[1, tap_y])
    row = jnp.sum(bias_terms[...], axis=0, keepdims=True)
    row = row + pltpu.roll(row, 64, 1)
    row = row + pltpu.roll(row, 32, 1)
    first = lax.broadcasted_iota(jnp.int32, (32, LANES), 0) == 0
    for place in range(7):
        if place < 6:
            extra = pltpu.roll(parts[7 + place // 3], 96 - 32 * (place % 3), 1)
        else:
            extra = jnp.where(first, jnp.broadcast_to(row, (32, LANES)), 0.0)
        packed[place * 32 : place * 32 + 32, :] = jnp.where(lane < 96, parts[place], extra)
    upper = flag[...] > 0.5
    keep[...] = jnp.where(upper, packed[HALF : 2 * HALF], packed[:HALF])
    send[...] = jnp.where(upper, packed[:HALF], packed[HALF : 2 * HALF])


def inner_sum(taps, weights, chunk, groups):
    total = None
    for plane in range(2):
        for tap_y in range(3):
            lhs = taps[plane, pl.ds(chunk * CHUNK + tap_y, CHUNK)].reshape(CHUNK * groups, 256)
            matrix = jnp.concatenate([weights[plane + 1, tap_y], weights[plane, tap_y]], axis=1)
            term = jnp.dot(lhs, matrix, preferred_element_type=F32)
            total = term if total is None else total + term
    return total


def outer_body(first, rest, weights_f, weights_g, partial_f, partial_g, line, *more):
    output, grad_input, taps, scratch, grad = more[-5:]
    rows, groups = partial_f.shape[1:3]
    act, edge = first.at[:rows], rest.at[rest.shape[0] - 4 :]
    gather_grad(first, rest, grad)
    for kind, (source, weights, partial, out, turn) in enumerate(
        (
            (act, weights_f, partial_f, output, rectified),
            (grad, weights_g, partial_g, grad_input, kept),
        )
    ):
        fill_plane(taps, kind, source, edge[kind], edge[2 + kind])
        for chunk in range(rows // CHUNK):
            start = chunk * CHUNK
            total = partial[0, start : start + CHUNK].reshape(CHUNK * groups, LANES)
            for tap_y in range(3):
                at = start + tap_y
                lhs = taps[kind, at : at + CHUNK].reshape(CHUNK * groups, 256)
                total = total + jnp.dot(lhs, weights[0, tap_y], preferred_element_type=F32)
            put_rows(scratch, turn(total, line), chunk, groups)
        lay_out(scratch, out, 0, rows, groups)


def rectified(total, line):
    return jnp.maximum(total + line[...], 0.0)


def kept(total, line):
    return total


def lay_out(scratch, out, plane, rows, groups):
    pitch = groups + 1
    for group in range(groups):
        halves = [scratch[pl.ds(half * 8 * pitch + group, 8, stride=pitch), :] for half in range(2)]
        block = jnp.concatenate(halves, axis=0).astype(BF16)
        out[plane, :, group * LANES : (group + 1) * LANES] = block


def put_rows(scratch, total, chunk, groups):
    for row in range(CHUNK):
        at = (chunk * CHUNK + row) * (groups + 1)
        scratch[at : at + groups, :] = total[row * groups : (row + 1) * groups]


HALF = 112


def join_body(part, other, flag, packed):
    upper = flag[...] > 0.5
    packed[:HALF] = jnp.where(upper, other[...], part[...])
    packed[HALF : 2 * HALF] = jnp.where(upper, part[...], other[...])


def unpack_body(scaling, part, one, two, three, grad_kernel, grad_bias):
    for place in range(7):
        span = slice(place * 32, place * 32 + 32)
        block = ((part[span, :] + one[span, :]) + (two[span, :] + three[span, :])) * scaling
        turned = block.T
        grad_kernel[place * 96 : place * 96 + 96, :] = turned[:96]
        if place < 6:
            grad_kernel[(21 + place) * 32 : (22 + place) * 32, :] = turned[96:]
        else:
            grad_bias[...] = pltpu.roll(block, 32, 1)[:1, :32]


def shifted(value, axis, step):
    count = lax.axis_size(axis)
    pairs = [(i, i + step) for i in range(count) if 0 <= i + step < count]
    return lax.ppermute(value, axis, pairs)


def swapped(value, bit):
    count = lax.axis_size("gz") * lax.axis_size("gy")
    return lax.ppermute(value, ("gz", "gy"), [(i, i ^ bit) for i in range(count)])


def sum_of_four(value, low, high):
    one, two, three = (swapped(value, bit) for bit in (low, high, low + high))
    return (value + one) + (two + three)


def local(activations, grad_out, relu_mask, kernel, bias):
    planes, rows, width = activations.shape
    groups = width // LANES
    block = activations.shape
    shape = jax.ShapeDtypeStruct
    pair = shape((2 * rows, groups, LANES), BF16)
    one_plane = pltpu.VMEM((rows, groups, LANES), BF16)
    lines = shape((4, groups, LANES), BF16)
    spread = pltpu.VMEM((rows * (groups + 1) + 8, LANES), F32)
    two_taps = pltpu.VMEM((2, rows + 2, groups, 2 * LANES), BF16)
    half = shape((HALF, LANES), F32)
    packed = pltpu.VMEM((2 * HALF, LANES), F32)
    flag = jnp.full((1, LANES), lax.axis_index("gy") % 2, F32)

    low, high_first, high_rest, firsts, lasts = pl.pallas_call(
        group_body,
        in_specs=[pl.BlockSpec(memory_space=pl.ANY)] * 3,
        out_shape=(
            pair, shape((rows + EARLY, groups, LANES), BF16), shape((rows - EARLY, groups, LANES), BF16), lines, lines,
        ),
        scratch_shapes=[
            spread, pltpu.VMEM(block, BF16), pltpu.VMEM(block, BF16), pltpu.VMEM(block, jnp.int32),
            pltpu.SemaphoreType.DMA((2, 3)),
        ],
        compiler_params=pltpu.CompilerParams(vmem_limit_bytes=56 * MIB),
    )(activations, grad_out, relu_mask)
    from_left = shifted(lasts, "gy", 1)
    from_right = shifted(firsts, "gy", -1)
    below_first = shifted(high_first, "gz", 1)
    below_rest = shifted(jnp.concatenate([high_rest, from_left[2:], from_right[2:]]), "gz", 1)

    line = jnp.tile(bias, 4).reshape(1, LANES)
    flat_kernel = kernel.reshape(27 * 32, 32)
    chunks = rows // CHUNK
    plane = (rows, groups, LANES)
    folded_shape, bias_shape, weights_shape = (3, 3, 32, LANES), (8, LANES), (3, 3, 256, LANES)
    piece = (2, CHUNK, groups, LANES)
    folded, bias_terms, partial_f, weights_f, partial_g, weights_g = blocked(
        own_body,
        2 * chunks,
        (
            shape(folded_shape, F32), shape(bias_shape, F32),
            shape((2, *plane), F32), shape(weights_shape, BF16),
            shape((2, *plane), F32), shape(weights_shape, BF16),
        ),
        (
            part_of(folded_shape, 0, 0, 0, 0), part_of(bias_shape, 0, 0),
            pl.BlockSpec(piece, lambda step: (0, jnp.minimum(step, chunks - 1), 0, 0)),
            part_of(weights_shape, 0, 0, 0, 0),
            pl.BlockSpec(piece, lambda step: (0, jnp.maximum(step - chunks, 0), 0, 0)),
            part_of(weights_shape, 0, 0, 0, 0),
        ),
        [pltpu.VMEM((2 * LANES, rows * groups), BF16), two_taps, one_plane],
        (low, high_first, high_rest, from_left, from_right, flat_kernel),
        [part_of(array.shape, 0, 0, 0) for array in (low, high_first, high_rest)] + [part_of(lines.shape, 0, 0, 0)] * 2 + [part_of(flat_kernel.shape, 0, 0)],
    )

    def outer(side, first, rest, done=()):
        weights, partial = part_of((1, 3, 256, LANES), 2 * side, 0, 0, 0), part_of((1, *plane), side, 0, 0, 0)
        return blocked(
            outer_body,
            1,
            (shape(block, BF16), shape(block, BF16)),
            (part_of((1, *block[1:]), side, 0, 0),) * 2,
            [two_taps, spread, one_plane],
            (first, rest, weights_f, weights_g, partial_f, partial_g, line, *done),
            [
                part_of(first.shape, 0, 0, 0), part_of(rest.shape, 0, 0, 0),
                weights, weights, partial, partial, part_of((1, LANES), 0, 0),
                *[pl.BlockSpec(memory_space=pl.ANY)] * len(done),
            ],
            {7: 0, 8: 1} if done else None,
        )

    ends = (from_left[:2], from_right[:2])
    ends, folded, partial_g = lax.optimization_barrier((ends, folded, partial_g))
    down = jnp.concatenate([low, *ends])
    above = shifted(down, "gz", -1)

    part, send = call(
        kernel_grad_body,
        (half, half),
        [packed, two_taps, pltpu.VMEM((2, 3, LANES, 256), F32), one_plane],
        (below_first, below_rest, low, from_left, from_right, folded, bias_terms, flag),
    )
    part = part + swapped(send, 1)
    part = sum_of_four(part, 4, 8)
    part = sum_of_four(part, 32, 64)
    results = outer(0, below_first, below_rest)
    part, results = lax.optimization_barrier((part, results))
    part = call(join_body, shape((2 * HALF, LANES), F32), [], (part, swapped(part, 1), flag))
    part, above = lax.optimization_barrier((part, above))
    others = [swapped(part, bit) for bit in (2, 16, 18)]
    results = outer(1, above, above, results)

    voxels = planes * lax.axis_size("gz") * rows * lax.axis_size("gy") * (width // 32)
    grad_kernel, grad_bias = call(
        functools.partial(unpack_body, 1.0 / math.sqrt(voxels)),
        (shape((27 * 32, 32), F32), shape((1, 32), F32)),
        [],
        (part, *others),
    )
    return *results, grad_kernel.reshape(3, 3, 3, 32, 32), grad_bias.reshape(32)


def solution(mesh):
    block = P("gz", "gy", None)
    return jax.shard_map(
        local,
        mesh=mesh,
        in_specs=(block, block, block, P(), P()),
        out_specs=(block, block, P(), P()),
        check_vma=False,
    )
```

```python
import functools
import math

import jax
import jax.numpy as jnp
from jax import lax
from jax.experimental import pallas as pl
from jax.experimental.pallas import tpu as pltpu
from jax.sharding import PartitionSpec as P

F32 = jnp.float32
BF16 = jnp.bfloat16
LANES = 128
MIB = 1024 * 1024


def call(body, outs, scratch, args):
    return pl.pallas_call(
        body,
        out_shape=outs,
        scratch_shapes=scratch,
        compiler_params=pltpu.CompilerParams(vmem_limit_bytes=20 * MIB),
    )(*args)


def blocked(body, grid, outs, out_specs, scratch, args, in_specs, aliases=None, flops=0):
    return pl.pallas_call(
        body,
        grid=(grid,),
        out_shape=outs,
        in_specs=in_specs,
        out_specs=out_specs,
        scratch_shapes=scratch,
        input_output_aliases=aliases or {},
        cost_estimate=pl.CostEstimate(flops=flops, bytes_accessed=0, transcendentals=0),
        compiler_params=pltpu.CompilerParams(vmem_limit_bytes=56 * MIB),
    )(*args)


def part_of(shape, *index):
    return pl.BlockSpec(shape, lambda step: index)


def spread_rows(scratch, groups, group, block):
    pitch = groups + 1
    for half in range(2):
        scratch[pl.ds(half * 8 * pitch + group, 8, stride=pitch), :] = block[half * 8 : half * 8 + 8]


def group_body(act_in, grad_in, mask_in, low, high_first, high_rest, firsts, lasts, scratch, act, grad, mask, arrived):
    rows, groups = act.shape[1], low.shape[1]
    copies = [
        [
            pltpu.make_async_copy(source.at[plane], target.at[plane], arrived.at[plane, place])
            for place, (source, target) in enumerate(((act_in, act), (mask_in, mask), (grad_in, grad)))
        ]
        for plane in range(2)
    ]
    for plane in (1, 0):
        for copy in copies[plane]:
            copy.start()
    for plane in (1, 0):
        for kind in range(2):
            out = high_first if plane else low
            for copy in copies[plane][:1] if kind == 0 else copies[plane][1:]:
                copy.wait()
            for group in range(groups):
                span = slice(group * LANES, (group + 1) * LANES)
                if kind == 0:
                    block = act[plane, :, span].astype(F32)
                else:
                    block = grad[plane, :, span].astype(F32) * mask[plane, :, span].astype(F32)
                spread_rows(scratch, groups, group, block)
            for row in range(rows):
                at = row * (groups + 1)
                cells = scratch[at : at + groups, :].astype(BF16)
                if plane and kind and row >= EARLY:
                    high_rest[row - EARLY] = cells
                else:
                    out[kind * rows + row] = cells
                if row == 0:
                    firsts[plane * 2 + kind] = cells
                if row == rows - 1:
                    lasts[plane * 2 + kind] = cells


def with_edges(cells):
    groups = cells.shape[0]
    wide = cells.astype(F32)
    lane = lax.broadcasted_iota(jnp.int32, wide.shape, 1)
    row = lax.broadcasted_iota(jnp.int32, wide.shape, 0)
    before = jnp.where(row == 0, 0.0, pltpu.roll(wide, 1, 0))
    after = jnp.where(row == groups - 1, 0.0, pltpu.roll(wide, groups - 1, 0))
    return jnp.concatenate([cells, jnp.where(lane < 64, after, before).astype(BF16)], axis=1)


def fill_plane(taps, place, source, first, last):
    rows = source.shape[0]
    taps[place, 0] = with_edges(first)
    taps[place, rows + 1] = with_edges(last)

    def step(row, carry):
        taps[place, row + 1] = with_edges(source[row])
        return carry

    lax.fori_loop(0, rows, step, 0, unroll=2)


def build_weights(kernel, flip, out):
    lane = lax.broadcasted_iota(jnp.int32, (32, LANES), 1) // 32
    for tap_z in range(3):
        for tap_y in range(3):
            blocks = []
            for tap_x in range(3):
                at = (tap_z * 3 + tap_y) * 3 + tap_x
                at = 26 - at if flip else at
                block = kernel[at * 32 : at * 32 + 32, :].astype(F32)
                block = block.T if flip else block
                blocks.append(jnp.concatenate([block] * 4, axis=1))
            for place in range(8):
                voxel = place if place < 6 else place - 8
                total = jnp.zeros((32, LANES), F32)
                for tap_x in range(3):
                    total = jnp.where(lane == voxel - tap_x + 1, blocks[tap_x], total)
                out[tap_z, tap_y, place * 32 : place * 32 + 32, :] = total.astype(BF16)


CHUNK = 4
WIDE_CHUNK = 8
EARLY = 8


def fold(term):
    near, far = term[:, :LANES], term[:, LANES:]
    lane = lax.broadcasted_iota(jnp.int32, (32, LANES), 1)
    first = pltpu.roll(jnp.where(lane < 96, near[:32], far[:32]), 32, 1)
    third = pltpu.roll(near[64:96], 96, 1)
    fourth = pltpu.roll(jnp.where(lane < 32, far[96:], near[96:]), 64, 1)
    return (first + near[32:64]) + (third + fourth)


def gather_grad(first, rest, grad):
    rows = grad.shape[0]
    early = first.shape[0] - rows
    if early:
        grad[:early] = first[rows:]
    grad[early:] = rest[: rows - early]


def own_body(
    low, high_first, high_rest, from_left, from_right, kernel,
    folded, bias_terms, partial, weights, turned, taps, high_grad,
):
    rows, groups = low.shape[0] // 2, low.shape[1]
    step = pl.program_id(0)

    def fill(kind):
        for plane, source in enumerate((low.at[kind * rows : kind * rows + rows], (high_first.at[:rows], high_grad)[kind])):
            at = 2 * plane + kind
            fill_plane(taps, plane, source, from_left[at], from_right[at])
        build_weights(kernel, kind == 1, weights.at[0])

    @pl.when(step == 0)
    def _():
        gather_grad(high_first, high_rest, high_grad)
        sums = jnp.zeros((8, LANES), F32)
        for plane, source in enumerate((low.at[rows:], high_grad)):
            flat = source[...].reshape(rows * groups, LANES)
            turned[plane * LANES : (plane + 1) * LANES, :] = flat.T
            sums = sums + jnp.sum(flat.astype(F32).reshape(-1, 8, LANES), axis=0)
        bias_terms[...] = sums
        fill(0)
        for tap_y in range(3):
            both = []
            for plane in range(2):
                rhs = taps[plane, tap_y : tap_y + rows].reshape(rows * groups, 256)
                both.append(jnp.dot(turned[...], rhs, preferred_element_type=F32))
            folded[1, tap_y] = fold(both[0][:LANES] + both[1][LANES:])
            folded[0, tap_y] = fold(both[0][LANES:])
            folded[2, tap_y] = fold(both[1][:LANES])

    @pl.when(step == 1)
    def _():
        fill(1)

    def add(chunk, carry):
        total = inner_sum(taps, weights.at[0], chunk, groups)
        for plane in range(2):
            part = total[:, plane * LANES : (plane + 1) * LANES]
            partial[0, plane, pl.ds(chunk * WIDE_CHUNK, WIDE_CHUNK)] = part.reshape(WIDE_CHUNK, groups, LANES)
        return carry

    lax.fori_loop(0, rows // WIDE_CHUNK, add, 0)


def kernel_grad_body(
    below_first, below_rest, low, from_left, from_right, folded, bias_terms, flag,
    keep, send, packed, taps, sums, below_grad,
):
    rows, groups = low.shape[0] // 2, low.shape[1]
    blank = jnp.zeros((groups, LANES), BF16)
    gather_grad(below_first, below_rest, below_grad)
    fill_plane(taps, 0, below_first.at[:rows], blank, blank)
    fill_plane(taps, 1, low.at[:rows], from_left[0], from_right[0])
    below_turned = below_grad[...].reshape(rows * groups, LANES).T
    low_turned = low[rows:].reshape(rows * groups, LANES).T
    for tap_y in range(3):
        rhs = taps[0, tap_y : tap_y + rows].reshape(rows * groups, 256)
        sums[0, tap_y] = jnp.dot(low_turned, rhs, preferred_element_type=F32)
        rhs = taps[1, tap_y : tap_y + rows].reshape(rows * groups, 256)
        sums[1, tap_y] = jnp.dot(below_turned, rhs, preferred_element_type=F32)
    sums[0, 2] += jnp.dot(from_left[1].T, taps[0, 1], preferred_element_type=F32)
    sums[0, 0] += jnp.dot(from_right[1].T, taps[0, rows], preferred_element_type=F32)
    lane = lax.broadcasted_iota(jnp.int32, (32, LANES), 1)
    parts = [folded[at // 3, at % 3] for at in range(9)]
    for tap_y in range(3):
        parts[tap_y] += fold(sums[0, tap_y])
        parts[6 + tap_y] += fold(sums[1, tap_y])
    row = jnp.sum(bias_terms[...], axis=0, keepdims=True)
    row = row + pltpu.roll(row, 64, 1)
    row = row + pltpu.roll(row, 32, 1)
    first = lax.broadcasted_iota(jnp.int32, (32, LANES), 0) == 0
    for place in range(7):
        if place < 6:
            extra = pltpu.roll(parts[7 + place // 3], 96 - 32 * (place % 3), 1)
        else:
            extra = jnp.where(first, jnp.broadcast_to(row, (32, LANES)), 0.0)
        packed[place * 32 : place * 32 + 32, :] = jnp.where(lane < 96, parts[place], extra)
    upper = flag[...] > 0.5
    keep[...] = jnp.where(upper, packed[HALF : 2 * HALF], packed[:HALF])
    send[...] = jnp.where(upper, packed[:HALF], packed[HALF : 2 * HALF])


def inner_sum(taps, weights, chunk, groups):
    total = None
    for plane in range(2):
        for tap_y in range(3):
            lhs = taps[plane, pl.ds(chunk * WIDE_CHUNK + tap_y, WIDE_CHUNK)].reshape(WIDE_CHUNK * groups, 256)
            matrix = jnp.concatenate([weights[plane + 1, tap_y], weights[plane, tap_y]], axis=1)
            term = jnp.dot(lhs, matrix, preferred_element_type=F32)
            total = term if total is None else total + term
    return total


def outer_body(first, rest, weights, partial, line, *more):
    output, grad_input, taps, scratch, grad = more[-5:]
    rows, groups = partial.shape[2:4]
    act, edge = first.at[:rows], rest.at[rest.shape[0] - 4 :]
    gather_grad(first, rest, grad)
    for kind, (source, out, turn) in enumerate(((act, output, rectified), (grad, grad_input, kept))):
        fill_plane(taps, kind, source, edge[kind], edge[2 + kind])
        for chunk in range(rows // CHUNK):
            start = chunk * CHUNK
            total = partial[kind, 0, start : start + CHUNK].reshape(CHUNK * groups, LANES)
            for tap_y in range(3):
                at = start + tap_y
                lhs = taps[kind, at : at + CHUNK].reshape(CHUNK * groups, 256)
                total = total + jnp.dot(lhs, weights[kind, 0, tap_y], preferred_element_type=F32)
            put_rows(scratch, turn(total, line), chunk, groups)
        lay_out(scratch, out, 0, rows, groups)


def rectified(total, line):
    return jnp.maximum(total + line[...], 0.0)


def kept(total, line):
    return total


def lay_out(scratch, out, plane, rows, groups):
    pitch = groups + PITCH
    for group in range(groups):
        halves = [scratch[pl.ds(half * 8 * pitch + group, 8, stride=pitch), :] for half in range(2)]
        block = jnp.concatenate(halves, axis=0).astype(BF16)
        out[plane, :, group * LANES : (group + 1) * LANES] = block


def put_rows(scratch, total, chunk, groups):
    for row in range(CHUNK):
        at = (chunk * CHUNK + row) * (groups + PITCH)
        scratch[at : at + groups, :] = total[row * groups : (row + 1) * groups]


HALF = 112
PITCH = 8


def unpack_body(scaling, part, other, flag, grad_kernel, grad_bias, packed):
    upper = flag[...] > 0.5
    packed[:HALF] = jnp.where(upper, other[...], part[...])
    packed[HALF : 2 * HALF] = jnp.where(upper, part[...], other[...])
    for place in range(7):
        block = packed[place * 32 : place * 32 + 32, :] * scaling
        turned = block.T
        grad_kernel[place * 96 : place * 96 + 96, :] = turned[:96]
        if place < 6:
            grad_kernel[(21 + place) * 32 : (22 + place) * 32, :] = turned[96:]
        else:
            grad_bias[...] = pltpu.roll(block, 32, 1)[:1, :32]


def shifted(value, axis, step):
    count = lax.axis_size(axis)
    pairs = [(i, i + step) for i in range(count) if 0 <= i + step < count]
    return lax.ppermute(value, axis, pairs)


def swapped(value, bit):
    count = lax.axis_size("gz") * lax.axis_size("gy")
    return lax.ppermute(value, ("gz", "gy"), [(i, i ^ bit) for i in range(count)])


def sum_of_four(value, low, high):
    one, two, three = (swapped(value, bit) for bit in (low, high, low + high))
    return (value + one) + (two + three)


def local(activations, grad_out, relu_mask, kernel, bias):
    planes, rows, width = activations.shape
    groups = width // LANES
    block = activations.shape
    shape = jax.ShapeDtypeStruct
    pair = shape((2 * rows, groups, LANES), BF16)
    one_plane = pltpu.VMEM((rows, groups, LANES), BF16)
    lines = shape((4, groups, LANES), BF16)
    spread = pltpu.VMEM((rows * (groups + 8), LANES), F32)
    two_taps = pltpu.VMEM((2, rows + 2, groups, 2 * LANES), BF16)
    half = shape((HALF, LANES), F32)
    packed = pltpu.VMEM((2 * HALF, LANES), F32)
    flag = jnp.full((1, LANES), lax.axis_index("gy") % 2, F32)

    low, high_first, high_rest, firsts, lasts = pl.pallas_call(
        group_body,
        in_specs=[pl.BlockSpec(memory_space=pl.ANY)] * 3,
        out_shape=(
            pair, shape((rows + EARLY, groups, LANES), BF16), shape((rows - EARLY, groups, LANES), BF16), lines, lines,
        ),
        scratch_shapes=[
            spread, pltpu.VMEM(block, BF16), pltpu.VMEM(block, BF16), pltpu.VMEM(block, jnp.int32),
            pltpu.SemaphoreType.DMA((2, 3)),
        ],
        compiler_params=pltpu.CompilerParams(vmem_limit_bytes=56 * MIB),
    )(activations, grad_out, relu_mask)
    from_left = shifted(lasts, "gy", 1)
    from_right = shifted(firsts, "gy", -1)
    below_first = shifted(high_first, "gz", 1)
    below_rest = shifted(jnp.concatenate([high_rest, from_left[2:], from_right[2:]]), "gz", 1)

    line = jnp.tile(bias, 4).reshape(1, LANES)
    flat_kernel = kernel.reshape(27 * 32, 32)
    plane = (rows, groups, LANES)
    folded_shape, bias_shape, weights_shape = (3, 3, 32, LANES), (8, LANES), (3, 3, 256, LANES)
    folded, bias_terms, partial, weights = blocked(
        own_body,
        2,
        (
            shape(folded_shape, F32), shape(bias_shape, F32),
            shape((2, 2, *plane), F32), shape((2, *weights_shape), BF16),
        ),
        (
            part_of(folded_shape, 0, 0, 0, 0), part_of(bias_shape, 0, 0),
            pl.BlockSpec((1, 2, *plane), lambda step: (step, 0, 0, 0, 0)),
            pl.BlockSpec((1, *weights_shape), lambda step: (step, 0, 0, 0, 0)),
        ),
        [pltpu.VMEM((2 * LANES, rows * groups), BF16), two_taps, one_plane],
        (low, high_first, high_rest, from_left, from_right, flat_kernel),
        [part_of(array.shape, 0, 0, 0) for array in (low, high_first, high_rest)] + [part_of(lines.shape, 0, 0, 0)] * 2 + [part_of(flat_kernel.shape, 0, 0)],
    )

    def outer(side, first, rest, done=()):
        return blocked(
            outer_body,
            1,
            (shape(block, BF16), shape(block, BF16)),
            (part_of((1, *block[1:]), side, 0, 0),) * 2,
            [two_taps, spread, one_plane],
            (first, rest, weights, partial, line, *done),
            [
                part_of(first.shape, 0, 0, 0), part_of(rest.shape, 0, 0, 0),
                part_of((2, 1, 3, 256, LANES), 0, 2 * side, 0, 0, 0), part_of((2, 1, *plane), 0, side, 0, 0, 0),
                part_of((1, LANES), 0, 0),
                *[pl.BlockSpec(memory_space=pl.ANY)] * len(done),
            ],
            {5: 0, 6: 1} if done else None,
        )

    split = rows + 4
    ends = (from_left[:2], from_right[:2])
    ends, folded, partial, low_late = lax.optimization_barrier((ends, folded, partial, low))
    above_first = shifted(low_late[:split], "gz", -1)
    down_rest = jnp.concatenate([low_late[split:], *ends])

    part, send = call(
        kernel_grad_body,
        (half, half),
        [packed, two_taps, pltpu.VMEM((2, 3, LANES, 256), F32), one_plane],
        (below_first, below_rest, low, from_left, from_right, folded, bias_terms, flag),
    )
    part = part + swapped(send, 1)
    part = sum_of_four(part, 4, 8)
    part, down_rest, above_first = lax.optimization_barrier((part, down_rest, above_first))
    part = sum_of_four(part, 2, 16)
    above_rest = shifted(down_rest, "gz", -1)
    part = sum_of_four(part, 32, 64)
    results = outer(0, below_first, below_rest)
    part, results, above_rest = lax.optimization_barrier((part, results, above_rest))
    other = swapped(part, 1)
    results = outer(1, above_first, above_rest, results)

    voxels = planes * lax.axis_size("gz") * rows * lax.axis_size("gy") * (width // 32)
    grad_kernel, grad_bias = call(
        functools.partial(unpack_body, 1.0 / math.sqrt(voxels)),
        (shape((27 * 32, 32), F32), shape((1, 32), F32)),
        [packed],
        (part, other, flag),
    )
    return *results, grad_kernel.reshape(3, 3, 3, 32, 32), grad_bias.reshape(32)


def solution(mesh):
    block = P("gz", "gy", None)
    return jax.shard_map(
        local,
        mesh=mesh,
        in_specs=(block, block, block, P(), P()),
        out_specs=(block, block, P(), P()),
        check_vma=False,
    )
```

```python
import functools
import math

import jax
import jax.numpy as jnp
from jax import lax
from jax.experimental import pallas as pl
from jax.experimental.pallas import tpu as pltpu
from jax.sharding import PartitionSpec as P

F32 = jnp.float32
BF16 = jnp.bfloat16
LANES = 128
MIB = 1024 * 1024


def call(body, outs, scratch, args):
    return pl.pallas_call(
        body,
        out_shape=outs,
        scratch_shapes=scratch,
        compiler_params=pltpu.CompilerParams(vmem_limit_bytes=20 * MIB),
    )(*args)


def blocked(body, grid, outs, out_specs, scratch, args, in_specs, aliases=None, flops=0):
    return pl.pallas_call(
        body,
        grid=(grid,),
        out_shape=outs,
        in_specs=in_specs,
        out_specs=out_specs,
        scratch_shapes=scratch,
        input_output_aliases=aliases or {},
        cost_estimate=pl.CostEstimate(flops=flops, bytes_accessed=0, transcendentals=0),
        compiler_params=pltpu.CompilerParams(vmem_limit_bytes=56 * MIB),
    )(*args)


def part_of(shape, *index):
    return pl.BlockSpec(shape, lambda step: index)


def spread_rows(scratch, groups, group, block):
    pitch = groups + 1
    for half in range(2):
        scratch[pl.ds(half * 8 * pitch + group, 8, stride=pitch), :] = block[half * 8 : half * 8 + 8]


def group_body(act_in, grad_in, mask_in, low, high_first, high_rest, firsts, lasts, scratch, act, grad, mask, arrived):
    rows, groups = act.shape[1], low.shape[1]
    copies = [
        [
            pltpu.make_async_copy(source.at[plane], target.at[plane], arrived.at[plane, place])
            for place, (source, target) in enumerate(((act_in, act), (mask_in, mask), (grad_in, grad)))
        ]
        for plane in range(2)
    ]
    for plane in (1, 0):
        for copy in copies[plane]:
            copy.start()
    for plane in (1, 0):
        for kind in range(2):
            out = high_first if plane else low
            for copy in copies[plane][:1] if kind == 0 else copies[plane][1:]:
                copy.wait()
            for group in range(groups):
                span = slice(group * LANES, (group + 1) * LANES)
                if kind == 0:
                    block = act[plane, :, span].astype(F32)
                else:
                    block = grad[plane, :, span].astype(F32) * mask[plane, :, span].astype(F32)
                spread_rows(scratch, groups, group, block)
            for row in range(rows):
                at = row * (groups + 1)
                cells = scratch[at : at + groups, :].astype(BF16)
                if plane and kind and row >= EARLY:
                    high_rest[row - EARLY] = cells
                else:
                    out[kind * rows + row] = cells
                if row == 0:
                    firsts[plane * 2 + kind] = cells
                if row == rows - 1:
                    lasts[plane * 2 + kind] = cells


def with_edges(cells):
    groups = cells.shape[0]
    wide = cells.astype(F32)
    lane = lax.broadcasted_iota(jnp.int32, wide.shape, 1)
    row = lax.broadcasted_iota(jnp.int32, wide.shape, 0)
    before = jnp.where(row == 0, 0.0, pltpu.roll(wide, 1, 0))
    after = jnp.where(row == groups - 1, 0.0, pltpu.roll(wide, groups - 1, 0))
    return jnp.concatenate([cells, jnp.where(lane < 64, after, before).astype(BF16)], axis=1)


def fill_plane(taps, place, source, first, last):
    rows = source.shape[0]
    taps[place, 0] = with_edges(first)
    taps[place, rows + 1] = with_edges(last)

    def step(row, carry):
        taps[place, row + 1] = with_edges(source[row])
        return carry

    lax.fori_loop(0, rows, step, 0, unroll=2)


def build_weights(kernel, flip, out):
    lane = lax.broadcasted_iota(jnp.int32, (32, LANES), 1) // 32
    for tap_z in range(3):
        for tap_y in range(3):
            blocks = []
            for tap_x in range(3):
                at = (tap_z * 3 + tap_y) * 3 + tap_x
                at = 26 - at if flip else at
                block = kernel[at * 32 : at * 32 + 32, :].astype(F32)
                block = block.T if flip else block
                blocks.append(jnp.concatenate([block] * 4, axis=1))
            for place in range(8):
                voxel = place if place < 6 else place - 8
                total = jnp.zeros((32, LANES), F32)
                for tap_x in range(3):
                    total = jnp.where(lane == voxel - tap_x + 1, blocks[tap_x], total)
                out[tap_z, tap_y, place * 32 : place * 32 + 32, :] = total.astype(BF16)


CHUNK = 4
WIDE_CHUNK = 8
EARLY = 8


def fold(term):
    near, far = term[:, :LANES], term[:, LANES:]
    lane = lax.broadcasted_iota(jnp.int32, (32, LANES), 1)
    first = pltpu.roll(jnp.where(lane < 96, near[:32], far[:32]), 32, 1)
    third = pltpu.roll(near[64:96], 96, 1)
    fourth = pltpu.roll(jnp.where(lane < 32, far[96:], near[96:]), 64, 1)
    return (first + near[32:64]) + (third + fourth)


def gather_grad(first, rest, grad):
    rows = grad.shape[0]
    if first.shape == rest.shape:
        grad[...] = first[rows : 2 * rows]
    else:
        grad[:EARLY] = first[rows:]
        grad[EARLY:] = rest[: rows - EARLY]


def own_body(
    low, high_first, high_rest, from_left, from_right, kernel,
    folded, bias_terms, partial, weights, turned, taps, high_grad,
):
    rows, groups = low.shape[0] // 2, low.shape[1]
    step = pl.program_id(0)

    def fill(kind):
        for plane, source in enumerate((low.at[kind * rows : kind * rows + rows], (high_first.at[:rows], high_grad)[kind])):
            at = 2 * plane + kind
            fill_plane(taps, plane, source, from_left[at], from_right[at])
        build_weights(kernel, kind == 1, weights.at[0])

    @pl.when(step == 0)
    def _():
        gather_grad(high_first, high_rest, high_grad)
        sums = jnp.zeros((8, LANES), F32)
        for plane, source in enumerate((low.at[rows:], high_grad)):
            flat = source[...].reshape(rows * groups, LANES)
            turned[plane * LANES : (plane + 1) * LANES, :] = flat.T
            sums = sums + jnp.sum(flat.astype(F32).reshape(-1, 8, LANES), axis=0)
        bias_terms[...] = sums
        fill(0)
        for tap_y in range(3):
            both = []
            for plane in range(2):
                rhs = taps[plane, tap_y : tap_y + rows].reshape(rows * groups, 256)
                both.append(jnp.dot(turned[...], rhs, preferred_element_type=F32))
            folded[1, tap_y] = fold(both[0][:LANES] + both[1][LANES:])
            folded[0, tap_y] = fold(both[0][LANES:])
            folded[2, tap_y] = fold(both[1][:LANES])

    @pl.when(step == 1)
    def _():
        fill(1)

    def add(chunk, carry):
        total = inner_sum(taps, weights.at[0], chunk, groups)
        for plane in range(2):
            part = total[:, plane * LANES : (plane + 1) * LANES]
            partial[0, plane, pl.ds(chunk * WIDE_CHUNK, WIDE_CHUNK)] = part.reshape(WIDE_CHUNK, groups, LANES)
        return carry

    lax.fori_loop(0, rows // WIDE_CHUNK, add, 0)


def kernel_grad_body(
    below_first, below_rest, low, from_left, from_right, folded, bias_terms, flag,
    keep, send, packed, taps, sums, below_grad,
):
    rows, groups = low.shape[0] // 2, low.shape[1]
    blank = jnp.zeros((groups, LANES), BF16)
    gather_grad(below_first, below_rest, below_grad)
    fill_plane(taps, 0, below_first.at[:rows], blank, blank)
    fill_plane(taps, 1, low.at[:rows], from_left[0], from_right[0])
    below_turned = below_grad[...].reshape(rows * groups, LANES).T
    low_turned = low[rows:].reshape(rows * groups, LANES).T
    for tap_y in range(3):
        rhs = taps[0, tap_y : tap_y + rows].reshape(rows * groups, 256)
        sums[0, tap_y] = jnp.dot(low_turned, rhs, preferred_element_type=F32)
        rhs = taps[1, tap_y : tap_y + rows].reshape(rows * groups, 256)
        sums[1, tap_y] = jnp.dot(below_turned, rhs, preferred_element_type=F32)
    sums[0, 2] += jnp.dot(from_left[1].T, taps[0, 1], preferred_element_type=F32)
    sums[0, 0] += jnp.dot(from_right[1].T, taps[0, rows], preferred_element_type=F32)
    lane = lax.broadcasted_iota(jnp.int32, (32, LANES), 1)
    parts = [folded[at // 3, at % 3] for at in range(9)]
    for tap_y in range(3):
        parts[tap_y] += fold(sums[0, tap_y])
        parts[6 + tap_y] += fold(sums[1, tap_y])
    row = jnp.sum(bias_terms[...], axis=0, keepdims=True)
    row = row + pltpu.roll(row, 64, 1)
    row = row + pltpu.roll(row, 32, 1)
    first = lax.broadcasted_iota(jnp.int32, (32, LANES), 0) == 0
    for place in range(7):
        if place < 6:
            extra = pltpu.roll(parts[7 + place // 3], 96 - 32 * (place % 3), 1)
        else:
            extra = jnp.where(first, jnp.broadcast_to(row, (32, LANES)), 0.0)
        packed[place * 32 : place * 32 + 32, :] = jnp.where(lane < 96, parts[place], extra)
    upper = flag[...] > 0.5
    keep[...] = jnp.where(upper, packed[HALF : 2 * HALF], packed[:HALF])
    send[...] = jnp.where(upper, packed[:HALF], packed[HALF : 2 * HALF])


def inner_sum(taps, weights, chunk, groups):
    total = None
    for plane in range(2):
        for tap_y in range(3):
            lhs = taps[plane, pl.ds(chunk * WIDE_CHUNK + tap_y, WIDE_CHUNK)].reshape(WIDE_CHUNK * groups, 256)
            matrix = jnp.concatenate([weights[plane + 1, tap_y], weights[plane, tap_y]], axis=1)
            term = jnp.dot(lhs, matrix, preferred_element_type=F32)
            total = term if total is None else total + term
    return total


def outer_body(count, *refs):
    first, rest = refs[0], refs[count - 1]
    weights, partial, line = refs[count : count + 3]
    output, grad_input, taps, scratch, grad = refs[-5:]
    rows, groups = partial.shape[2:4]
    act, edge = first.at[:rows], rest.at[rest.shape[0] - 4 :]
    gather_grad(first, rest, grad)
    for kind, (source, out, turn) in enumerate(((act, output, rectified), (grad, grad_input, kept))):
        fill_plane(taps, kind, source, edge[kind], edge[2 + kind])
        for chunk in range(rows // CHUNK):
            start = chunk * CHUNK
            total = partial[kind, 0, start : start + CHUNK].reshape(CHUNK * groups, LANES)
            for tap_y in range(3):
                at = start + tap_y
                lhs = taps[kind, at : at + CHUNK].reshape(CHUNK * groups, 256)
                total = total + jnp.dot(lhs, weights[kind, 0, tap_y], preferred_element_type=F32)
            put_rows(scratch, turn(total, line), chunk, groups)
        lay_out(scratch, out, 0, rows, groups)


def rectified(total, line):
    return jnp.maximum(total + line[...], 0.0)


def kept(total, line):
    return total


def lay_out(scratch, out, plane, rows, groups):
    pitch = groups + PITCH
    for group in range(groups):
        halves = [scratch[pl.ds(half * 8 * pitch + group, 8, stride=pitch), :] for half in range(2)]
        block = jnp.concatenate(halves, axis=0).astype(BF16)
        out[plane, :, group * LANES : (group + 1) * LANES] = block


def put_rows(scratch, total, chunk, groups):
    for row in range(CHUNK):
        at = (chunk * CHUNK + row) * (groups + PITCH)
        scratch[at : at + groups, :] = total[row * groups : (row + 1) * groups]


HALF = 112
PITCH = 8


def join_body(part, other, flag, packed):
    upper = flag[...] > 0.5
    packed[:HALF] = jnp.where(upper, other[...], part[...])
    packed[HALF : 2 * HALF] = jnp.where(upper, part[...], other[...])


def unpack_body(scaling, part, one, two, three, grad_kernel, grad_bias):
    for place in range(7):
        span = slice(place * 32, place * 32 + 32)
        block = ((part[span, :] + one[span, :]) + (two[span, :] + three[span, :])) * scaling
        turned = block.T
        grad_kernel[place * 96 : place * 96 + 96, :] = turned[:96]
        if place < 6:
            grad_kernel[(21 + place) * 32 : (22 + place) * 32, :] = turned[96:]
        else:
            grad_bias[...] = pltpu.roll(block, 32, 1)[:1, :32]


def shifted(value, axis, step):
    count = lax.axis_size(axis)
    pairs = [(i, i + step) for i in range(count) if 0 <= i + step < count]
    return lax.ppermute(value, axis, pairs)


def swapped(value, bit):
    count = lax.axis_size("gz") * lax.axis_size("gy")
    return lax.ppermute(value, ("gz", "gy"), [(i, i ^ bit) for i in range(count)])


def sum_of_four(value, low, high):
    one, two, three = (swapped(value, bit) for bit in (low, high, low + high))
    return (value + one) + (two + three)


def local(activations, grad_out, relu_mask, kernel, bias):
    planes, rows, width = activations.shape
    groups = width // LANES
    block = activations.shape
    shape = jax.ShapeDtypeStruct
    pair = shape((2 * rows, groups, LANES), BF16)
    one_plane = pltpu.VMEM((rows, groups, LANES), BF16)
    lines = shape((4, groups, LANES), BF16)
    spread = pltpu.VMEM((rows * (groups + 8), LANES), F32)
    two_taps = pltpu.VMEM((2, rows + 2, groups, 2 * LANES), BF16)
    half = shape((HALF, LANES), F32)
    packed = pltpu.VMEM((2 * HALF, LANES), F32)
    flag = jnp.full((1, LANES), lax.axis_index("gy") % 2, F32)

    low, high_first, high_rest, firsts, lasts = pl.pallas_call(
        group_body,
        in_specs=[pl.BlockSpec(memory_space=pl.ANY)] * 3,
        out_shape=(
            pair, shape((rows + EARLY, groups, LANES), BF16), shape((rows - EARLY, groups, LANES), BF16), lines, lines,
        ),
        scratch_shapes=[
            spread, pltpu.VMEM(block, BF16), pltpu.VMEM(block, BF16), pltpu.VMEM(block, jnp.int32),
            pltpu.SemaphoreType.DMA((2, 3)),
        ],
        compiler_params=pltpu.CompilerParams(vmem_limit_bytes=56 * MIB),
    )(activations, grad_out, relu_mask)
    from_left = shifted(lasts, "gy", 1)
    from_right = shifted(firsts, "gy", -1)
    below_first = shifted(high_first, "gz", 1)
    below_rest = shifted(jnp.concatenate([high_rest, from_left[2:], from_right[2:]]), "gz", 1)

    line = jnp.tile(bias, 4).reshape(1, LANES)
    flat_kernel = kernel.reshape(27 * 32, 32)
    plane = (rows, groups, LANES)
    folded_shape, bias_shape, weights_shape = (3, 3, 32, LANES), (8, LANES), (3, 3, 256, LANES)
    folded, bias_terms, partial, weights = blocked(
        own_body,
        2,
        (
            shape(folded_shape, F32), shape(bias_shape, F32),
            shape((2, 2, *plane), F32), shape((2, *weights_shape), BF16),
        ),
        (
            part_of(folded_shape, 0, 0, 0, 0), part_of(bias_shape, 0, 0),
            pl.BlockSpec((1, 2, *plane), lambda step: (step, 0, 0, 0, 0)),
            pl.BlockSpec((1, *weights_shape), lambda step: (step, 0, 0, 0, 0)),
        ),
        [pltpu.VMEM((2 * LANES, rows * groups), BF16), two_taps, one_plane],
        (low, high_first, high_rest, from_left, from_right, flat_kernel),
        [part_of(array.shape, 0, 0, 0) for array in (low, high_first, high_rest)] + [part_of(lines.shape, 0, 0, 0)] * 2 + [part_of(flat_kernel.shape, 0, 0)],
    )

    def outer(side, planes_beside, done=()):
        count = len(planes_beside)
        return blocked(
            functools.partial(outer_body, count),
            1,
            (shape(block, BF16), shape(block, BF16)),
            (part_of((1, *block[1:]), side, 0, 0),) * 2,
            [two_taps, spread, one_plane],
            (*planes_beside, weights, partial, line, *done),
            [
                *[part_of(array.shape, 0, 0, 0) for array in planes_beside],
                part_of((2, 1, 3, 256, LANES), 0, 2 * side, 0, 0, 0), part_of((2, 1, *plane), 0, side, 0, 0, 0),
                part_of((1, LANES), 0, 0),
                *[pl.BlockSpec(memory_space=pl.ANY)] * len(done),
            ],
            {count + 3: 0, count + 4: 1} if done else None,
        )

    ends = (from_left[:2], from_right[:2])
    ends, folded, partial = lax.optimization_barrier((ends, folded, partial))
    down = jnp.concatenate([low, *ends])
    down, below_rest = lax.optimization_barrier((down, below_rest))
    above = shifted(down, "gz", -1)

    part, send = call(
        kernel_grad_body,
        (half, half),
        [packed, two_taps, pltpu.VMEM((2, 3, LANES, 256), F32), one_plane],
        (below_first, below_rest, low, from_left, from_right, folded, bias_terms, flag),
    )
    part = part + swapped(send, 1)
    part = sum_of_four(part, 4, 8)
    part = sum_of_four(part, 32, 64)
    results = outer(0, (below_first, below_rest))
    part, results = lax.optimization_barrier((part, results))
    part = call(join_body, shape((2 * HALF, LANES), F32), [], (part, swapped(part, 1), flag))
    part, above = lax.optimization_barrier((part, above))
    others = [swapped(part, bit) for bit in (2, 16, 18)]
    results = outer(1, (above,), results)

    voxels = planes * lax.axis_size("gz") * rows * lax.axis_size("gy") * (width // 32)
    grad_kernel, grad_bias = call(
        functools.partial(unpack_body, 1.0 / math.sqrt(voxels)),
        (shape((27 * 32, 32), F32), shape((1, 32), F32)),
        [],
        (part, *others),
    )
    return *results, grad_kernel.reshape(3, 3, 3, 32, 32), grad_bias.reshape(32)


def solution(mesh):
    block = P("gz", "gy", None)
    return jax.shard_map(
        local,
        mesh=mesh,
        in_specs=(block, block, block, P(), P()),
        out_specs=(block, block, P(), P()),
        check_vma=False,
    )
```

```python
import functools
import math

import jax
import jax.numpy as jnp
from jax import lax
from jax.experimental import pallas as pl
from jax.experimental.pallas import tpu as pltpu
from jax.sharding import PartitionSpec as P

F32 = jnp.float32
BF16 = jnp.bfloat16
LANES = 128
MIB = 1024 * 1024


def call(body, outs, scratch, args):
    return pl.pallas_call(
        body,
        out_shape=outs,
        scratch_shapes=scratch,
        compiler_params=pltpu.CompilerParams(vmem_limit_bytes=20 * MIB),
    )(*args)


def blocked(body, grid, outs, out_specs, scratch, args, in_specs, aliases=None, flops=0):
    return pl.pallas_call(
        body,
        grid=(grid,),
        out_shape=outs,
        in_specs=in_specs,
        out_specs=out_specs,
        scratch_shapes=scratch,
        input_output_aliases=aliases or {},
        cost_estimate=pl.CostEstimate(flops=flops, bytes_accessed=0, transcendentals=0),
        compiler_params=pltpu.CompilerParams(vmem_limit_bytes=20 * MIB),
    )(*args)


def part_of(shape, *index):
    return pl.BlockSpec(shape, lambda step: index)


def spread_rows(scratch, groups, group, block):
    pitch = groups + 1
    for half in range(2):
        scratch[pl.ds(half * 8 * pitch + group, 8, stride=pitch), :] = block[half * 8 : half * 8 + 8]


def group_body(act_in, grad_in, mask_in, low, high_first, high_rest, firsts, lasts, scratch, act, grad, mask, arrived):
    rows, groups = act.shape[1], low.shape[1]
    copies = [
        [
            pltpu.make_async_copy(source.at[plane], target.at[plane], arrived.at[plane, place])
            for place, (source, target) in enumerate(((act_in, act), (mask_in, mask), (grad_in, grad)))
        ]
        for plane in range(2)
    ]
    for plane in (1, 0):
        for copy in copies[plane]:
            copy.start()
    for plane in (1, 0):
        for kind in range(2):
            out = high_first if plane else low
            for copy in copies[plane][:1] if kind == 0 else copies[plane][1:]:
                copy.wait()
            for group in range(groups):
                span = slice(group * LANES, (group + 1) * LANES)
                if kind == 0:
                    block = act[plane, :, span].astype(F32)
                else:
                    block = grad[plane, :, span].astype(F32) * mask[plane, :, span].astype(F32)
                spread_rows(scratch, groups, group, block)
            for row in range(rows):
                at = row * (groups + 1)
                cells = scratch[at : at + groups, :].astype(BF16)
                if plane and kind and row >= EARLY:
                    high_rest[row - EARLY] = cells
                else:
                    out[kind * rows + row] = cells
                if row == 0:
                    firsts[plane * 2 + kind] = cells
                if row == rows - 1:
                    lasts[plane * 2 + kind] = cells


def with_edges(cells):
    groups = cells.shape[0]
    wide = cells.astype(F32)
    lane = lax.broadcasted_iota(jnp.int32, wide.shape, 1)
    row = lax.broadcasted_iota(jnp.int32, wide.shape, 0)
    before = jnp.where(row == 0, 0.0, pltpu.roll(wide, 1, 0))
    after = jnp.where(row == groups - 1, 0.0, pltpu.roll(wide, groups - 1, 0))
    return jnp.concatenate([cells, jnp.where(lane < 64, after, before).astype(BF16)], axis=1)


def fill_plane(taps, place, source, first, last):
    rows = source.shape[0]
    taps[place, 0] = with_edges(first)
    taps[place, rows + 1] = with_edges(last)

    def step(row, carry):
        taps[place, row + 1] = with_edges(source[row])
        return carry

    lax.fori_loop(0, rows, step, 0, unroll=2)


def build_weights(kernel, flip, out):
    lane = lax.broadcasted_iota(jnp.int32, (32, LANES), 1) // 32
    for tap_z in range(3):
        for tap_y in range(3):
            blocks = []
            for tap_x in range(3):
                at = (tap_z * 3 + tap_y) * 3 + tap_x
                at = 26 - at if flip else at
                block = kernel[at * 32 : at * 32 + 32, :].astype(F32)
                block = block.T if flip else block
                blocks.append(jnp.concatenate([block] * 4, axis=1))
            for place in range(8):
                voxel = place if place < 6 else place - 8
                total = jnp.zeros((32, LANES), F32)
                for tap_x in range(3):
                    total = jnp.where(lane == voxel - tap_x + 1, blocks[tap_x], total)
                out[tap_z, tap_y, place * 32 : place * 32 + 32, :] = total.astype(BF16)


CHUNK = 4
WIDE_CHUNK = 8
EARLY = 8


def fold(term):
    near, far = term[:, :LANES], term[:, LANES:]
    lane = lax.broadcasted_iota(jnp.int32, (32, LANES), 1)
    first = pltpu.roll(jnp.where(lane < 96, near[:32], far[:32]), 32, 1)
    third = pltpu.roll(near[64:96], 96, 1)
    fourth = pltpu.roll(jnp.where(lane < 32, far[96:], near[96:]), 64, 1)
    return (first + near[32:64]) + (third + fourth)


def gather_grad(first, rest, grad):
    rows = grad.shape[0]
    if first.shape == rest.shape:
        grad[...] = first[rows : 2 * rows]
    else:
        grad[:EARLY] = first[rows:]
        grad[EARLY:] = rest[: rows - EARLY]


def own_body(
    low, high_first, high_rest, from_left, from_right, kernel,
    folded, bias_terms, partial, weights, turned, taps, high_grad,
):
    rows, groups = low.shape[0] // 2, low.shape[1]
    step = pl.program_id(0)

    def fill(kind):
        for plane, source in enumerate((low.at[kind * rows : kind * rows + rows], (high_first.at[:rows], high_grad)[kind])):
            at = 2 * plane + kind
            fill_plane(taps, plane, source, from_left[at], from_right[at])
        build_weights(kernel, kind == 1, weights.at[0])

    @pl.when(step == 0)
    def _():
        gather_grad(high_first, high_rest, high_grad)
        sums = jnp.zeros((8, LANES), F32)
        for plane, source in enumerate((low.at[rows:], high_grad)):
            flat = source[...].reshape(rows * groups, LANES)
            turned[plane * LANES : (plane + 1) * LANES, :] = flat.T
            sums = sums + jnp.sum(flat.astype(F32).reshape(-1, 8, LANES), axis=0)
        bias_terms[...] = sums
        fill(0)
        for tap_y in range(3):
            both = []
            for plane in range(2):
                rhs = taps[plane, tap_y : tap_y + rows].reshape(rows * groups, 256)
                both.append(jnp.dot(turned[...], rhs, preferred_element_type=F32))
            folded[1, tap_y] = fold(both[0][:LANES] + both[1][LANES:])
            folded[0, tap_y] = fold(both[0][LANES:])
            folded[2, tap_y] = fold(both[1][:LANES])

    @pl.when(step == 1)
    def _():
        fill(1)

    def add(chunk, carry):
        total = inner_sum(taps, weights.at[0], chunk, groups)
        for plane in range(2):
            part = total[:, plane * LANES : (plane + 1) * LANES]
            partial[0, plane, pl.ds(chunk * WIDE_CHUNK, WIDE_CHUNK)] = part.reshape(WIDE_CHUNK, groups, LANES)
        return carry

    lax.fori_loop(0, rows // WIDE_CHUNK, add, 0)


def kernel_grad_body(
    below_first, below_rest, low, from_left, from_right, folded, bias_terms, flag,
    keep, send, packed, taps, sums, below_grad,
):
    rows, groups = low.shape[0] // 2, low.shape[1]
    blank = jnp.zeros((groups, LANES), BF16)
    gather_grad(below_first, below_rest, below_grad)
    fill_plane(taps, 0, below_first.at[:rows], blank, blank)
    fill_plane(taps, 1, low.at[:rows], from_left[0], from_right[0])
    below_turned = below_grad[...].reshape(rows * groups, LANES).T
    low_turned = low[rows:].reshape(rows * groups, LANES).T
    for tap_y in range(3):
        rhs = taps[0, tap_y : tap_y + rows].reshape(rows * groups, 256)
        sums[0, tap_y] = jnp.dot(low_turned, rhs, preferred_element_type=F32)
        rhs = taps[1, tap_y : tap_y + rows].reshape(rows * groups, 256)
        sums[1, tap_y] = jnp.dot(below_turned, rhs, preferred_element_type=F32)
    sums[0, 2] += jnp.dot(from_left[1].T, taps[0, 1], preferred_element_type=F32)
    sums[0, 0] += jnp.dot(from_right[1].T, taps[0, rows], preferred_element_type=F32)
    lane = lax.broadcasted_iota(jnp.int32, (32, LANES), 1)
    parts = [folded[at // 3, at % 3] for at in range(9)]
    for tap_y in range(3):
        parts[tap_y] += fold(sums[0, tap_y])
        parts[6 + tap_y] += fold(sums[1, tap_y])
    row = jnp.sum(bias_terms[...], axis=0, keepdims=True)
    row = row + pltpu.roll(row, 64, 1)
    row = row + pltpu.roll(row, 32, 1)
    first = lax.broadcasted_iota(jnp.int32, (32, LANES), 0) == 0
    for place in range(7):
        if place < 6:
            extra = pltpu.roll(parts[7 + place // 3], 96 - 32 * (place % 3), 1)
        else:
            extra = jnp.where(first, jnp.broadcast_to(row, (32, LANES)), 0.0)
        packed[place * 32 : place * 32 + 32, :] = jnp.where(lane < 96, parts[place], extra)
    upper = flag[...] > 0.5
    keep[...] = jnp.where(upper, packed[HALF : 2 * HALF], packed[:HALF])
    send[...] = jnp.where(upper, packed[:HALF], packed[HALF : 2 * HALF])


def inner_sum(taps, weights, chunk, groups):
    total = None
    for plane in range(2):
        for tap_y in range(3):
            lhs = taps[plane, pl.ds(chunk * WIDE_CHUNK + tap_y, WIDE_CHUNK)].reshape(WIDE_CHUNK * groups, 256)
            matrix = jnp.concatenate([weights[plane + 1, tap_y], weights[plane, tap_y]], axis=1)
            term = jnp.dot(lhs, matrix, preferred_element_type=F32)
            total = term if total is None else total + term
    return total


def outer_body(count, *refs):
    first, rest = refs[0], refs[count - 1]
    weights, partial, line = refs[count : count + 3]
    output, grad_input, taps, scratch, grad = refs[-5:]
    rows, groups = partial.shape[2:4]
    act, edge = first.at[:rows], rest.at[rest.shape[0] - 4 :]
    gather_grad(first, rest, grad)
    for kind, (source, out, turn) in enumerate(((act, output, rectified), (grad, grad_input, kept))):
        fill_plane(taps, kind, source, edge[kind], edge[2 + kind])
        for chunk in range(rows // CHUNK):
            start = chunk * CHUNK
            total = partial[kind, 0, start : start + CHUNK].reshape(CHUNK * groups, LANES)
            for tap_y in range(3):
                at = start + tap_y
                lhs = taps[kind, at : at + CHUNK].reshape(CHUNK * groups, 256)
                total = total + jnp.dot(lhs, weights[kind, 0, tap_y], preferred_element_type=F32)
            put_rows(scratch, turn(total, line), chunk, groups)
        lay_out(scratch, out, 0, rows, groups)


def rectified(total, line):
    return jnp.maximum(total + line[...], 0.0)


def kept(total, line):
    return total


def lay_out(scratch, out, plane, rows, groups):
    pitch = groups + PITCH
    for group in range(groups):
        halves = [scratch[pl.ds(half * 8 * pitch + group, 8, stride=pitch), :] for half in range(2)]
        block = jnp.concatenate(halves, axis=0).astype(BF16)
        out[plane, :, group * LANES : (group + 1) * LANES] = block


def put_rows(scratch, total, chunk, groups):
    for row in range(CHUNK):
        at = (chunk * CHUNK + row) * (groups + PITCH)
        scratch[at : at + groups, :] = total[row * groups : (row + 1) * groups]


HALF = 112
PITCH = 8


def join_body(part, other, flag, packed):
    upper = flag[...] > 0.5
    packed[:HALF] = jnp.where(upper, other[...], part[...])
    packed[HALF : 2 * HALF] = jnp.where(upper, part[...], other[...])


def unpack_body(scaling, part, one, two, three, grad_kernel, grad_bias):
    for place in range(7):
        span = slice(place * 32, place * 32 + 32)
        block = ((part[span, :] + one[span, :]) + (two[span, :] + three[span, :])) * scaling
        turned = block.T
        grad_kernel[place * 96 : place * 96 + 96, :] = turned[:96]
        if place < 6:
            grad_kernel[(21 + place) * 32 : (22 + place) * 32, :] = turned[96:]
        else:
            grad_bias[...] = pltpu.roll(block, 32, 1)[:1, :32]


def shifted(value, axis, step):
    count = lax.axis_size(axis)
    pairs = [(i, i + step) for i in range(count) if 0 <= i + step < count]
    return lax.ppermute(value, axis, pairs)


def swapped(value, bit):
    count = lax.axis_size("gz") * lax.axis_size("gy")
    return lax.ppermute(value, ("gz", "gy"), [(i, i ^ bit) for i in range(count)])


def sum_of_four(value, low, high):
    one, two, three = (swapped(value, bit) for bit in (low, high, low + high))
    return (value + one) + (two + three)


def local(activations, grad_out, relu_mask, kernel, bias):
    planes, rows, width = activations.shape
    groups = width // LANES
    block = activations.shape
    shape = jax.ShapeDtypeStruct
    pair = shape((2 * rows, groups, LANES), BF16)
    one_plane = pltpu.VMEM((rows, groups, LANES), BF16)
    lines = shape((4, groups, LANES), BF16)
    spread = pltpu.VMEM((rows * (groups + 8), LANES), F32)
    two_taps = pltpu.VMEM((2, rows + 2, groups, 2 * LANES), BF16)
    half = shape((HALF, LANES), F32)
    packed = pltpu.VMEM((2 * HALF, LANES), F32)
    flag = jnp.full((1, LANES), lax.axis_index("gy") % 2, F32)

    low, high_first, high_rest, firsts, lasts = pl.pallas_call(
        group_body,
        in_specs=[pl.BlockSpec(memory_space=pl.ANY)] * 3,
        out_shape=(
            pair, shape((rows + EARLY, groups, LANES), BF16), shape((rows - EARLY, groups, LANES), BF16), lines, lines,
        ),
        scratch_shapes=[
            spread, pltpu.VMEM(block, BF16), pltpu.VMEM(block, BF16), pltpu.VMEM(block, jnp.int32),
            pltpu.SemaphoreType.DMA((2, 3)),
        ],
        compiler_params=pltpu.CompilerParams(vmem_limit_bytes=56 * MIB),
    )(activations, grad_out, relu_mask)
    from_left = shifted(lasts, "gy", 1)
    from_right = shifted(firsts, "gy", -1)
    below_first = shifted(high_first, "gz", 1)
    below_rest = shifted(jnp.concatenate([high_rest, from_left[2:], from_right[2:]]), "gz", 1)

    line = jnp.tile(bias, 4).reshape(1, LANES)
    flat_kernel = kernel.reshape(27 * 32, 32)
    plane = (rows, groups, LANES)
    folded_shape, bias_shape, weights_shape = (3, 3, 32, LANES), (8, LANES), (3, 3, 256, LANES)
    folded, bias_terms, partial, weights = blocked(
        own_body,
        2,
        (
            shape(folded_shape, F32), shape(bias_shape, F32),
            shape((2, 2, *plane), F32), shape((2, *weights_shape), BF16),
        ),
        (
            part_of(folded_shape, 0, 0, 0, 0), part_of(bias_shape, 0, 0),
            pl.BlockSpec((1, 2, *plane), lambda step: (step, 0, 0, 0, 0)),
            pl.BlockSpec((1, *weights_shape), lambda step: (step, 0, 0, 0, 0)),
        ),
        [pltpu.VMEM((2 * LANES, rows * groups), BF16), two_taps, one_plane],
        (low, high_first, high_rest, from_left, from_right, flat_kernel),
        [part_of(array.shape, 0, 0, 0) for array in (low, high_first, high_rest)] + [part_of(lines.shape, 0, 0, 0)] * 2 + [part_of(flat_kernel.shape, 0, 0)],
    )

    def outer(side, planes_beside, done=()):
        count = len(planes_beside)
        return blocked(
            functools.partial(outer_body, count),
            1,
            (shape(block, BF16), shape(block, BF16)),
            (part_of((1, *block[1:]), side, 0, 0),) * 2,
            [two_taps, spread, one_plane],
            (*planes_beside, weights, partial, line, *done),
            [
                *[part_of(array.shape, 0, 0, 0) for array in planes_beside],
                part_of((2, 1, 3, 256, LANES), 0, 2 * side, 0, 0, 0), part_of((2, 1, *plane), 0, side, 0, 0, 0),
                part_of((1, LANES), 0, 0),
                *[pl.BlockSpec(memory_space=pl.ANY)] * len(done),
            ],
            {count + 3: 0, count + 4: 1} if done else None,
        )

    ends = (from_left[:2], from_right[:2])
    ends, folded, partial = lax.optimization_barrier((ends, folded, partial))
    down = jnp.concatenate([low, *ends])
    above = shifted(down, "gz", -1)

    part, send = call(
        kernel_grad_body,
        (half, half),
        [packed, two_taps, pltpu.VMEM((2, 3, LANES, 256), F32), one_plane],
        (below_first, below_rest, low, from_left, from_right, folded, bias_terms, flag),
    )
    part = part + swapped(send, 1)
    part = sum_of_four(part, 4, 8)
    part = sum_of_four(part, 32, 64)
    results = outer(0, (below_first, below_rest))
    part, results = lax.optimization_barrier((part, results))
    part = call(join_body, shape((2 * HALF, LANES), F32), [], (part, swapped(part, 1), flag))
    part, above = lax.optimization_barrier((part, above))
    others = [swapped(part, bit) for bit in (2, 16, 18)]
    results = outer(1, (above,), results)

    voxels = planes * lax.axis_size("gz") * rows * lax.axis_size("gy") * (width // 32)
    grad_kernel, grad_bias = call(
        functools.partial(unpack_body, 1.0 / math.sqrt(voxels)),
        (shape((27 * 32, 32), F32), shape((1, 32), F32)),
        [],
        (part, *others),
    )
    return *results, grad_kernel.reshape(3, 3, 3, 32, 32), grad_bias.reshape(32)


def solution(mesh):
    block = P("gz", "gy", None)
    return jax.shard_map(
        local,
        mesh=mesh,
        in_specs=(block, block, block, P(), P()),
        out_specs=(block, block, P(), P()),
        check_vma=False,
    )
```

```python
import functools
import math

import jax
import jax.numpy as jnp
from jax import lax
from jax.experimental import pallas as pl
from jax.experimental.pallas import tpu as pltpu
from jax.sharding import PartitionSpec as P

F32 = jnp.float32
BF16 = jnp.bfloat16
LANES = 128
MIB = 1024 * 1024


def call(body, outs, scratch, args):
    return pl.pallas_call(
        body,
        out_shape=outs,
        scratch_shapes=scratch,
        compiler_params=pltpu.CompilerParams(vmem_limit_bytes=20 * MIB),
    )(*args)


def blocked(body, grid, outs, out_specs, scratch, args, in_specs, aliases=None, flops=0):
    return pl.pallas_call(
        body,
        grid=(grid,),
        out_shape=outs,
        in_specs=in_specs,
        out_specs=out_specs,
        scratch_shapes=scratch,
        input_output_aliases=aliases or {},
        cost_estimate=pl.CostEstimate(flops=flops, bytes_accessed=0, transcendentals=0),
        compiler_params=pltpu.CompilerParams(vmem_limit_bytes=56 * MIB),
    )(*args)


def part_of(shape, *index):
    return pl.BlockSpec(shape, lambda step: index)


def spread_rows(scratch, groups, group, block):
    pitch = groups + 1
    for half in range(2):
        scratch[pl.ds(half * 8 * pitch + group, 8, stride=pitch), :] = block[half * 8 : half * 8 + 8]


def group_body(act_in, grad_in, mask_in, low, high_first, high_rest, firsts, lasts, scratch, act, grad, mask, arrived):
    rows, groups = act.shape[1], low.shape[1]
    copies = [
        [
            pltpu.make_async_copy(source.at[plane], target.at[plane], arrived.at[plane, place])
            for place, (source, target) in enumerate(((act_in, act), (mask_in, mask), (grad_in, grad)))
        ]
        for plane in range(2)
    ]
    for plane in (1, 0):
        for copy in copies[plane]:
            copy.start()
    for plane in (1, 0):
        for kind in range(2):
            out = high_first if plane else low
            for copy in copies[plane][:1] if kind == 0 else copies[plane][1:]:
                copy.wait()
            for group in range(groups):
                span = slice(group * LANES, (group + 1) * LANES)
                if kind == 0:
                    block = act[plane, :, span].astype(F32)
                else:
                    block = grad[plane, :, span].astype(F32) * mask[plane, :, span].astype(F32)
                spread_rows(scratch, groups, group, block)
            for row in range(rows):
                at = row * (groups + 1)
                cells = scratch[at : at + groups, :].astype(BF16)
                if plane and kind and row >= EARLY:
                    high_rest[row - EARLY] = cells
                else:
                    out[kind * rows + row] = cells
                if row == 0:
                    firsts[plane * 2 + kind] = cells
                if row == rows - 1:
                    lasts[plane * 2 + kind] = cells


def with_edges(cells):
    groups = cells.shape[0]
    wide = cells.astype(F32)
    lane = lax.broadcasted_iota(jnp.int32, wide.shape, 1)
    row = lax.broadcasted_iota(jnp.int32, wide.shape, 0)
    before = jnp.where(row == 0, 0.0, pltpu.roll(wide, 1, 0))
    after = jnp.where(row == groups - 1, 0.0, pltpu.roll(wide, groups - 1, 0))
    return jnp.concatenate([cells, jnp.where(lane < 64, after, before).astype(BF16)], axis=1)


def fill_plane(taps, place, source, first, last):
    rows = source.shape[0]
    taps[place, 0] = with_edges(first)
    taps[place, rows + 1] = with_edges(last)

    def step(row, carry):
        taps[place, row + 1] = with_edges(source[row])
        return carry

    lax.fori_loop(0, rows, step, 0, unroll=2)


def build_weights(kernel, flip, out):
    lane = lax.broadcasted_iota(jnp.int32, (32, LANES), 1) // 32
    for tap_z in range(3):
        for tap_y in range(3):
            blocks = []
            for tap_x in range(3):
                at = (tap_z * 3 + tap_y) * 3 + tap_x
                at = 26 - at if flip else at
                block = kernel[at * 32 : at * 32 + 32, :].astype(F32)
                block = block.T if flip else block
                blocks.append(jnp.concatenate([block] * 4, axis=1))
            for place in range(8):
                voxel = place if place < 6 else place - 8
                total = jnp.zeros((32, LANES), F32)
                for tap_x in range(3):
                    total = jnp.where(lane == voxel - tap_x + 1, blocks[tap_x], total)
                out[tap_z, tap_y, place * 32 : place * 32 + 32, :] = total.astype(BF16)


CHUNK = 4
WIDE_CHUNK = 8
EARLY = 8


def fold(term):
    near, far = term[:, :LANES], term[:, LANES:]
    lane = lax.broadcasted_iota(jnp.int32, (32, LANES), 1)
    first = pltpu.roll(jnp.where(lane < 96, near[:32], far[:32]), 32, 1)
    third = pltpu.roll(near[64:96], 96, 1)
    fourth = pltpu.roll(jnp.where(lane < 32, far[96:], near[96:]), 64, 1)
    return (first + near[32:64]) + (third + fourth)


def gather_grad(first, rest, grad):
    rows = grad.shape[0]
    if first.shape == rest.shape:
        grad[...] = first[rows : 2 * rows]
    else:
        grad[:EARLY] = first[rows:]
        grad[EARLY:] = rest[: rows - EARLY]


def own_body(
    low, high_first, high_rest, from_left, from_right, kernel,
    folded, bias_terms, partial, weights, turned, taps, high_grad,
):
    rows, groups = low.shape[0] // 2, low.shape[1]
    step = pl.program_id(0)

    def fill(kind):
        for plane, source in enumerate((low.at[kind * rows : kind * rows + rows], (high_first.at[:rows], high_grad)[kind])):
            at = 2 * plane + kind
            fill_plane(taps, plane, source, from_left[at], from_right[at])
        build_weights(kernel, kind == 1, weights.at[0])

    @pl.when(step == 0)
    def _():
        gather_grad(high_first, high_rest, high_grad)
        sums = jnp.zeros((8, LANES), F32)
        for plane, source in enumerate((low.at[rows:], high_grad)):
            flat = source[...].reshape(rows * groups, LANES)
            turned[plane * LANES : (plane + 1) * LANES, :] = flat.T
            sums = sums + jnp.sum(flat.astype(F32).reshape(-1, 8, LANES), axis=0)
        bias_terms[...] = sums
        fill(0)
        for tap_y in range(3):
            both = []
            for plane in range(2):
                rhs = taps[plane, tap_y : tap_y + rows].reshape(rows * groups, 256)
                both.append(jnp.dot(turned[...], rhs, preferred_element_type=F32))
            folded[1, tap_y] = fold(both[0][:LANES] + both[1][LANES:])
            folded[0, tap_y] = fold(both[0][LANES:])
            folded[2, tap_y] = fold(both[1][:LANES])

    @pl.when(step == 1)
    def _():
        fill(1)

    def add(chunk, carry):
        total = inner_sum(taps, weights.at[0], chunk, groups)
        for plane in range(2):
            part = total[:, plane * LANES : (plane + 1) * LANES]
            partial[0, plane, pl.ds(chunk * WIDE_CHUNK, WIDE_CHUNK)] = part.reshape(WIDE_CHUNK, groups, LANES)
        return carry

    lax.fori_loop(0, rows // WIDE_CHUNK, add, 0)


def kernel_grad_body(
    below_first, below_rest, low, from_left, from_right, folded, bias_terms, flag,
    keep, send, packed, taps, sums, below_grad,
):
    rows, groups = low.shape[0] // 2, low.shape[1]
    blank = jnp.zeros((groups, LANES), BF16)
    gather_grad(below_first, below_rest, below_grad)
    fill_plane(taps, 0, below_first.at[:rows], blank, blank)
    fill_plane(taps, 1, low.at[:rows], from_left[0], from_right[0])
    below_turned = below_grad[...].reshape(rows * groups, LANES).T
    low_turned = low[rows:].reshape(rows * groups, LANES).T
    for tap_y in range(3):
        rhs = taps[0, tap_y : tap_y + rows].reshape(rows * groups, 256)
        sums[0, tap_y] = jnp.dot(low_turned, rhs, preferred_element_type=F32)
        rhs = taps[1, tap_y : tap_y + rows].reshape(rows * groups, 256)
        sums[1, tap_y] = jnp.dot(below_turned, rhs, preferred_element_type=F32)
    sums[0, 2] += jnp.dot(from_left[1].T, taps[0, 1], preferred_element_type=F32)
    sums[0, 0] += jnp.dot(from_right[1].T, taps[0, rows], preferred_element_type=F32)
    lane = lax.broadcasted_iota(jnp.int32, (32, LANES), 1)
    parts = [folded[at // 3, at % 3] for at in range(9)]
    for tap_y in range(3):
        parts[tap_y] += fold(sums[0, tap_y])
        parts[6 + tap_y] += fold(sums[1, tap_y])
    row = jnp.sum(bias_terms[...], axis=0, keepdims=True)
    row = row + pltpu.roll(row, 64, 1)
    row = row + pltpu.roll(row, 32, 1)
    first = lax.broadcasted_iota(jnp.int32, (32, LANES), 0) == 0
    for place in range(7):
        if place < 6:
            extra = pltpu.roll(parts[7 + place // 3], 96 - 32 * (place % 3), 1)
        else:
            extra = jnp.where(first, jnp.broadcast_to(row, (32, LANES)), 0.0)
        packed[place * 32 : place * 32 + 32, :] = jnp.where(lane < 96, parts[place], extra)
    upper = flag[...] > 0.5
    keep[...] = jnp.where(upper, packed[HALF : 2 * HALF], packed[:HALF])
    send[...] = jnp.where(upper, packed[:HALF], packed[HALF : 2 * HALF])


def inner_sum(taps, weights, chunk, groups):
    total = None
    for plane in range(2):
        for tap_y in range(3):
            lhs = taps[plane, pl.ds(chunk * WIDE_CHUNK + tap_y, WIDE_CHUNK)].reshape(WIDE_CHUNK * groups, 256)
            matrix = jnp.concatenate([weights[plane + 1, tap_y], weights[plane, tap_y]], axis=1)
            term = jnp.dot(lhs, matrix, preferred_element_type=F32)
            total = term if total is None else total + term
    return total


def outer_body(count, *refs):
    first, rest = refs[0], refs[count - 1]
    weights, partial, line = refs[count : count + 3]
    output, grad_input, taps, scratch, grad = refs[-5:]
    rows, groups = partial.shape[2:4]
    repeated = jnp.concatenate([line[...]] * 4, axis=1)
    act, edge = first.at[:rows], rest.at[rest.shape[0] - 4 :]
    gather_grad(first, rest, grad)
    for kind, (source, out, turn) in enumerate(((act, output, rectified), (grad, grad_input, kept))):
        fill_plane(taps, kind, source, edge[kind], edge[2 + kind])
        for chunk in range(rows // CHUNK):
            start = chunk * CHUNK
            total = partial[kind, 0, start : start + CHUNK].reshape(CHUNK * groups, LANES)
            for tap_y in range(3):
                at = start + tap_y
                lhs = taps[kind, at : at + CHUNK].reshape(CHUNK * groups, 256)
                total = total + jnp.dot(lhs, weights[kind, 0, tap_y], preferred_element_type=F32)
            put_rows(scratch, turn(total, repeated), chunk, groups)
        lay_out(scratch, out, 0, rows, groups)


def rectified(total, line):
    return jnp.maximum(total + line, 0.0)


def kept(total, line):
    return total


def lay_out(scratch, out, plane, rows, groups):
    pitch = groups + PITCH
    for group in range(groups):
        halves = [scratch[pl.ds(half * 8 * pitch + group, 8, stride=pitch), :] for half in range(2)]
        block = jnp.concatenate(halves, axis=0).astype(BF16)
        out[plane, :, group * LANES : (group + 1) * LANES] = block


def put_rows(scratch, total, chunk, groups):
    for row in range(CHUNK):
        at = (chunk * CHUNK + row) * (groups + PITCH)
        scratch[at : at + groups, :] = total[row * groups : (row + 1) * groups]


HALF = 112
PITCH = 8


def join_body(part, other, flag, packed):
    upper = flag[...] > 0.5
    packed[:HALF] = jnp.where(upper, other[...], part[...])
    packed[HALF : 2 * HALF] = jnp.where(upper, part[...], other[...])


def unpack_body(scaling, part, one, two, three, grad_kernel, grad_bias):
    for place in range(7):
        span = slice(place * 32, place * 32 + 32)
        block = ((part[span, :] + one[span, :]) + (two[span, :] + three[span, :])) * scaling
        turned = block.T
        grad_kernel[place * 96 : place * 96 + 96, :] = turned[:96]
        if place < 6:
            grad_kernel[(21 + place) * 32 : (22 + place) * 32, :] = turned[96:]
        else:
            grad_bias[...] = pltpu.roll(block, 32, 1)[:1, :32]


def shifted(value, axis, step):
    count = lax.axis_size(axis)
    pairs = [(i, i + step) for i in range(count) if 0 <= i + step < count]
    return lax.ppermute(value, axis, pairs)


def swapped(value, bit):
    count = lax.axis_size("gz") * lax.axis_size("gy")
    return lax.ppermute(value, ("gz", "gy"), [(i, i ^ bit) for i in range(count)])


def sum_of_four(value, low, high):
    one, two, three = (swapped(value, bit) for bit in (low, high, low + high))
    return (value + one) + (two + three)


def local(activations, grad_out, relu_mask, kernel, bias):
    planes, rows, width = activations.shape
    groups = width // LANES
    block = activations.shape
    shape = jax.ShapeDtypeStruct
    pair = shape((2 * rows, groups, LANES), BF16)
    one_plane = pltpu.VMEM((rows, groups, LANES), BF16)
    lines = shape((4, groups, LANES), BF16)
    spread = pltpu.VMEM((rows * (groups + 8), LANES), F32)
    two_taps = pltpu.VMEM((2, rows + 2, groups, 2 * LANES), BF16)
    half = shape((HALF, LANES), F32)
    packed = pltpu.VMEM((2 * HALF, LANES), F32)
    flag = jnp.full((1, LANES), lax.axis_index("gy") % 2, F32)

    low, high_first, high_rest, firsts, lasts = pl.pallas_call(
        group_body,
        in_specs=[pl.BlockSpec(memory_space=pl.ANY)] * 3,
        out_shape=(
            pair, shape((rows + EARLY, groups, LANES), BF16), shape((rows - EARLY, groups, LANES), BF16), lines, lines,
        ),
        scratch_shapes=[
            spread, pltpu.VMEM(block, BF16), pltpu.VMEM(block, BF16), pltpu.VMEM(block, jnp.int32),
            pltpu.SemaphoreType.DMA((2, 3)),
        ],
        compiler_params=pltpu.CompilerParams(vmem_limit_bytes=56 * MIB),
    )(activations, grad_out, relu_mask)
    from_left = shifted(lasts, "gy", 1)
    from_right = shifted(firsts, "gy", -1)
    below_first = shifted(high_first, "gz", 1)
    below_rest = shifted(jnp.concatenate([high_rest, from_left[2:], from_right[2:]]), "gz", 1)

    line = bias.reshape(1, 32)
    flat_kernel = kernel.reshape(27 * 32, 32)
    plane = (rows, groups, LANES)
    folded_shape, bias_shape, weights_shape = (3, 3, 32, LANES), (8, LANES), (3, 3, 256, LANES)
    folded, bias_terms, partial, weights = blocked(
        own_body,
        2,
        (
            shape(folded_shape, F32), shape(bias_shape, F32),
            shape((2, 2, *plane), F32), shape((2, *weights_shape), BF16),
        ),
        (
            part_of(folded_shape, 0, 0, 0, 0), part_of(bias_shape, 0, 0),
            pl.BlockSpec((1, 2, *plane), lambda step: (step, 0, 0, 0, 0)),
            pl.BlockSpec((1, *weights_shape), lambda step: (step, 0, 0, 0, 0)),
        ),
        [pltpu.VMEM((2 * LANES, rows * groups), BF16), two_taps, one_plane],
        (low, high_first, high_rest, from_left, from_right, flat_kernel),
        [part_of(array.shape, 0, 0, 0) for array in (low, high_first, high_rest)] + [part_of(lines.shape, 0, 0, 0)] * 2 + [part_of(flat_kernel.shape, 0, 0)],
    )

    def outer(side, planes_beside, done=()):
        count = len(planes_beside)
        return blocked(
            functools.partial(outer_body, count),
            1,
            (shape(block, BF16), shape(block, BF16)),
            (part_of((1, *block[1:]), side, 0, 0),) * 2,
            [two_taps, spread, one_plane],
            (*planes_beside, weights, partial, line, *done),
            [
                *[part_of(array.shape, 0, 0, 0) for array in planes_beside],
                part_of((2, 1, 3, 256, LANES), 0, 2 * side, 0, 0, 0), part_of((2, 1, *plane), 0, side, 0, 0, 0),
                part_of(line.shape, 0, 0),
                *[pl.BlockSpec(memory_space=pl.ANY)] * len(done),
            ],
            {count + 3: 0, count + 4: 1} if done else None,
        )

    ends = (from_left[:2], from_right[:2])
    ends, folded, partial = lax.optimization_barrier((ends, folded, partial))
    down = jnp.concatenate([low, *ends])
    above = shifted(down, "gz", -1)

    part, send = call(
        kernel_grad_body,
        (half, half),
        [packed, two_taps, pltpu.VMEM((2, 3, LANES, 256), F32), one_plane],
        (below_first, below_rest, low, from_left, from_right, folded, bias_terms, flag),
    )
    part = part + swapped(send, 1)
    part = sum_of_four(part, 4, 8)
    part = sum_of_four(part, 32, 64)
    results = outer(0, (below_first, below_rest))
    part, results = lax.optimization_barrier((part, results))
    part = call(join_body, shape((2 * HALF, LANES), F32), [], (part, swapped(part, 1), flag))
    part, above = lax.optimization_barrier((part, above))
    others = [swapped(part, bit) for bit in (2, 16, 18)]
    results = outer(1, (above,), results)

    voxels = planes * lax.axis_size("gz") * rows * lax.axis_size("gy") * (width // 32)
    grad_kernel, grad_bias = call(
        functools.partial(unpack_body, 1.0 / math.sqrt(voxels)),
        (shape((27 * 32, 32), F32), shape((1, 32), F32)),
        [],
        (part, *others),
    )
    return *results, grad_kernel.reshape(3, 3, 3, 32, 32), grad_bias.reshape(32)


def solution(mesh):
    block = P("gz", "gy", None)
    return jax.shard_map(
        local,
        mesh=mesh,
        in_specs=(block, block, block, P(), P()),
        out_specs=(block, block, P(), P()),
        check_vma=False,
    )
```

```python
import functools
import math

import jax
import jax.numpy as jnp
from jax import lax
from jax.experimental import pallas as pl
from jax.experimental.pallas import tpu as pltpu
from jax.sharding import PartitionSpec as P

F32 = jnp.float32
BF16 = jnp.bfloat16
LANES = 128
MIB = 1024 * 1024


def call(body, outs, scratch, args):
    return pl.pallas_call(
        body,
        out_shape=outs,
        scratch_shapes=scratch,
        compiler_params=pltpu.CompilerParams(vmem_limit_bytes=20 * MIB),
    )(*args)


def blocked(body, grid, outs, out_specs, scratch, args, in_specs, aliases=None, flops=0):
    return pl.pallas_call(
        body,
        grid=(grid,),
        out_shape=outs,
        in_specs=in_specs,
        out_specs=out_specs,
        scratch_shapes=scratch,
        input_output_aliases=aliases or {},
        cost_estimate=pl.CostEstimate(flops=flops, bytes_accessed=0, transcendentals=0),
        compiler_params=pltpu.CompilerParams(vmem_limit_bytes=56 * MIB),
    )(*args)


def part_of(shape, *index):
    return pl.BlockSpec(shape, lambda step: index)


def spread_rows(scratch, groups, group, block):
    pitch = groups + 1
    for half in range(2):
        scratch[pl.ds(half * 8 * pitch + group, 8, stride=pitch), :] = block[half * 8 : half * 8 + 8]


def group_body(act_in, grad_in, mask_in, low, high_first, high_rest, firsts, lasts, scratch, act, grad, mask, arrived):
    rows, groups = act.shape[1], low.shape[1]
    copies = [
        [
            pltpu.make_async_copy(source.at[plane], target.at[plane], arrived.at[plane, place])
            for place, (source, target) in enumerate(((act_in, act), (mask_in, mask), (grad_in, grad)))
        ]
        for plane in range(2)
    ]
    for plane in (1, 0):
        for copy in copies[plane]:
            copy.start()
    for plane in (1, 0):
        for kind in range(2):
            out = high_first if plane else low
            for copy in copies[plane][:1] if kind == 0 else copies[plane][1:]:
                copy.wait()
            for group in range(groups):
                span = slice(group * LANES, (group + 1) * LANES)
                if kind == 0:
                    block = act[plane, :, span].astype(F32)
                else:
                    block = grad[plane, :, span].astype(F32) * mask[plane, :, span].astype(F32)
                spread_rows(scratch, groups, group, block)
            for row in range(rows):
                at = row * (groups + 1)
                cells = scratch[at : at + groups, :].astype(BF16)
                if plane and kind and row >= EARLY:
                    high_rest[row - EARLY] = cells
                else:
                    out[kind * rows + row] = cells
                if row == 0:
                    firsts[plane * 2 + kind] = cells
                if row == rows - 1:
                    lasts[plane * 2 + kind] = cells


def with_edges(cells):
    groups = cells.shape[0]
    wide = cells.astype(F32)
    lane = lax.broadcasted_iota(jnp.int32, wide.shape, 1)
    row = lax.broadcasted_iota(jnp.int32, wide.shape, 0)
    before = jnp.where(row == 0, 0.0, pltpu.roll(wide, 1, 0))
    after = jnp.where(row == groups - 1, 0.0, pltpu.roll(wide, groups - 1, 0))
    return jnp.concatenate([cells, jnp.where(lane < 64, after, before).astype(BF16)], axis=1)


def fill_plane(taps, place, source, first, last):
    rows = source.shape[0]
    taps[place, 0] = with_edges(first)
    taps[place, rows + 1] = with_edges(last)

    def step(row, carry):
        taps[place, row + 1] = with_edges(source[row])
        return carry

    lax.fori_loop(0, rows, step, 0, unroll=2)


def build_weights(kernel, flip, out):
    lane = lax.broadcasted_iota(jnp.int32, (32, LANES), 1) // 32
    for tap_z in range(3):
        for tap_y in range(3):
            blocks = []
            for tap_x in range(3):
                at = (tap_z * 3 + tap_y) * 3 + tap_x
                at = 26 - at if flip else at
                block = kernel[at * 32 : at * 32 + 32, :].astype(F32)
                block = block.T if flip else block
                blocks.append(jnp.concatenate([block] * 4, axis=1))
            for place in range(8):
                voxel = place if place < 6 else place - 8
                total = jnp.zeros((32, LANES), F32)
                for tap_x in range(3):
                    total = jnp.where(lane == voxel - tap_x + 1, blocks[tap_x], total)
                out[tap_z, tap_y, place * 32 : place * 32 + 32, :] = total.astype(BF16)


CHUNK = 4
EARLY = 8


def fold(term):
    total = None
    for voxel in range(4):
        part = term[voxel * 32 : voxel * 32 + 32]
        shift = (-(voxel - 1) * 32) % 256
        if shift:
            part = pltpu.roll(part, shift, 1)
        total = part if total is None else total + part
    return total[:, :LANES]


def gather_grad(first, rest, grad):
    rows = grad.shape[0]
    if first.shape == rest.shape:
        grad[...] = first[rows : 2 * rows]
    else:
        grad[:EARLY] = first[rows:]
        grad[EARLY:] = rest[: rows - EARLY]


def own_body(
    low, high_first, high_rest, from_left, from_right, kernel,
    folded, bias_terms, partial_f, weights_f, partial_g, weights_g, turned, taps, high_grad,
):
    rows, groups = low.shape[0] // 2, low.shape[1]
    chunks = rows // CHUNK
    step = pl.program_id(0)

    def fill(kind):
        for plane, source in enumerate((low.at[kind * rows : kind * rows + rows], (high_first.at[:rows], high_grad)[kind])):
            at = 2 * plane + kind
            fill_plane(taps, plane, source, from_left[at], from_right[at])

    @pl.when(step == 0)
    def _():
        gather_grad(high_first, high_rest, high_grad)
        sums = jnp.zeros((8, LANES), F32)
        for plane, source in enumerate((low.at[rows:], high_grad)):
            flat = source[...].reshape(rows * groups, LANES)
            turned[plane * LANES : (plane + 1) * LANES, :] = flat.T
            sums = sums + jnp.sum(flat.astype(F32).reshape(-1, 8, LANES), axis=0)
        bias_terms[...] = sums
        build_weights(kernel, False, weights_f)
        build_weights(kernel, True, weights_g)
        fill(0)
        for tap_y in range(3):
            both = []
            for plane in range(2):
                rhs = taps[plane, tap_y : tap_y + rows].reshape(rows * groups, 256)
                both.append(jnp.dot(turned[...], rhs, preferred_element_type=F32))
            folded[1, tap_y] = fold(both[0][:LANES] + both[1][LANES:])
            folded[0, tap_y] = fold(both[0][LANES:])
            folded[2, tap_y] = fold(both[1][:LANES])

    @pl.when(step == chunks)
    def _():
        fill(1)

    def add(weights, partial, chunk):
        total = inner_sum(taps, weights, chunk, groups)
        for plane in range(2):
            part = total[:, plane * LANES : (plane + 1) * LANES]
            partial[plane] = part.reshape(CHUNK, groups, LANES)

    @pl.when(step < chunks)
    def _():
        add(weights_f, partial_f, step)

    @pl.when(step >= chunks)
    def _():
        add(weights_g, partial_g, step - chunks)


def kernel_grad_body(
    below_first, below_rest, low, from_left, from_right, folded, bias_terms, flag,
    keep, send, packed, taps, sums, below_grad,
):
    rows, groups = low.shape[0] // 2, low.shape[1]
    blank = jnp.zeros((groups, LANES), BF16)
    gather_grad(below_first, below_rest, below_grad)
    fill_plane(taps, 0, below_first.at[:rows], blank, blank)
    fill_plane(taps, 1, low.at[:rows], from_left[0], from_right[0])
    below_turned = below_grad[...].reshape(rows * groups, LANES).T
    low_turned = low[rows:].reshape(rows * groups, LANES).T
    for tap_y in range(3):
        rhs = taps[0, tap_y : tap_y + rows].reshape(rows * groups, 256)
        sums[0, tap_y] = jnp.dot(low_turned, rhs, preferred_element_type=F32)
        rhs = taps[1, tap_y : tap_y + rows].reshape(rows * groups, 256)
        sums[1, tap_y] = jnp.dot(below_turned, rhs, preferred_element_type=F32)
    sums[0, 2] += jnp.dot(from_left[1].T, taps[0, 1], preferred_element_type=F32)
    sums[0, 0] += jnp.dot(from_right[1].T, taps[0, rows], preferred_element_type=F32)
    lane = lax.broadcasted_iota(jnp.int32, (32, LANES), 1)
    parts = [folded[at // 3, at % 3] for at in range(9)]
    for tap_y in range(3):
        parts[tap_y] += fold(sums[0, tap_y])
        parts[6 + tap_y] += fold(sums[1, tap_y])
    row = jnp.sum(bias_terms[...], axis=0, keepdims=True)
    row = row + pltpu.roll(row, 64, 1)
    row = row + pltpu.roll(row, 32, 1)
    first = lax.broadcasted_iota(jnp.int32, (32, LANES), 0) == 0
    for place in range(7):
        if place < 6:
            extra = pltpu.roll(parts[7 + place // 3], 96 - 32 * (place % 3), 1)
        else:
            extra = jnp.where(first, jnp.broadcast_to(row, (32, LANES)), 0.0)
        packed[place * 32 : place * 32 + 32, :] = jnp.where(lane < 96, parts[place], extra)
    upper = flag[...] > 0.5
    keep[...] = jnp.where(upper, packed[HALF : 2 * HALF], packed[:HALF])
    send[...] = jnp.where(upper, packed[:HALF], packed[HALF : 2 * HALF])


def inner_sum(taps, weights, chunk, groups):
    total = None
    for plane in range(2):
        for tap_y in range(3):
            lhs = taps[plane, pl.ds(chunk * CHUNK + tap_y, CHUNK)].reshape(CHUNK * groups, 256)
            matrix = jnp.concatenate([weights[plane + 1, tap_y], weights[plane, tap_y]], axis=1)
            term = jnp.dot(lhs, matrix, preferred_element_type=F32)
            total = term if total is None else total + term
    return total


def outer_body(count, *refs):
    first, rest = refs[0], refs[count - 1]
    weights_f, weights_g, partial_f, partial_g, line = refs[count : count + 5]
    output, grad_input, taps, scratch, grad = refs[-5:]
    rows, groups = partial_f.shape[1:3]
    repeated = jnp.concatenate([line[...]] * 4, axis=1)
    act, edge = first.at[:rows], rest.at[rest.shape[0] - 4 :]
    gather_grad(first, rest, grad)
    for kind, (source, weights, partial, out, turn) in enumerate(
        (
            (act, weights_f, partial_f, output, rectified),
            (grad, weights_g, partial_g, grad_input, kept),
        )
    ):
        fill_plane(taps, kind, source, edge[kind], edge[2 + kind])
        for chunk in range(rows // CHUNK):
            start = chunk * CHUNK
            total = partial[0, start : start + CHUNK].reshape(CHUNK * groups, LANES)
            for tap_y in range(3):
                at = start + tap_y
                lhs = taps[kind, at : at + CHUNK].reshape(CHUNK * groups, 256)
                total = total + jnp.dot(lhs, weights[0, tap_y], preferred_element_type=F32)
            put_rows(scratch, turn(total, repeated), chunk, groups)
        lay_out(scratch, out, 0, rows, groups)


def rectified(total, line):
    return jnp.maximum(total + line, 0.0)


def kept(total, line):
    return total


def lay_out(scratch, out, plane, rows, groups):
    pitch = groups + 1
    for group in range(groups):
        halves = [scratch[pl.ds(half * 8 * pitch + group, 8, stride=pitch), :] for half in range(2)]
        block = jnp.concatenate(halves, axis=0).astype(BF16)
        out[plane, :, group * LANES : (group + 1) * LANES] = block


def put_rows(scratch, total, chunk, groups):
    for row in range(CHUNK):
        at = (chunk * CHUNK + row) * (groups + 1)
        scratch[at : at + groups, :] = total[row * groups : (row + 1) * groups]


HALF = 112


def join_body(part, other, flag, packed):
    upper = flag[...] > 0.5
    packed[:HALF] = jnp.where(upper, other[...], part[...])
    packed[HALF : 2 * HALF] = jnp.where(upper, part[...], other[...])


def unpack_body(scaling, part, one, two, three, grad_kernel, grad_bias):
    for place in range(7):
        span = slice(place * 32, place * 32 + 32)
        block = ((part[span, :] + one[span, :]) + (two[span, :] + three[span, :])) * scaling
        turned = block.T
        grad_kernel[place * 96 : place * 96 + 96, :] = turned[:96]
        if place < 6:
            grad_kernel[(21 + place) * 32 : (22 + place) * 32, :] = turned[96:]
        else:
            grad_bias[...] = pltpu.roll(block, 32, 1)[:1, :32]


def shifted(value, axis, step):
    count = lax.axis_size(axis)
    pairs = [(i, i + step) for i in range(count) if 0 <= i + step < count]
    return lax.ppermute(value, axis, pairs)


def swapped(value, bit):
    count = lax.axis_size("gz") * lax.axis_size("gy")
    return lax.ppermute(value, ("gz", "gy"), [(i, i ^ bit) for i in range(count)])


def sum_of_four(value, low, high):
    one, two, three = (swapped(value, bit) for bit in (low, high, low + high))
    return (value + one) + (two + three)


def local(activations, grad_out, relu_mask, kernel, bias):
    planes, rows, width = activations.shape
    groups = width // LANES
    block = activations.shape
    shape = jax.ShapeDtypeStruct
    pair = shape((2 * rows, groups, LANES), BF16)
    one_plane = pltpu.VMEM((rows, groups, LANES), BF16)
    lines = shape((4, groups, LANES), BF16)
    spread = pltpu.VMEM((rows * (groups + 1) + 8, LANES), F32)
    two_taps = pltpu.VMEM((2, rows + 2, groups, 2 * LANES), BF16)
    half = shape((HALF, LANES), F32)
    packed = pltpu.VMEM((2 * HALF, LANES), F32)
    flag = jnp.full((1, LANES), lax.axis_index("gy") % 2, F32)

    low, high_first, high_rest, firsts, lasts = pl.pallas_call(
        group_body,
        in_specs=[pl.BlockSpec(memory_space=pl.ANY)] * 3,
        out_shape=(
            pair, shape((rows + EARLY, groups, LANES), BF16), shape((rows - EARLY, groups, LANES), BF16), lines, lines,
        ),
        scratch_shapes=[
            spread, pltpu.VMEM(block, BF16), pltpu.VMEM(block, BF16), pltpu.VMEM(block, jnp.int32),
            pltpu.SemaphoreType.DMA((2, 3)),
        ],
        compiler_params=pltpu.CompilerParams(vmem_limit_bytes=56 * MIB),
    )(activations, grad_out, relu_mask)
    from_left = shifted(lasts, "gy", 1)
    from_right = shifted(firsts, "gy", -1)
    below_first = shifted(high_first, "gz", 1)
    below_rest = shifted(jnp.concatenate([high_rest, from_left[2:], from_right[2:]]), "gz", 1)

    line = bias.reshape(1, 32)
    flat_kernel = kernel.reshape(27 * 32, 32)
    chunks = rows // CHUNK
    plane = (rows, groups, LANES)
    folded_shape, bias_shape, weights_shape = (3, 3, 32, LANES), (8, LANES), (3, 3, 256, LANES)
    piece = (2, CHUNK, groups, LANES)
    folded, bias_terms, partial_f, weights_f, partial_g, weights_g = blocked(
        own_body,
        2 * chunks,
        (
            shape(folded_shape, F32), shape(bias_shape, F32),
            shape((2, *plane), F32), shape(weights_shape, BF16),
            shape((2, *plane), F32), shape(weights_shape, BF16),
        ),
        (
            part_of(folded_shape, 0, 0, 0, 0), part_of(bias_shape, 0, 0),
            pl.BlockSpec(piece, lambda step: (0, jnp.minimum(step, chunks - 1), 0, 0)),
            part_of(weights_shape, 0, 0, 0, 0),
            pl.BlockSpec(piece, lambda step: (0, jnp.maximum(step - chunks, 0), 0, 0)),
            part_of(weights_shape, 0, 0, 0, 0),
        ),
        [pltpu.VMEM((2 * LANES, rows * groups), BF16), two_taps, one_plane],
        (low, high_first, high_rest, from_left, from_right, flat_kernel),
        [part_of(array.shape, 0, 0, 0) for array in (low, high_first, high_rest)] + [part_of(lines.shape, 0, 0, 0)] * 2 + [part_of(flat_kernel.shape, 0, 0)],
    )

    def outer(side, beside, done=()):
        weights, partial = part_of((1, 3, 256, LANES), 2 * side, 0, 0, 0), part_of((1, *plane), side, 0, 0, 0)
        return blocked(
            functools.partial(outer_body, len(beside)),
            1,
            (shape(block, BF16), shape(block, BF16)),
            (part_of((1, *block[1:]), side, 0, 0),) * 2,
            [two_taps, spread, one_plane],
            (*beside, weights_f, weights_g, partial_f, partial_g, line, *done),
            [
                *[part_of(array.shape, 0, 0, 0) for array in beside],
                weights, weights, partial, partial, part_of(line.shape, 0, 0),
                *[pl.BlockSpec(memory_space=pl.ANY)] * len(done),
            ],
            {len(beside) + 5: 0, len(beside) + 6: 1} if done else None,
        )

    ends = (from_left[:2], from_right[:2])
    ends, folded, partial_g = lax.optimization_barrier((ends, folded, partial_g))
    down = jnp.concatenate([low, *ends])
    above = shifted(down, "gz", -1)

    part, send = call(
        kernel_grad_body,
        (half, half),
        [packed, two_taps, pltpu.VMEM((2, 3, LANES, 256), F32), one_plane],
        (below_first, below_rest, low, from_left, from_right, folded, bias_terms, flag),
    )
    part = part + swapped(send, 1)
    part = sum_of_four(part, 4, 8)
    part = sum_of_four(part, 32, 64)
    results = outer(0, (below_first, below_rest))
    part, results = lax.optimization_barrier((part, results))
    part = call(join_body, shape((2 * HALF, LANES), F32), [], (part, swapped(part, 1), flag))
    part, above = lax.optimization_barrier((part, above))
    others = [swapped(part, bit) for bit in (2, 16, 18)]
    results = outer(1, (above,), results)

    voxels = planes * lax.axis_size("gz") * rows * lax.axis_size("gy") * (width // 32)
    grad_kernel, grad_bias = call(
        functools.partial(unpack_body, 1.0 / math.sqrt(voxels)),
        (shape((27 * 32, 32), F32), shape((1, 32), F32)),
        [],
        (part, *others),
    )
    return *results, grad_kernel.reshape(3, 3, 3, 32, 32), grad_bias.reshape(32)


def solution(mesh):
    block = P("gz", "gy", None)
    return jax.shard_map(
        local,
        mesh=mesh,
        in_specs=(block, block, block, P(), P()),
        out_specs=(block, block, P(), P()),
        check_vma=False,
    )
```

```python
import functools
import math

import jax
import jax.numpy as jnp
from jax import lax
from jax.experimental import pallas as pl
from jax.experimental.pallas import tpu as pltpu
from jax.sharding import PartitionSpec as P

F32 = jnp.float32
BF16 = jnp.bfloat16
LANES = 128
MIB = 1024 * 1024


def call(body, outs, scratch, args):
    return pl.pallas_call(
        body,
        out_shape=outs,
        scratch_shapes=scratch,
        compiler_params=pltpu.CompilerParams(vmem_limit_bytes=20 * MIB),
    )(*args)


def blocked(body, grid, outs, out_specs, scratch, args, in_specs, aliases=None, flops=0):
    return pl.pallas_call(
        body,
        grid=(grid,),
        out_shape=outs,
        in_specs=in_specs,
        out_specs=out_specs,
        scratch_shapes=scratch,
        input_output_aliases=aliases or {},
        cost_estimate=pl.CostEstimate(flops=flops, bytes_accessed=0, transcendentals=0),
        compiler_params=pltpu.CompilerParams(vmem_limit_bytes=56 * MIB),
    )(*args)


def part_of(shape, *index):
    return pl.BlockSpec(shape, lambda step: index)


def spread_rows(scratch, groups, group, block):
    pitch = groups + 1
    for half in range(2):
        scratch[pl.ds(half * 8 * pitch + group, 8, stride=pitch), :] = block[half * 8 : half * 8 + 8]


def group_body(act_in, grad_in, mask_in, low, high_first, high_rest, firsts, lasts, scratch, act, grad, mask, arrived):
    rows, groups = act.shape[1], low.shape[1]
    copies = [
        [
            pltpu.make_async_copy(source.at[plane], target.at[plane], arrived.at[plane, place])
            for place, (source, target) in enumerate(((act_in, act), (mask_in, mask), (grad_in, grad)))
        ]
        for plane in range(2)
    ]
    for plane in (1, 0):
        for copy in copies[plane]:
            copy.start()
    for plane in (1, 0):
        for kind in range(2):
            out = high_first if plane else low
            for copy in copies[plane][:1] if kind == 0 else copies[plane][1:]:
                copy.wait()
            for group in range(groups):
                span = slice(group * LANES, (group + 1) * LANES)
                if kind == 0:
                    block = act[plane, :, span].astype(F32)
                else:
                    block = grad[plane, :, span].astype(F32) * mask[plane, :, span].astype(F32)
                spread_rows(scratch, groups, group, block)
            for row in range(rows):
                at = row * (groups + 1)
                cells = scratch[at : at + groups, :].astype(BF16)
                if plane and kind and row >= EARLY:
                    high_rest[row - EARLY] = cells
                else:
                    out[kind * rows + row] = cells
                if row == 0:
                    firsts[plane * 2 + kind] = cells
                if row == rows - 1:
                    lasts[plane * 2 + kind] = cells


def with_edges(cells):
    groups = cells.shape[0]
    wide = cells.astype(F32)
    lane = lax.broadcasted_iota(jnp.int32, wide.shape, 1)
    row = lax.broadcasted_iota(jnp.int32, wide.shape, 0)
    before = jnp.where(row == 0, 0.0, pltpu.roll(wide, 1, 0))
    after = jnp.where(row == groups - 1, 0.0, pltpu.roll(wide, groups - 1, 0))
    return jnp.concatenate([cells, jnp.where(lane < 64, after, before).astype(BF16)], axis=1)


def fill_plane(taps, place, source, first, last):
    rows = source.shape[0]
    taps[place, 0] = with_edges(first)
    taps[place, rows + 1] = with_edges(last)

    def step(row, carry):
        taps[place, row + 1] = with_edges(source[row])
        return carry

    lax.fori_loop(0, rows, step, 0, unroll=2)


def build_weights(kernel, flip, out):
    lane = lax.broadcasted_iota(jnp.int32, (32, LANES), 1) // 32
    for tap_z in range(3):
        for tap_y in range(3):
            blocks = []
            for tap_x in range(3):
                at = (tap_z * 3 + tap_y) * 3 + tap_x
                at = 26 - at if flip else at
                block = kernel[at * 32 : at * 32 + 32, :].astype(F32)
                block = block.T if flip else block
                blocks.append(jnp.concatenate([block] * 4, axis=1))
            for place in range(8):
                voxel = place if place < 6 else place - 8
                total = jnp.zeros((32, LANES), F32)
                for tap_x in range(3):
                    total = jnp.where(lane == voxel - tap_x + 1, blocks[tap_x], total)
                out[tap_z, tap_y, place * 32 : place * 32 + 32, :] = total.astype(BF16)


CHUNK = 4
EARLY = 8


def fold(term):
    total = None
    for voxel in range(4):
        part = term[voxel * 32 : voxel * 32 + 32]
        shift = (-(voxel - 1) * 32) % 256
        if shift:
            part = pltpu.roll(part, shift, 1)
        total = part if total is None else total + part
    return total[:, :LANES]


def gather_grad(first, rest, grad):
    rows = grad.shape[0]
    if first.shape == rest.shape:
        grad[...] = first[rows : 2 * rows]
    else:
        grad[:EARLY] = first[rows:]
        grad[EARLY:] = rest[: rows - EARLY]


def own_body(
    low, high_first, high_rest, from_left, from_right, kernel,
    folded, bias_terms, partial_f, weights_f, partial_g, weights_g, turned, taps, high_grad,
):
    rows, groups = low.shape[0] // 2, low.shape[1]
    chunks = rows // CHUNK
    step = pl.program_id(0)

    def fill(kind):
        for plane, source in enumerate((low.at[kind * rows : kind * rows + rows], (high_first.at[:rows], high_grad)[kind])):
            at = 2 * plane + kind
            fill_plane(taps, plane, source, from_left[at], from_right[at])

    @pl.when(step == 0)
    def _():
        gather_grad(high_first, high_rest, high_grad)
        sums = jnp.zeros((8, LANES), F32)
        for plane, source in enumerate((low.at[rows:], high_grad)):
            flat = source[...].reshape(rows * groups, LANES)
            turned[plane * LANES : (plane + 1) * LANES, :] = flat.T
            sums = sums + jnp.sum(flat.astype(F32).reshape(-1, 8, LANES), axis=0)
        bias_terms[...] = sums
        build_weights(kernel, False, weights_f)
        build_weights(kernel, True, weights_g)
        fill(0)
        for tap_y in range(3):
            both = []
            for plane in range(2):
                rhs = taps[plane, tap_y : tap_y + rows].reshape(rows * groups, 256)
                both.append(jnp.dot(turned[...], rhs, preferred_element_type=F32))
            folded[1, tap_y] = fold(both[0][:LANES] + both[1][LANES:])
            folded[0, tap_y] = fold(both[0][LANES:])
            folded[2, tap_y] = fold(both[1][:LANES])

    @pl.when(step == chunks)
    def _():
        fill(1)

    def add(weights, partial, chunk):
        total = inner_sum(taps, weights, chunk, groups)
        for plane in range(2):
            part = total[:, plane * LANES : (plane + 1) * LANES]
            partial[plane] = part.reshape(CHUNK, groups, LANES)

    @pl.when(step < chunks)
    def _():
        add(weights_f, partial_f, step)

    @pl.when(step >= chunks)
    def _():
        add(weights_g, partial_g, step - chunks)


def kernel_grad_body(
    below_first, below_rest, low, from_left, from_right, folded, bias_terms,
    keep, send, packed, taps, sums, below_grad,
):
    rows, groups = low.shape[0] // 2, low.shape[1]
    blank = jnp.zeros((groups, LANES), BF16)
    gather_grad(below_first, below_rest, below_grad)
    fill_plane(taps, 0, below_first.at[:rows], blank, blank)
    fill_plane(taps, 1, low.at[:rows], from_left[0], from_right[0])
    below_turned = below_grad[...].reshape(rows * groups, LANES).T
    low_turned = low[rows:].reshape(rows * groups, LANES).T
    for tap_y in range(3):
        rhs = taps[0, tap_y : tap_y + rows].reshape(rows * groups, 256)
        sums[0, tap_y] = jnp.dot(low_turned, rhs, preferred_element_type=F32)
        rhs = taps[1, tap_y : tap_y + rows].reshape(rows * groups, 256)
        sums[1, tap_y] = jnp.dot(below_turned, rhs, preferred_element_type=F32)
    sums[0, 2] += jnp.dot(from_left[1].T, taps[0, 1], preferred_element_type=F32)
    sums[0, 0] += jnp.dot(from_right[1].T, taps[0, rows], preferred_element_type=F32)
    lane = lax.broadcasted_iota(jnp.int32, (32, LANES), 1)
    parts = [folded[at // 3, at % 3] for at in range(9)]
    for tap_y in range(3):
        parts[tap_y] += fold(sums[0, tap_y])
        parts[6 + tap_y] += fold(sums[1, tap_y])
    row = jnp.sum(bias_terms[...], axis=0, keepdims=True)
    row = row + pltpu.roll(row, 64, 1)
    row = row + pltpu.roll(row, 32, 1)
    first = lax.broadcasted_iota(jnp.int32, (32, LANES), 0) == 0
    for place in range(7):
        if place < 6:
            extra = pltpu.roll(parts[7 + place // 3], 96 - 32 * (place % 3), 1)
        else:
            extra = jnp.where(first, jnp.broadcast_to(row, (32, LANES)), 0.0)
        packed[place * 32 : place * 32 + 32, :] = jnp.where(lane < 96, parts[place], extra)
    upper = lax.rem(lax.axis_index("gy"), 2) == 1
    keep[...] = jnp.where(upper, packed[HALF : 2 * HALF], packed[:HALF])
    send[...] = jnp.where(upper, packed[:HALF], packed[HALF : 2 * HALF])


def inner_sum(taps, weights, chunk, groups):
    total = None
    for plane in range(2):
        for tap_y in range(3):
            lhs = taps[plane, pl.ds(chunk * CHUNK + tap_y, CHUNK)].reshape(CHUNK * groups, 256)
            matrix = jnp.concatenate([weights[plane + 1, tap_y], weights[plane, tap_y]], axis=1)
            term = jnp.dot(lhs, matrix, preferred_element_type=F32)
            total = term if total is None else total + term
    return total


def outer_body(count, *refs):
    first, rest = refs[0], refs[count - 1]
    weights_f, weights_g, partial_f, partial_g, line = refs[count : count + 5]
    output, grad_input, taps, scratch, grad = refs[-5:]
    rows, groups = partial_f.shape[1:3]
    repeated = jnp.concatenate([line[...]] * 4, axis=1)
    act, edge = first.at[:rows], rest.at[rest.shape[0] - 4 :]
    gather_grad(first, rest, grad)
    for kind, (source, weights, partial, out, turn) in enumerate(
        (
            (act, weights_f, partial_f, output, rectified),
            (grad, weights_g, partial_g, grad_input, kept),
        )
    ):
        fill_plane(taps, kind, source, edge[kind], edge[2 + kind])
        for chunk in range(rows // CHUNK):
            start = chunk * CHUNK
            total = partial[0, start : start + CHUNK].reshape(CHUNK * groups, LANES)
            for tap_y in range(3):
                at = start + tap_y
                lhs = taps[kind, at : at + CHUNK].reshape(CHUNK * groups, 256)
                total = total + jnp.dot(lhs, weights[0, tap_y], preferred_element_type=F32)
            put_rows(scratch, turn(total, repeated), chunk, groups)
        lay_out(scratch, out, 0, rows, groups)


def rectified(total, line):
    return jnp.maximum(total + line, 0.0)


def kept(total, line):
    return total


def lay_out(scratch, out, plane, rows, groups):
    pitch = groups + 1
    for group in range(groups):
        halves = [scratch[pl.ds(half * 8 * pitch + group, 8, stride=pitch), :] for half in range(2)]
        block = jnp.concatenate(halves, axis=0).astype(BF16)
        out[plane, :, group * LANES : (group + 1) * LANES] = block


def put_rows(scratch, total, chunk, groups):
    for row in range(CHUNK):
        at = (chunk * CHUNK + row) * (groups + 1)
        scratch[at : at + groups, :] = total[row * groups : (row + 1) * groups]


HALF = 112


def join_body(part, other, packed):
    upper = lax.rem(lax.axis_index("gy"), 2) == 1
    packed[:HALF] = jnp.where(upper, other[...], part[...])
    packed[HALF : 2 * HALF] = jnp.where(upper, part[...], other[...])


def unpack_body(scaling, part, one, two, three, grad_kernel, grad_bias):
    for place in range(7):
        span = slice(place * 32, place * 32 + 32)
        block = ((part[span, :] + one[span, :]) + (two[span, :] + three[span, :])) * scaling
        turned = block.T
        grad_kernel[place * 96 : place * 96 + 96, :] = turned[:96]
        if place < 6:
            grad_kernel[(21 + place) * 32 : (22 + place) * 32, :] = turned[96:]
        else:
            grad_bias[...] = pltpu.roll(block, 32, 1)[:1, :32]


def shifted(value, axis, step):
    count = lax.axis_size(axis)
    pairs = [(i, i + step) for i in range(count) if 0 <= i + step < count]
    return lax.ppermute(value, axis, pairs)


def swapped(value, bit):
    count = lax.axis_size("gz") * lax.axis_size("gy")
    return lax.ppermute(value, ("gz", "gy"), [(i, i ^ bit) for i in range(count)])


def sum_of_four(value, low, high):
    one, two, three = (swapped(value, bit) for bit in (low, high, low + high))
    return (value + one) + (two + three)


def local(activations, grad_out, relu_mask, kernel, bias):
    planes, rows, width = activations.shape
    groups = width // LANES
    block = activations.shape
    shape = jax.ShapeDtypeStruct
    pair = shape((2 * rows, groups, LANES), BF16)
    one_plane = pltpu.VMEM((rows, groups, LANES), BF16)
    lines = shape((4, groups, LANES), BF16)
    spread = pltpu.VMEM((rows * (groups + 1) + 8, LANES), F32)
    two_taps = pltpu.VMEM((2, rows + 2, groups, 2 * LANES), BF16)
    half = shape((HALF, LANES), F32)
    packed = pltpu.VMEM((2 * HALF, LANES), F32)

    low, high_first, high_rest, firsts, lasts = pl.pallas_call(
        group_body,
        in_specs=[pl.BlockSpec(memory_space=pl.ANY)] * 3,
        out_shape=(
            pair, shape((rows + EARLY, groups, LANES), BF16), shape((rows - EARLY, groups, LANES), BF16), lines, lines,
        ),
        scratch_shapes=[
            spread, pltpu.VMEM(block, BF16), pltpu.VMEM(block, BF16), pltpu.VMEM(block, jnp.int32),
            pltpu.SemaphoreType.DMA((2, 3)),
        ],
        compiler_params=pltpu.CompilerParams(vmem_limit_bytes=56 * MIB),
    )(activations, grad_out, relu_mask)
    from_left = shifted(lasts, "gy", 1)
    from_right = shifted(firsts, "gy", -1)
    below_first = shifted(high_first, "gz", 1)
    below_rest = shifted(jnp.concatenate([high_rest, from_left[2:], from_right[2:]]), "gz", 1)

    line = bias.reshape(1, 32)
    flat_kernel = kernel.reshape(27 * 32, 32)
    chunks = rows // CHUNK
    plane = (rows, groups, LANES)
    folded_shape, bias_shape, weights_shape = (3, 3, 32, LANES), (8, LANES), (3, 3, 256, LANES)
    piece = (2, CHUNK, groups, LANES)
    folded, bias_terms, partial_f, weights_f, partial_g, weights_g = blocked(
        own_body,
        2 * chunks,
        (
            shape(folded_shape, F32), shape(bias_shape, F32),
            shape((2, *plane), F32), shape(weights_shape, BF16),
            shape((2, *plane), F32), shape(weights_shape, BF16),
        ),
        (
            part_of(folded_shape, 0, 0, 0, 0), part_of(bias_shape, 0, 0),
            pl.BlockSpec(piece, lambda step: (0, jnp.minimum(step, chunks - 1), 0, 0)),
            part_of(weights_shape, 0, 0, 0, 0),
            pl.BlockSpec(piece, lambda step: (0, jnp.maximum(step - chunks, 0), 0, 0)),
            part_of(weights_shape, 0, 0, 0, 0),
        ),
        [pltpu.VMEM((2 * LANES, rows * groups), BF16), two_taps, one_plane],
        (low, high_first, high_rest, from_left, from_right, flat_kernel),
        [part_of(array.shape, 0, 0, 0) for array in (low, high_first, high_rest)] + [part_of(lines.shape, 0, 0, 0)] * 2 + [part_of(flat_kernel.shape, 0, 0)],
    )

    def outer(side, beside, done=()):
        weights, partial = part_of((1, 3, 256, LANES), 2 * side, 0, 0, 0), part_of((1, *plane), side, 0, 0, 0)
        return blocked(
            functools.partial(outer_body, len(beside)),
            1,
            (shape(block, BF16), shape(block, BF16)),
            (part_of((1, *block[1:]), side, 0, 0),) * 2,
            [two_taps, spread, one_plane],
            (*beside, weights_f, weights_g, partial_f, partial_g, line, *done),
            [
                *[part_of(array.shape, 0, 0, 0) for array in beside],
                weights, weights, partial, partial, part_of(line.shape, 0, 0),
                *[pl.BlockSpec(memory_space=pl.ANY)] * len(done),
            ],
            {len(beside) + 5: 0, len(beside) + 6: 1} if done else None,
        )

    ends = (from_left[:2], from_right[:2])
    ends, folded, partial_g = lax.optimization_barrier((ends, folded, partial_g))
    down = jnp.concatenate([low, *ends])
    above = shifted(down, "gz", -1)

    part, send = call(
        kernel_grad_body,
        (half, half),
        [packed, two_taps, pltpu.VMEM((2, 3, LANES, 256), F32), one_plane],
        (below_first, below_rest, low, from_left, from_right, folded, bias_terms),
    )
    part = part + swapped(send, 1)
    part = sum_of_four(part, 4, 8)
    part = sum_of_four(part, 32, 64)
    results = outer(0, (below_first, below_rest))
    part, results = lax.optimization_barrier((part, results))
    part = call(join_body, shape((2 * HALF, LANES), F32), [], (part, swapped(part, 1)))
    part, above = lax.optimization_barrier((part, above))
    others = [swapped(part, bit) for bit in (2, 16, 18)]
    results = outer(1, (above,), results)

    voxels = planes * lax.axis_size("gz") * rows * lax.axis_size("gy") * (width // 32)
    grad_kernel, grad_bias = call(
        functools.partial(unpack_body, 1.0 / math.sqrt(voxels)),
        (shape((27 * 32, 32), F32), shape((1, 32), F32)),
        [],
        (part, *others),
    )
    return *results, grad_kernel.reshape(3, 3, 3, 32, 32), grad_bias.reshape(32)


def solution(mesh):
    block = P("gz", "gy", None)
    return jax.shard_map(
        local,
        mesh=mesh,
        in_specs=(block, block, block, P(), P()),
        out_specs=(block, block, P(), P()),
        check_vma=False,
    )
```

```python
import functools
import math

import jax
import jax.numpy as jnp
from jax import lax
from jax.experimental import pallas as pl
from jax.experimental.pallas import tpu as pltpu
from jax.sharding import PartitionSpec as P

F32 = jnp.float32
BF16 = jnp.bfloat16
LANES = 128
MIB = 1024 * 1024


def call(body, outs, scratch, args):
    return pl.pallas_call(
        body,
        out_shape=outs,
        scratch_shapes=scratch,
        compiler_params=pltpu.CompilerParams(vmem_limit_bytes=20 * MIB),
    )(*args)


def blocked(body, grid, outs, out_specs, scratch, args, in_specs, aliases=None, flops=0):
    return pl.pallas_call(
        body,
        grid=(grid,),
        out_shape=outs,
        in_specs=in_specs,
        out_specs=out_specs,
        scratch_shapes=scratch,
        input_output_aliases=aliases or {},
        cost_estimate=pl.CostEstimate(flops=flops, bytes_accessed=0, transcendentals=0),
        compiler_params=pltpu.CompilerParams(vmem_limit_bytes=56 * MIB),
    )(*args)


def part_of(shape, *index):
    return pl.BlockSpec(shape, lambda step: index)


def spread_rows(scratch, groups, group, block):
    pitch = groups + 1
    for half in range(2):
        scratch[pl.ds(half * 8 * pitch + group, 8, stride=pitch), :] = block[half * 8 : half * 8 + 8]


def group_body(act_in, grad_in, mask_in, low, high_first, high_rest, firsts, lasts, scratch, act, grad, mask, arrived):
    rows, groups = act.shape[1], low.shape[1]
    copies = [
        [
            pltpu.make_async_copy(source.at[plane], target.at[plane], arrived.at[plane, place])
            for place, (source, target) in enumerate(((act_in, act), (mask_in, mask), (grad_in, grad)))
        ]
        for plane in range(2)
    ]
    for plane in (1, 0):
        for copy in copies[plane]:
            copy.start()
    for plane in (1, 0):
        for kind in range(2):
            out = high_first if plane else low
            for copy in copies[plane][:1] if kind == 0 else copies[plane][1:]:
                copy.wait()
            for group in range(groups):
                span = slice(group * LANES, (group + 1) * LANES)
                if kind == 0:
                    block = act[plane, :, span].astype(F32)
                else:
                    block = grad[plane, :, span].astype(F32) * mask[plane, :, span].astype(F32)
                spread_rows(scratch, groups, group, block)
            for row in range(rows):
                at = row * (groups + 1)
                cells = scratch[at : at + groups, :].astype(BF16)
                if plane and kind and row >= EARLY:
                    high_rest[row - EARLY] = cells
                else:
                    out[kind * rows + row] = cells
                if row == 0:
                    firsts[plane * 2 + kind] = cells
                if row == rows - 1:
                    lasts[plane * 2 + kind] = cells


def with_edges(cells):
    groups = cells.shape[0]
    wide = cells.astype(F32)
    lane = lax.broadcasted_iota(jnp.int32, wide.shape, 1)
    row = lax.broadcasted_iota(jnp.int32, wide.shape, 0)
    before = jnp.where(row == 0, 0.0, pltpu.roll(wide, 1, 0))
    after = jnp.where(row == groups - 1, 0.0, pltpu.roll(wide, groups - 1, 0))
    return jnp.concatenate([cells, jnp.where(lane < 64, after, before).astype(BF16)], axis=1)


def fill_plane(taps, place, source, first, last):
    rows = source.shape[0]
    taps[place, 0] = with_edges(first)
    taps[place, rows + 1] = with_edges(last)

    def step(row, carry):
        taps[place, row + 1] = with_edges(source[row])
        return carry

    lax.fori_loop(0, rows, step, 0, unroll=2)


def build_weights(kernel, flip, out):
    lane = lax.broadcasted_iota(jnp.int32, (32, LANES), 1) // 32
    for tap_z in range(3):
        for tap_y in range(3):
            blocks = []
            for tap_x in range(3):
                at = (tap_z * 3 + tap_y) * 3 + tap_x
                at = 26 - at if flip else at
                block = kernel[at * 32 : at * 32 + 32, :].astype(F32)
                block = block.T if flip else block
                blocks.append(jnp.concatenate([block] * 4, axis=1))
            for place in range(8):
                voxel = place if place < 6 else place - 8
                total = jnp.zeros((32, LANES), F32)
                for tap_x in range(3):
                    total = jnp.where(lane == voxel - tap_x + 1, blocks[tap_x], total)
                out[tap_z, tap_y, place * 32 : place * 32 + 32, :] = total.astype(BF16)


CHUNK = 4
EARLY = 12


def fold(term):
    total = None
    for voxel in range(4):
        part = term[voxel * 32 : voxel * 32 + 32]
        shift = (-(voxel - 1) * 32) % 256
        if shift:
            part = pltpu.roll(part, shift, 1)
        total = part if total is None else total + part
    return total[:, :LANES]


def gather_grad(first, rest, grad):
    rows = grad.shape[0]
    if first.shape == rest.shape:
        grad[...] = first[rows : 2 * rows]
    else:
        grad[:EARLY] = first[rows:]
        grad[EARLY:] = rest[: rows - EARLY]


def own_body(
    low, high_first, high_rest, from_left, from_right, kernel,
    folded, bias_terms, partial_f, weights_f, partial_g, weights_g, turned, taps, high_grad,
):
    rows, groups = low.shape[0] // 2, low.shape[1]
    chunks = rows // CHUNK
    step = pl.program_id(0)

    def fill(kind):
        for plane, source in enumerate((low.at[kind * rows : kind * rows + rows], (high_first.at[:rows], high_grad)[kind])):
            at = 2 * plane + kind
            fill_plane(taps, plane, source, from_left[at], from_right[at])

    @pl.when(step == 0)
    def _():
        gather_grad(high_first, high_rest, high_grad)
        sums = jnp.zeros((8, LANES), F32)
        for plane, source in enumerate((low.at[rows:], high_grad)):
            flat = source[...].reshape(rows * groups, LANES)
            turned[plane * LANES : (plane + 1) * LANES, :] = flat.T
            sums = sums + jnp.sum(flat.astype(F32).reshape(-1, 8, LANES), axis=0)
        bias_terms[...] = sums
        build_weights(kernel, False, weights_f)
        build_weights(kernel, True, weights_g)
        fill(0)
        for tap_y in range(3):
            both = []
            for plane in range(2):
                rhs = taps[plane, tap_y : tap_y + rows].reshape(rows * groups, 256)
                both.append(jnp.dot(turned[...], rhs, preferred_element_type=F32))
            folded[1, tap_y] = fold(both[0][:LANES] + both[1][LANES:])
            folded[0, tap_y] = fold(both[0][LANES:])
            folded[2, tap_y] = fold(both[1][:LANES])

    @pl.when(step == chunks)
    def _():
        fill(1)

    def add(weights, partial, chunk):
        total = inner_sum(taps, weights, chunk, groups)
        for plane in range(2):
            part = total[:, plane * LANES : (plane + 1) * LANES]
            partial[plane] = part.reshape(CHUNK, groups, LANES)

    @pl.when(step < chunks)
    def _():
        add(weights_f, partial_f, step)

    @pl.when(step >= chunks)
    def _():
        add(weights_g, partial_g, step - chunks)


def kernel_grad_body(
    below_first, below_rest, low, from_left, from_right, folded, bias_terms,
    keep, send, packed, taps, sums, below_grad,
):
    rows, groups = low.shape[0] // 2, low.shape[1]
    blank = jnp.zeros((groups, LANES), BF16)
    gather_grad(below_first, below_rest, below_grad)
    fill_plane(taps, 0, below_first.at[:rows], blank, blank)
    fill_plane(taps, 1, low.at[:rows], from_left[0], from_right[0])
    below_turned = below_grad[...].reshape(rows * groups, LANES).T
    low_turned = low[rows:].reshape(rows * groups, LANES).T
    for tap_y in range(3):
        rhs = taps[0, tap_y : tap_y + rows].reshape(rows * groups, 256)
        sums[0, tap_y] = jnp.dot(low_turned, rhs, preferred_element_type=F32)
        rhs = taps[1, tap_y : tap_y + rows].reshape(rows * groups, 256)
        sums[1, tap_y] = jnp.dot(below_turned, rhs, preferred_element_type=F32)
    sums[0, 2] += jnp.dot(from_left[1].T, taps[0, 1], preferred_element_type=F32)
    sums[0, 0] += jnp.dot(from_right[1].T, taps[0, rows], preferred_element_type=F32)
    lane = lax.broadcasted_iota(jnp.int32, (32, LANES), 1)
    parts = [folded[at // 3, at % 3] for at in range(9)]
    for tap_y in range(3):
        parts[tap_y] += fold(sums[0, tap_y])
        parts[6 + tap_y] += fold(sums[1, tap_y])
    row = jnp.sum(bias_terms[...], axis=0, keepdims=True)
    row = row + pltpu.roll(row, 64, 1)
    row = row + pltpu.roll(row, 32, 1)
    first = lax.broadcasted_iota(jnp.int32, (32, LANES), 0) == 0
    for place in range(7):
        if place < 6:
            extra = pltpu.roll(parts[7 + place // 3], 96 - 32 * (place % 3), 1)
        else:
            extra = jnp.where(first, jnp.broadcast_to(row, (32, LANES)), 0.0)
        packed[place * 32 : place * 32 + 32, :] = jnp.where(lane < 96, parts[place], extra)
    upper = lax.rem(lax.axis_index("gy"), 2) == 1
    keep[...] = jnp.where(upper, packed[HALF : 2 * HALF], packed[:HALF])
    send[...] = jnp.where(upper, packed[:HALF], packed[HALF : 2 * HALF])


def inner_sum(taps, weights, chunk, groups):
    total = None
    for plane in range(2):
        for tap_y in range(3):
            lhs = taps[plane, pl.ds(chunk * CHUNK + tap_y, CHUNK)].reshape(CHUNK * groups, 256)
            matrix = jnp.concatenate([weights[plane + 1, tap_y], weights[plane, tap_y]], axis=1)
            term = jnp.dot(lhs, matrix, preferred_element_type=F32)
            total = term if total is None else total + term
    return total


def outer_body(count, *refs):
    first, rest = refs[0], refs[count - 1]
    weights_f, weights_g, partial_f, partial_g, line = refs[count : count + 5]
    output, grad_input, taps, scratch, grad = refs[-5:]
    rows, groups = partial_f.shape[1:3]
    repeated = jnp.concatenate([line[...]] * 4, axis=1)
    act, edge = first.at[:rows], rest.at[rest.shape[0] - 4 :]
    gather_grad(first, rest, grad)
    for kind, (source, weights, partial, out, turn) in enumerate(
        (
            (act, weights_f, partial_f, output, rectified),
            (grad, weights_g, partial_g, grad_input, kept),
        )
    ):
        fill_plane(taps, kind, source, edge[kind], edge[2 + kind])
        for chunk in range(rows // CHUNK):
            start = chunk * CHUNK
            total = partial[0, start : start + CHUNK].reshape(CHUNK * groups, LANES)
            for tap_y in range(3):
                at = start + tap_y
                lhs = taps[kind, at : at + CHUNK].reshape(CHUNK * groups, 256)
                total = total + jnp.dot(lhs, weights[0, tap_y], preferred_element_type=F32)
            put_rows(scratch, turn(total, repeated), chunk, groups)
        lay_out(scratch, out, 0, rows, groups)


def rectified(total, line):
    return jnp.maximum(total + line, 0.0)


def kept(total, line):
    return total


def lay_out(scratch, out, plane, rows, groups):
    pitch = groups + 1
    for group in range(groups):
        halves = [scratch[pl.ds(half * 8 * pitch + group, 8, stride=pitch), :] for half in range(2)]
        block = jnp.concatenate(halves, axis=0).astype(BF16)
        out[plane, :, group * LANES : (group + 1) * LANES] = block


def put_rows(scratch, total, chunk, groups):
    for row in range(CHUNK):
        at = (chunk * CHUNK + row) * (groups + 1)
        scratch[at : at + groups, :] = total[row * groups : (row + 1) * groups]


HALF = 112


def join_body(part, other, packed):
    upper = lax.rem(lax.axis_index("gy"), 2) == 1
    packed[:HALF] = jnp.where(upper, other[...], part[...])
    packed[HALF : 2 * HALF] = jnp.where(upper, part[...], other[...])


def unpack_body(scaling, part, one, two, three, grad_kernel, grad_bias):
    for place in range(7):
        span = slice(place * 32, place * 32 + 32)
        block = ((part[span, :] + one[span, :]) + (two[span, :] + three[span, :])) * scaling
        turned = block.T
        grad_kernel[place * 96 : place * 96 + 96, :] = turned[:96]
        if place < 6:
            grad_kernel[(21 + place) * 32 : (22 + place) * 32, :] = turned[96:]
        else:
            grad_bias[...] = pltpu.roll(block, 32, 1)[:1, :32]


def shifted(value, axis, step):
    count = lax.axis_size(axis)
    pairs = [(i, i + step) for i in range(count) if 0 <= i + step < count]
    return lax.ppermute(value, axis, pairs)


def swapped(value, bit):
    count = lax.axis_size("gz") * lax.axis_size("gy")
    return lax.ppermute(value, ("gz", "gy"), [(i, i ^ bit) for i in range(count)])


def sum_of_four(value, low, high):
    one, two, three = (swapped(value, bit) for bit in (low, high, low + high))
    return (value + one) + (two + three)


def local(activations, grad_out, relu_mask, kernel, bias):
    planes, rows, width = activations.shape
    groups = width // LANES
    block = activations.shape
    shape = jax.ShapeDtypeStruct
    pair = shape((2 * rows, groups, LANES), BF16)
    one_plane = pltpu.VMEM((rows, groups, LANES), BF16)
    lines = shape((4, groups, LANES), BF16)
    spread = pltpu.VMEM((rows * (groups + 1) + 8, LANES), F32)
    two_taps = pltpu.VMEM((2, rows + 2, groups, 2 * LANES), BF16)
    half = shape((HALF, LANES), F32)
    packed = pltpu.VMEM((2 * HALF, LANES), F32)

    low, high_first, high_rest, firsts, lasts = pl.pallas_call(
        group_body,
        in_specs=[pl.BlockSpec(memory_space=pl.ANY)] * 3,
        out_shape=(
            pair, shape((rows + EARLY, groups, LANES), BF16), shape((rows - EARLY, groups, LANES), BF16), lines, lines,
        ),
        scratch_shapes=[
            spread, pltpu.VMEM(block, BF16), pltpu.VMEM(block, BF16), pltpu.VMEM(block, jnp.int32),
            pltpu.SemaphoreType.DMA((2, 3)),
        ],
        compiler_params=pltpu.CompilerParams(vmem_limit_bytes=56 * MIB),
    )(activations, grad_out, relu_mask)
    from_left = shifted(lasts, "gy", 1)
    from_right = shifted(firsts, "gy", -1)
    below_first = shifted(high_first, "gz", 1)
    below_rest = shifted(jnp.concatenate([high_rest, from_left[2:], from_right[2:]]), "gz", 1)

    line = bias.reshape(1, 32)
    flat_kernel = kernel.reshape(27 * 32, 32)
    chunks = rows // CHUNK
    plane = (rows, groups, LANES)
    folded_shape, bias_shape, weights_shape = (3, 3, 32, LANES), (8, LANES), (3, 3, 256, LANES)
    piece = (2, CHUNK, groups, LANES)
    folded, bias_terms, partial_f, weights_f, partial_g, weights_g = blocked(
        own_body,
        2 * chunks,
        (
            shape(folded_shape, F32), shape(bias_shape, F32),
            shape((2, *plane), F32), shape(weights_shape, BF16),
            shape((2, *plane), F32), shape(weights_shape, BF16),
        ),
        (
            part_of(folded_shape, 0, 0, 0, 0), part_of(bias_shape, 0, 0),
            pl.BlockSpec(piece, lambda step: (0, jnp.minimum(step, chunks - 1), 0, 0)),
            part_of(weights_shape, 0, 0, 0, 0),
            pl.BlockSpec(piece, lambda step: (0, jnp.maximum(step - chunks, 0), 0, 0)),
            part_of(weights_shape, 0, 0, 0, 0),
        ),
        [pltpu.VMEM((2 * LANES, rows * groups), BF16), two_taps, one_plane],
        (low, high_first, high_rest, from_left, from_right, flat_kernel),
        [part_of(array.shape, 0, 0, 0) for array in (low, high_first, high_rest)] + [part_of(lines.shape, 0, 0, 0)] * 2 + [part_of(flat_kernel.shape, 0, 0)],
    )

    def outer(side, beside, done=()):
        weights, partial = part_of((1, 3, 256, LANES), 2 * side, 0, 0, 0), part_of((1, *plane), side, 0, 0, 0)
        return blocked(
            functools.partial(outer_body, len(beside)),
            1,
            (shape(block, BF16), shape(block, BF16)),
            (part_of((1, *block[1:]), side, 0, 0),) * 2,
            [two_taps, spread, one_plane],
            (*beside, weights_f, weights_g, partial_f, partial_g, line, *done),
            [
                *[part_of(array.shape, 0, 0, 0) for array in beside],
                weights, weights, partial, partial, part_of(line.shape, 0, 0),
                *[pl.BlockSpec(memory_space=pl.ANY)] * len(done),
            ],
            {len(beside) + 5: 0, len(beside) + 6: 1} if done else None,
        )

    ends = (from_left[:2], from_right[:2])
    ends, folded, partial_g = lax.optimization_barrier((ends, folded, partial_g))
    down = jnp.concatenate([low, *ends])
    above = shifted(down, "gz", -1)

    part, send = call(
        kernel_grad_body,
        (half, half),
        [packed, two_taps, pltpu.VMEM((2, 3, LANES, 256), F32), one_plane],
        (below_first, below_rest, low, from_left, from_right, folded, bias_terms),
    )
    part = part + swapped(send, 1)
    part = sum_of_four(part, 4, 8)
    part = sum_of_four(part, 32, 64)
    results = outer(0, (below_first, below_rest))
    part, results = lax.optimization_barrier((part, results))
    part = call(join_body, shape((2 * HALF, LANES), F32), [], (part, swapped(part, 1)))
    part, above = lax.optimization_barrier((part, above))
    others = [swapped(part, bit) for bit in (2, 16, 18)]
    results = outer(1, (above,), results)

    voxels = planes * lax.axis_size("gz") * rows * lax.axis_size("gy") * (width // 32)
    grad_kernel, grad_bias = call(
        functools.partial(unpack_body, 1.0 / math.sqrt(voxels)),
        (shape((27 * 32, 32), F32), shape((1, 32), F32)),
        [],
        (part, *others),
    )
    return *results, grad_kernel.reshape(3, 3, 3, 32, 32), grad_bias.reshape(32)


def solution(mesh):
    block = P("gz", "gy", None)
    return jax.shard_map(
        local,
        mesh=mesh,
        in_specs=(block, block, block, P(), P()),
        out_specs=(block, block, P(), P()),
        check_vma=False,
    )
```
